32 devices in a mesh: frame: 8 (over z, x), head: 4 (over y, core).
Axes of the slice: x: 2, y: 2, z: 4, core: 2. Of those that a mesh axis runs over, the one named last changes fastest.
Arguments:
- latents: bfloat16 [64, 64, 1152], P('frame', None, 'head'), may hold values from -6 to 6
- fresh: bfloat16 [2, 64, 1152], P(None, None, 'head'), may hold values from -6 to 6
- noise_level: int32 [64], P('frame'), may hold values from 0 to 63
- window_mask: int32 [64, 17], P('frame'), may hold values from 0 to 1, as said below
- mod_table: float32 [64, 6, 1152], replicated, may hold values from -3 to 3
- keep_coef: float32 [64], replicated, may hold values from 0.3 to 1
- layer_coef: float32 [64], replicated, may hold values from 0.2 to 1
- w_qkv: bfloat16 [3, 1152, 1152], P(None, None, 'head')
- w_out: bfloat16 [1152, 1152], P('head'), may hold values from -0.1875 to 0.1875
- w_fc1: bfloat16 [1152, 4608], P(None, 'head'), may hold values from -0.1875 to 0.1875
- w_fc2: bfloat16 [4608, 1152], P('head'), may hold values from -0.09375 to 0.09375
Outputs:
- queue_out: bfloat16 [64, 64, 1152], P('frame', None, 'head')
The draws below stay inside these ranges and needn't reach their ends.
Inputs may be any that keep to these rules, and one draw needn't show every extreme that they name: `window_mask`: column 8 (offset zero) is 1 in every row.
All inputs are finite; a program needn't handle non-finite values.
Results may differ from the reference program's by a relative error of at most 0.029.
Values may be sent and summed in bfloat16 or wider, within the bound.
No kernel may reach another device: no remote copies, remote signals or barrier semaphores. Data moves between devices by JAX's collectives and lax.ppermute only.
A program may use at most 64 MiB of HBM per device.

```python
import math
import jax
import jax.numpy as jnp
from jax import lax

D = 1152
HD = 72
FF = 4608
LEVELS = 64
W = 8
P_SIZE = 64
FRAMES = 64
N_HEAD = 4


def draw_noise_level(key, part):
    key = jax.random.fold_in(key, 11)
    position = jnp.arange(FRAMES, dtype=jnp.int32)
    base_level = position * LEVELS // FRAMES
    jitter = jax.random.randint(key, (FRAMES,), -1, 2, dtype=jnp.int32)
    levels = jnp.clip(base_level + jitter, 0, LEVELS - 1)
    levels = jnp.where(position == 0, 0, levels)
    levels = jnp.where(position == FRAMES - 1, LEVELS - 1, levels)
    return levels.astype(jnp.int32)


def draw_window_mask(key, part):
    key = jax.random.fold_in(key, 12)
    ticket = jax.random.randint(key, (FRAMES, 2 * W + 1), 0, 4, dtype=jnp.int32)
    opened = (ticket > 0).astype(jnp.int32)
    column = jnp.arange(2 * W + 1, dtype=jnp.int32)[None, :]
    return jnp.where(column == W, 1, opened).astype(jnp.int32)


def draw_w_qkv(key, part):
    key = jax.random.fold_in(key, 13)
    matrix = jax.random.normal(key, (3, D, D), jnp.float32) * D ** (-0.5)
    return matrix.astype(jnp.bfloat16)


def level_of(rng, shape, cuts, low, top_value):
    factor_of = 1.0
    for axis_at, blocks in cuts:
        draws = jax.random.uniform(jax.random.fold_in(jax.random.fold_in(rng, 6), axis_at), (blocks,), jnp.float32, low / len(cuts), top_value / len(cuts))
        factor_of = factor_of * jnp.repeat(jnp.exp(draws), shape[axis_at] // blocks).reshape((-1,) + (1,) * (len(shape) - 1 - axis_at))
    return factor_of


def centred(rng, extent, width, bound, shards=(), held_as=jnp.bfloat16):
    drawn = width * jax.random.normal(rng, extent, jnp.float32)
    if shards:
        drawn = drawn * level_of(rng, extent, shards, -0.22, 0.18)
    return jnp.clip(drawn, -bound, bound).astype(held_as)


def setup_inputs(seed: int = 0) -> dict:
    arg_keys = jax.random.split(jax.random.key(seed), 12)
    latents = centred(arg_keys[0], (FRAMES, P_SIZE, D), 1.0, 6.0, ((0, 8), (2, 4)))
    fresh = centred(arg_keys[1], (2, P_SIZE, D), 1.0, 6.0, ((2, 4),))
    noise_level = draw_noise_level(jax.random.fold_in(arg_keys[11], 71), 0)
    window_mask = draw_window_mask(jax.random.fold_in(arg_keys[11], 71), 0)
    mod_table = centred(arg_keys[4], (LEVELS, 6, D), 0.5, 3.0, (), jnp.float32)
    keep_coef = jnp.clip(jnp.exp(jax.random.uniform(arg_keys[5], (LEVELS,), jnp.float32, math.log(0.3), math.log(1.0))), 0.3, 1.0)
    layer_coef = jnp.clip(jnp.exp(jax.random.uniform(arg_keys[6], (LEVELS,), jnp.float32, math.log(0.2), math.log(1.0))), 0.2, 1.0)
    w_qkv = draw_w_qkv(jax.random.fold_in(arg_keys[11], 71), 0)
    w_out = centred(arg_keys[8], (D, D), D ** -0.5, 0.1875, ((0, 4),))
    w_fc1 = centred(arg_keys[9], (D, FF), D ** -0.5, 0.1875, ((1, 4),))
    w_fc2 = centred(arg_keys[10], (FF, D), FF ** -0.5, 0.09375, ((0, 4),))
    return dict(latents=latents, fresh=fresh, noise_level=noise_level, window_mask=window_mask, mod_table=mod_table, keep_coef=keep_coef, layer_coef=layer_coef, w_qkv=w_qkv, w_out=w_out, w_fc1=w_fc1, w_fc2=w_fc2)


epsilon = 1e-06

def modulate(values, shift_row, scale_row):
    center = values - lax.optimization_barrier(jnp.mean(values, axis=-1, keepdims=True))
    spread_sq = lax.optimization_barrier(jnp.mean(center * center, axis=-1, keepdims=True))
    return center * lax.rsqrt(spread_sq + epsilon) * (1.0 + scale_row) + shift_row

def window_attention(queries, padded, allowed):
    frame_count, token_count, feature_width = queries.shape
    head_count = feature_width // HD
    query_heads = queries.astype(jnp.float32).reshape(frame_count, token_count, head_count, HD)
    scaling = 1.0 / math.sqrt(HD)
    score_list = []
    for offset in range(2 * W + 1):
        key_rows = padded[0, offset:offset + frame_count].astype(jnp.float32).reshape(frame_count, token_count, head_count, HD)
        score_list.append(lax.optimization_barrier(jnp.sum(query_heads * key_rows, axis=-1)) * scaling)
    scores = jnp.stack(score_list, axis=-1)
    open_mask = allowed[:, None, None, :]
    scores = jnp.where(open_mask, scores, -1e+30)
    top_score = lax.optimization_barrier(jnp.max(scores, axis=-1, keepdims=True))
    weights = jnp.where(open_mask, jnp.exp(scores - top_score), 0.0)
    probabilities = (weights / lax.optimization_barrier(jnp.sum(weights, axis=-1, keepdims=True))).astype(jnp.bfloat16)
    mixed_sum = jnp.zeros_like(query_heads)
    for offset in range(2 * W + 1):
        value_rows = padded[1, offset:offset + frame_count].astype(jnp.float32).reshape(frame_count, token_count, head_count, HD)
        mixed_sum = mixed_sum + probabilities[..., offset:offset + 1].astype(jnp.float32) * value_rows
    return mixed_sum.reshape(frame_count, token_count, feature_width).astype(jnp.bfloat16)

def group_sums(left, right):
    group_width = left.shape[-1] // N_HEAD
    running = jnp.zeros(left.shape[:-1] + (right.shape[1],), jnp.float32)
    for group_idx in range(N_HEAD):
        lower = group_idx * group_width
        group_term = jnp.dot(left[..., lower:lower + group_width], right[lower:lower + group_width], preferred_element_type=jnp.float32).astype(jnp.bfloat16)
        running = running + lax.optimization_barrier(group_term).astype(jnp.float32)
    return running

def denoise(current, noise_level, window_mask, mod_table, keep_coef, layer_coef, w_qkv, w_out, w_fc1, w_fc2):
    frame_count = current.shape[0]
    modulation = mod_table[noise_level]
    current_wide = current.astype(jnp.float32)
    normed = modulate(current_wide, modulation[:, None, 0], modulation[:, None, 1]).astype(jnp.bfloat16)
    queries = jnp.dot(normed, w_qkv[0], preferred_element_type=jnp.float32).astype(jnp.bfloat16)
    key_rows = jnp.dot(normed, w_qkv[1], preferred_element_type=jnp.float32).astype(jnp.bfloat16)
    value_rows = jnp.dot(normed, w_qkv[2], preferred_element_type=jnp.float32).astype(jnp.bfloat16)
    padded = jnp.pad(jnp.stack([key_rows, value_rows], 0), ((0, 0), (W, W), (0, 0), (0, 0)))
    positions = jnp.arange(frame_count, dtype=jnp.int32)[:, None] + jnp.arange(2 * W + 1, dtype=jnp.int32)[None, :] - W
    allowed = (window_mask == 1) & (positions >= 0) & (positions < frame_count)
    attended = window_attention(queries, padded, allowed)
    attention_total = group_sums(attended, w_out)
    after = (current_wide + modulation[:, None, 2] * attention_total).astype(jnp.bfloat16)
    after_wide = after.astype(jnp.float32)
    normed_two = modulate(after_wide, modulation[:, None, 3], modulation[:, None, 4]).astype(jnp.bfloat16)
    hidden = jax.nn.gelu(jnp.dot(normed_two, w_fc1, preferred_element_type=jnp.float32), approximate=True).astype(jnp.bfloat16)
    feed_total = group_sums(hidden, w_fc2)
    output_rows = after_wide + modulation[:, None, 5] * feed_total
    keep_here = keep_coef[noise_level][:, None, None]
    layer_here = layer_coef[noise_level][:, None, None]
    return (keep_here * current_wide + layer_here * output_rows).astype(jnp.bfloat16)

def reference(latents, fresh, noise_level, window_mask, mod_table, keep_coef, layer_coef, w_qkv, w_out, w_fc1, w_fc2):
    current = latents
    for step_idx in range(2):
        current = jnp.concatenate([fresh[step_idx:step_idx + 1], current[:-1]], 0)
        current = denoise(current, noise_level, window_mask, mod_table, keep_coef, layer_coef, w_qkv, w_out, w_fc1, w_fc2)
    return current
```

```python
import functools
import math

import jax
import jax.numpy as jnp
from jax import lax
from jax.experimental import pallas as pl
from jax.experimental.pallas import tpu as pltpu
from jax.sharding import Mesh, PartitionSpec as P

HD = 72
W = 8
OFFSETS = 2 * W + 1
EPSILON = 1e-06
F32 = jnp.float32
BF16 = jnp.bfloat16
LANES = 128
VMEM_LIMIT = 56 * 1024 * 1024

VMEM_SPEC = pl.BlockSpec(memory_space=pltpu.VMEM)
SMEM_SPEC = pl.BlockSpec(memory_space=pltpu.SMEM)
ANY_SPEC = pl.BlockSpec(memory_space=pl.ANY)


def params():
    return pltpu.CompilerParams(vmem_limit_bytes=VMEM_LIMIT)


def padded_width(width):
    return -(-(width + 1 + OFFSETS) // LANES) * LANES


def normalise(values, shift_rows, scale_rows):
    center = values - jnp.mean(values, axis=-1, keepdims=True)
    spread = jnp.mean(center * center, axis=-1, keepdims=True)
    return center * lax.rsqrt(spread + EPSILON) * (1.0 + scale_rows) + shift_rows


def payload_kernel(x_ref, meta_ref, out_ref, rows_ref):
    frames, tokens, width = x_ref.shape
    wide = out_ref.shape[1]
    meta = meta_ref[...].astype(F32)
    for i in range(frames):
        tail = jnp.broadcast_to(meta[i : i + 1, :], (tokens, wide - width))
        row = jnp.concatenate([x_ref[i].astype(F32), tail], axis=1)
        for lane in range(0, wide, LANES):
            rows_ref[lane // LANES, pl.ds(i, tokens, stride=frames), :] = row[:, lane : lane + LANES]
    for lane in range(0, wide, LANES):
        out_ref[:, lane : lane + LANES] = rows_ref[lane // LANES].astype(BF16)


def make_payload(x, meta):
    frames, tokens, width = x.shape
    wide = padded_width(width)
    meta = jnp.pad(meta, ((0, 0), (0, wide - width - meta.shape[1])))
    return pl.pallas_call(
        payload_kernel,
        out_shape=jax.ShapeDtypeStruct((tokens * frames, wide), BF16),
        in_specs=[VMEM_SPEC, VMEM_SPEC],
        out_specs=VMEM_SPEC,
        scratch_shapes=[pltpu.VMEM((wide // LANES, tokens * frames, LANES), F32)],
        compiler_params=params(),
        name="payload",
    )(x, meta)


def prepare_kernel(width, meta_ref, table_ref, coef_ref, mod_ref, pair_ref, mask_ref):
    groups, here, wide = meta_ref.shape
    frames = groups * here
    levels = table_ref.shape[0]
    meta = meta_ref[...].astype(F32).reshape(frames, wide)
    level = meta[:, 0:1]
    ids = lax.broadcasted_iota(jnp.int32, (frames, levels), 1).astype(F32)
    hot = level == ids
    hot_bf = hot.astype(BF16)
    features = mod_ref.shape[2]
    for j in range(mod_ref.shape[0]):
        rows = table_ref[:, j * features : (j + 1) * features]
        high = rows.astype(BF16)
        rest = rows - high.astype(F32)
        middle = rest.astype(BF16)
        low = (rest - middle.astype(F32)).astype(BF16)
        total = jnp.dot(hot_bf, high, preferred_element_type=F32)
        total += jnp.dot(hot_bf, middle, preferred_element_type=F32)
        total += jnp.dot(hot_bf, low, preferred_element_type=F32)
        mod_ref[j] = total
    keep = jnp.sum(jnp.where(hot, coef_ref[0:1, :], 0.0), axis=1, keepdims=True)
    layer = jnp.sum(jnp.where(hot, coef_ref[1:2, :], 0.0), axis=1, keepdims=True)
    lane = lax.broadcasted_iota(jnp.int32, (frames, LANES), 1)
    pair_ref[...] = jnp.where(lane == 0, keep, layer)

    block = mask_ref.shape[0]
    repeat = block // frames
    row = lax.broadcasted_iota(jnp.int32, (frames, block), 0)
    column = lax.broadcasted_iota(jnp.int32, (frames, block), 1)
    for t in range(repeat):
        distance = column - t * frames - row
        inside = (column >= t * frames) & (column < (t + 1) * frames)
        is_open = jnp.zeros((frames, block), F32)
        for o in range(OFFSETS):
            is_open = jnp.where(distance == o - W, meta[:, 1 + o : 2 + o], is_open)
        mask_ref[t * frames : (t + 1) * frames, :] = jnp.where(inside, is_open, 0.0)


def prepare(meta, table, coefs, block):
    groups, here, _ = meta.shape
    frames = groups * here
    levels, kinds, features = table.shape
    return pl.pallas_call(
        functools.partial(prepare_kernel, features),
        out_shape=(
            jax.ShapeDtypeStruct((kinds, frames, features), F32),
            jax.ShapeDtypeStruct((frames, LANES), F32),
            jax.ShapeDtypeStruct((block, block), F32),
        ),
        in_specs=[VMEM_SPEC] * 3,
        out_specs=(VMEM_SPEC,) * 3,
        compiler_params=params(),
        name="prepare",
    )(meta, table.reshape(levels, kinds * features), coefs)


def start_copies(sources, targets, sems):
    copies = []
    for n, (source, target) in enumerate(zip(sources, targets)):
        copy = pltpu.make_async_copy(source, target, sems.at[n])
        copy.start()
        copies.append(copy)
    return copies


def attend(q, k, v, is_open):
    rows, share = q.shape
    heads = share // HD
    lane = lax.broadcasted_iota(jnp.int32, (1, share), 1)
    scaling = 1.0 / math.sqrt(HD)
    pieces = {}
    for h in range(heads):
        low = HD * h // LANES * LANES
        high = min(share, -(-HD * (h + 1) // LANES) * LANES)
        mine = (lane[:, low:high] >= HD * h) & (lane[:, low:high] < HD * (h + 1))
        qh = jnp.where(mine, q[:, low:high].astype(F32), 0.0).astype(BF16)
        scores = lax.dot_general(
            qh, k[:, low:high], (((1,), (1,)), ((), ())), preferred_element_type=F32
        )
        scores = jnp.where(is_open, scores * scaling, -1e30)
        top = jnp.max(scores, axis=-1, keepdims=True)
        weights = jnp.exp(scores - top)
        probabilities = (weights / jnp.sum(weights, axis=-1, keepdims=True)).astype(BF16)
        mixed = jnp.dot(probabilities, v[:, low:high], preferred_element_type=F32)
        mixed = jnp.where(mine, mixed, 0.0)
        for start in range(low, high, LANES):
            stop = min(start + LANES, high)
            part = mixed[:, start - low : stop - low]
            pieces[start] = part if start not in pieces else pieces[start] + part
    return jnp.concatenate([pieces[s] for s in sorted(pieces)], axis=1).astype(BF16)


def attention_rows(current, mod_ref, mask_ref, copies, weights, tokens, out_ref, normed_ref):
    for p, rows in enumerate(current):
        frames = rows.shape[0]
        normed_ref[p * frames : (p + 1) * frames, :] = normalise(
            rows, mod_ref[0], mod_ref[1]
        ).astype(BF16)
    qkv_me, qkv_other, out_me, out_other = weights
    rows_total = normed_ref.shape[0]
    block = mask_ref.shape[0]
    is_open = mask_ref[...] > 0.5
    normed = normed_ref[...]
    total = None
    for side, (qkv, w_out) in enumerate(((qkv_me, out_me), (qkv_other, out_other))):
        copies[2 * side].wait()
        q, k, v = (
            jnp.dot(normed, qkv[t], preferred_element_type=F32).astype(BF16) for t in range(3)
        )
        mixed = [
            attend(q[b : b + block], k[b : b + block], v[b : b + block], is_open)
            for b in range(0, rows_total, block)
        ]
        attended = mixed[0] if len(mixed) == 1 else jnp.concatenate(mixed, axis=0)
        copies[2 * side + 1].wait()
        part = jnp.dot(attended, w_out[...], preferred_element_type=F32)
        total = part if total is None else total + part
    out_ref[...] = total.astype(BF16)


def shifted_in(rows, fresh_row):
    frames = rows.shape[0]
    first = lax.broadcasted_iota(jnp.int32, (frames, 1), 0) == 0
    return jnp.where(first, fresh_row, pltpu.roll(rows, 1, 0))


def fresh_rows(place_ref, fresh_refs, step, tokens, split):
    me = place_ref[0]
    core = lax.rem(me, 2)
    own = []
    for ref in fresh_refs:
        value = ref[step].astype(F32)
        if split:
            value = jnp.where(core == 0, value[:tokens], value[tokens:])
        own.append(value)
    ordered = []
    for h in range(len(own)):
        pick = own[h]
        for d in range(len(own)):
            pick = jnp.where(lax.bitwise_xor(me, d) == h, own[d], pick)
        ordered.append(pick)
    return jnp.concatenate(ordered, axis=1)


def first_attention_kernel(
    split, place_ref, mine_ref, other_ref, f0, f1, f2, f3, mod_ref, mask_ref,
    qkv_me, qkv_other, out_me, out_other,
    cur_ref, part_ref, vq_me, vo_me, vq_other, vo_other, normed_ref, sems,
):
    copies = start_copies(
        (qkv_me, out_me, qkv_other, out_other), (vq_me, vo_me, vq_other, vo_other), sems
    )
    groups, cores, rows_here, _ = mine_ref.shape
    features = cur_ref.shape[1]
    frames = mod_ref.shape[1]
    here = frames // groups
    tokens = rows_here // here
    share = qkv_me.shape[2]
    fresh = fresh_rows(place_ref, (f0, f1, f2, f3), 0, tokens, split)
    first_half = place_ref[0] < 2
    blocks = []
    for g in range(groups):
        mine = [mine_ref[g, c].astype(F32)[:, :share] for c in range(cores)]
        other = [other_ref[g, c].astype(F32)[:, :share] for c in range(cores)]
        left = [jnp.where(first_half, a, b) for a, b in zip(mine, other)]
        right = [jnp.where(first_half, b, a) for a, b in zip(mine, other)]
        blocks.append(jnp.concatenate(left + right, axis=1))
    current = []
    for p in range(tokens):
        rows = jnp.concatenate([b[p * here : (p + 1) * here] for b in blocks], axis=0)
        rows = shifted_in(rows, fresh[p : p + 1])
        cur_ref[p * frames : (p + 1) * frames, :] = rows.astype(BF16)
        current.append(rows)
    attention_rows(
        current, mod_ref, mask_ref, copies, (vq_me, vq_other, vo_me, vo_other), tokens,
        part_ref, normed_ref,
    )


def next_attention_kernel(
    split, place_ref, old_ref, after_ref, mine_ref, other_ref, f0, f1, f2, f3, mod_ref, pair_ref,
    mask_ref, qkv_me, qkv_other, out_me, out_other,
    cur_ref, part_ref, vq_me, vo_me, vq_other, vo_other, normed_ref, sems,
):
    copies = start_copies(
        (qkv_me, out_me, qkv_other, out_other), (vq_me, vo_me, vq_other, vo_other), sems
    )
    frames = mod_ref.shape[1]
    tokens = old_ref.shape[0] // frames
    fresh = fresh_rows(place_ref, (f0, f1, f2, f3), 1, tokens, split)
    keep, layer = pair_ref[:, 0:1], pair_ref[:, 1:2]
    current = []
    for p in range(tokens):
        at = slice(p * frames, (p + 1) * frames)
        total = mine_ref[at, :].astype(F32) + other_ref[at, :].astype(F32)
        rows = keep * old_ref[at, :].astype(F32) + layer * (
            after_ref[at, :].astype(F32) + mod_ref[5] * total
        )
        rows = shifted_in(rows, fresh[p : p + 1]).astype(BF16)
        cur_ref[at, :] = rows
        current.append(rows.astype(F32))
    attention_rows(
        current, mod_ref, mask_ref, copies, (vq_me, vq_other, vo_me, vo_other), tokens,
        part_ref, normed_ref,
    )


def attention_call(kernel, vmem_args, weights, rows, features):
    qkv, w_out = weights[0], weights[2]
    return pl.pallas_call(
        kernel,
        out_shape=(jax.ShapeDtypeStruct((rows, features), BF16),) * 2,
        in_specs=[SMEM_SPEC] + [VMEM_SPEC] * (len(vmem_args) - 1) + [ANY_SPEC] * 4,
        out_specs=(VMEM_SPEC,) * 2,
        scratch_shapes=[
            pltpu.VMEM(qkv.shape, BF16),
            pltpu.VMEM(w_out.shape, BF16),
            pltpu.VMEM(qkv.shape, BF16),
            pltpu.VMEM(w_out.shape, BF16),
            pltpu.VMEM((rows, features), BF16),
            pltpu.SemaphoreType.DMA((4,)),
        ],
        compiler_params=params(),
        name="attention",
    )(*vmem_args, *weights)


def gelu(x):
    inner = math.sqrt(2.0 / math.pi) * (x + 0.044715 * (x * x * x))
    return x * (0.5 * (1.0 + jnp.tanh(inner)))


def pieces_of(width, size):
    return [(s, min(size, width - s)) for s in range(0, width, size)]


def feed_kernel(
    halves, place_ref, cur_ref, mine_ref, other_ref, mod_ref,
    fc1_me, fc1_other, fc2_me, fc2_other, *rest,
):
    outs, scratch = rest[: 3 if halves else 2], rest[3 if halves else 2 :]
    after_ref = outs[0]
    v1_me, v1_other, v2_me, v2_other, normed_ref, hidden_ref, sems = scratch
    copies = start_copies(
        (fc1_me, fc1_other, fc2_me, fc2_other), (v1_me, v1_other, v2_me, v2_other), sems
    )
    frames = mod_ref.shape[1]
    tokens = cur_ref.shape[0] // frames
    for p in range(tokens):
        at = slice(p * frames, (p + 1) * frames)
        total = mine_ref[at, :].astype(F32) + other_ref[at, :].astype(F32)
        after = (cur_ref[at, :].astype(F32) + mod_ref[2] * total).astype(BF16)
        after_ref[at, :] = after
        normed_ref[at, :] = normalise(after.astype(F32), mod_ref[3], mod_ref[4]).astype(BF16)
    normed = normed_ref[...]
    units = v1_me.shape[1]
    for side, w1 in enumerate((v1_me, v1_other)):
        copies[side].wait()
        for start, size in pieces_of(units, 256):
            hidden = gelu(
                jnp.dot(normed, w1[:, start : start + size], preferred_element_type=F32)
            )
            hidden_ref[:, side * units + start : side * units + start + size] = hidden.astype(BF16)
    copies[2].wait()
    copies[3].wait()
    features = v2_me.shape[1]
    if not halves:
        for start, size in pieces_of(features, 256):
            at = slice(start, start + size)
            outs[1][:, at] = (
                jnp.dot(hidden_ref[:, :units], v2_me[:, at], preferred_element_type=F32)
                + jnp.dot(hidden_ref[:, units:], v2_other[:, at], preferred_element_type=F32)
            ).astype(BF16)
        return
    total = jnp.dot(hidden_ref[:, :units], v2_me[...], preferred_element_type=F32) + jnp.dot(
        hidden_ref[:, units:], v2_other[...], preferred_element_type=F32
    )
    left, right = total[:, : features // 2], total[:, features // 2 :]
    first_half = place_ref[0] < 2
    outs[1][...] = jnp.where(first_half, left, right).astype(BF16)
    outs[2][...] = jnp.where(first_half, right, left).astype(BF16)


def feed_call(place, cur, mine, other, mod, weights, halves):
    rows, features = cur.shape
    fc1, fc2 = weights[0], weights[2]
    shape = jax.ShapeDtypeStruct((rows, features), BF16)
    half = jax.ShapeDtypeStruct((rows, features // 2), BF16)
    outs = (shape, half, half) if halves else (shape, shape)
    return pl.pallas_call(
        functools.partial(feed_kernel, halves),
        out_shape=outs,
        in_specs=[SMEM_SPEC] + [VMEM_SPEC] * 4 + [ANY_SPEC] * 4,
        out_specs=(VMEM_SPEC,) * len(outs),
        scratch_shapes=[
            pltpu.VMEM(fc1.shape, BF16),
            pltpu.VMEM(fc1.shape, BF16),
            pltpu.VMEM(fc2.shape, BF16),
            pltpu.VMEM(fc2.shape, BF16),
            pltpu.VMEM((rows, features), BF16),
            pltpu.VMEM((rows, 2 * fc1.shape[1]), BF16),
            pltpu.SemaphoreType.DMA((4,)),
        ],
        compiler_params=params(),
        name="feed",
    )(place, cur, mine, other, mod, *weights)


def finish_kernel(place_ref, old_ref, after_ref, mine_ref, other_ref, mod_ref, pair_ref, out_ref):
    groups, cores, rows_here, share = out_ref.shape
    frames, features = mod_ref.shape[1:]
    here = frames // groups
    tokens = rows_here // here
    half = features // 2
    first_half = place_ref[0] < 2
    keep, layer = pair_ref[:, 0:1], pair_ref[:, 1:2]

    def mine(value):
        return jnp.where(first_half, value[:, :half], value[:, half:])

    gate = mine(mod_ref[5])
    results = []
    for p in range(tokens):
        at = slice(p * frames, (p + 1) * frames)
        total = mine_ref[at, :].astype(F32) + other_ref[at, :].astype(F32)
        results.append(
            keep * mine(old_ref[at, :].astype(F32))
            + layer * (mine(after_ref[at, :].astype(F32)) + gate * total)
        )
    for c in range(cores):
        shares = [r[:, c * share : (c + 1) * share] for r in results]
        for g in range(groups):
            rows = [s[g * here : (g + 1) * here] for s in shares]
            out_ref[g, c] = jnp.concatenate(rows, axis=0).astype(BF16)


def finish(place, old, after, mine, other, mod, pair, groups):
    rows, features = old.shape
    share = features // 4
    return pl.pallas_call(
        finish_kernel,
        out_shape=jax.ShapeDtypeStruct((groups, 2, rows // groups, share), BF16),
        in_specs=[SMEM_SPEC] + [VMEM_SPEC] * 6,
        out_specs=VMEM_SPEC,
        compiler_params=params(),
        name="finish",
    )(place, old, after, mine, other, mod, pair)


def unpack_kernel(rows_ref, out_ref, wide_ref):
    frames, tokens, width = out_ref.shape
    slabs = wide_ref.shape[0]
    for s in range(slabs):
        value = rows_ref[:, s * LANES : min((s + 1) * LANES, width)].astype(F32)
        wide_ref[s, :, : value.shape[1]] = value
    for i in range(frames):
        pieces = [wide_ref[s, pl.ds(i, tokens, stride=frames), :] for s in range(slabs)]
        out_ref[i] = jnp.concatenate(pieces, axis=1)[:, :width].astype(BF16)


def unpack(rows, frames):
    count, width = rows.shape
    wide = -(-width // LANES) * LANES
    return pl.pallas_call(
        unpack_kernel,
        out_shape=jax.ShapeDtypeStruct((frames, count // frames, width), BF16),
        in_specs=[VMEM_SPEC],
        out_specs=VMEM_SPEC,
        scratch_shapes=[pltpu.VMEM((wide // LANES, count, LANES), F32)],
        compiler_params=params(),
        name="unpack",
    )(rows)


SWAP = [(0, 1), (1, 0)]


def on_device(
    latents, fresh, noise_level, window_mask, mod_table, keep_coef, layer_coef,
    w_qkv, w_out, w_fc1, w_fc2,
):
    here, tokens_all, share = latents.shape
    features = mod_table.shape[2]
    groups = lax.axis_size("frame")
    frames = groups * here
    frame_index = lax.axis_index("frame")
    y_index, core_index = lax.axis_index("y"), lax.axis_index("core")
    place = (2 * y_index + core_index).astype(jnp.int32).reshape(1)
    group_tokens = tokens_all // groups
    split = group_tokens % 2 == 0
    tokens = group_tokens // 2 if split else group_tokens
    block = max(frames, LANES)

    positions = (
        frame_index * here
        + jnp.arange(here, dtype=jnp.int32)[:, None]
        + jnp.arange(OFFSETS, dtype=jnp.int32)[None, :]
        - W
    )
    allowed = (window_mask == 1) & (positions >= 0) & (positions < frames)
    meta = jnp.concatenate([noise_level[:, None], allowed.astype(jnp.int32)], axis=1)

    fresh_here = lax.dynamic_slice_in_dim(fresh, frame_index * group_tokens, group_tokens, 1)
    fresh_parts = (
        fresh_here,
        lax.ppermute(fresh_here, "core", SWAP),
        lax.ppermute(fresh_here, "y", SWAP),
        lax.ppermute(fresh_here, ("y", "core"), [(i, i ^ 3) for i in range(4)]),
    )
    swap_core = functools.partial(lax.ppermute, axis_name="core", perm=SWAP)
    swap_y = functools.partial(lax.ppermute, axis_name="y", perm=SWAP)
    attention_weights = (w_qkv, swap_core(w_qkv), w_out, swap_core(w_out))
    feed_weights = (w_fc1, swap_core(w_fc1), w_fc2, swap_core(w_fc2))

    payload = make_payload(latents, meta)
    wide = payload.shape[1]
    if split:
        payload = payload.reshape(groups * 2, tokens * here, wide)
        received = lax.all_to_all(payload, ("frame", "core"), 0, 0, tiled=True)
        received = received.reshape(groups, 2, tokens * here, wide)
    else:
        payload = payload.reshape(groups, tokens * here, wide)
        received = lax.all_to_all(payload, "frame", 0, 0, tiled=True)
        partner = swap_core(received)
        first = core_index == 0
        received = jnp.stack(
            [jnp.where(first, received, partner), jnp.where(first, partner, received)], axis=1
        )
    received_other = swap_y(received)
    mod, pair, mask = prepare(
        received[:, 0, :here, share:], mod_table, jnp.stack([keep_coef, layer_coef]), block
    )

    rows = tokens * frames
    current, part = attention_call(
        functools.partial(first_attention_kernel, split),
        (place, received, received_other) + fresh_parts + (mod, mask),
        attention_weights, rows, features,
    )
    after, feed = feed_call(place, current, part, swap_y(part), mod, feed_weights, False)
    current, part = attention_call(
        functools.partial(next_attention_kernel, split),
        (place, current, after, feed, swap_y(feed)) + fresh_parts + (mod, pair, mask),
        attention_weights, rows, features,
    )
    after, feed_here, feed_there = feed_call(
        place, current, part, swap_y(part), mod, feed_weights, True
    )
    result = finish(place, current, after, feed_here, swap_y(feed_there), mod, pair, groups)
    if split:
        result = result.reshape(groups * 2, tokens * here, share)
        result = lax.all_to_all(result, ("frame", "core"), 0, 0, tiled=True)
    else:
        result = jnp.where(core_index == 0, result[:, 0], result[:, 1])
        result = lax.all_to_all(result, "frame", 0, 0, tiled=True)
    return unpack(result.reshape(tokens_all * here, share), here)


def solution(mesh):
    groups, heads = mesh.shape["frame"], mesh.shape["head"]
    inner = Mesh(mesh.devices.reshape(groups, heads // 2, 2), ("frame", "y", "core"))
    head = ("y", "core")
    in_specs = (
        P("frame", None, head),
        P(None, None, head),
        P("frame"),
        P("frame", None),
        P(),
        P(),
        P(),
        P(None, None, head),
        P(head, None),
        P(None, head),
        P(head, None),
    )
    return jax.shard_map(
        on_device, mesh=inner, in_specs=in_specs, out_specs=P("frame", None, head), check_vma=False
    )
```

```python
import functools
import math

import jax
import jax.numpy as jnp
from jax import lax
from jax.experimental import pallas as pl
from jax.experimental.pallas import tpu as pltpu
from jax.sharding import Mesh, PartitionSpec as P

HD = 72
W = 8
OFFSETS = 2 * W + 1
EPSILON = 1e-06
F32 = jnp.float32
BF16 = jnp.bfloat16
LANES = 128
VMEM_LIMIT = 30 * 1024 * 1024

VMEM_SPEC = pl.BlockSpec(memory_space=pltpu.VMEM)
SMEM_SPEC = pl.BlockSpec(memory_space=pltpu.SMEM)
ANY_SPEC = pl.BlockSpec(memory_space=pl.ANY)


def params():
    return pltpu.CompilerParams(vmem_limit_bytes=VMEM_LIMIT)


def padded_width(width):
    return -(-(width + 1 + OFFSETS) // LANES) * LANES


def normalise(values, shift_rows, scale_rows):
    center = values - jnp.mean(values, axis=-1, keepdims=True)
    spread = jnp.mean(center * center, axis=-1, keepdims=True)
    return center * lax.rsqrt(spread + EPSILON) * (1.0 + scale_rows) + shift_rows


def payload_kernel(x_ref, meta_ref, out_ref, rows_ref):
    frames, tokens, width = x_ref.shape
    wide = out_ref.shape[1]
    meta = meta_ref[...].astype(F32)
    for i in range(frames):
        tail = jnp.broadcast_to(meta[i : i + 1, :], (tokens, wide - width))
        row = jnp.concatenate([x_ref[i].astype(F32), tail], axis=1)
        for lane in range(0, wide, LANES):
            rows_ref[lane // LANES, pl.ds(i, tokens, stride=frames), :] = row[:, lane : lane + LANES]
    for lane in range(0, wide, LANES):
        out_ref[:, lane : lane + LANES] = rows_ref[lane // LANES].astype(BF16)


def make_payload(x, meta):
    frames, tokens, width = x.shape
    wide = padded_width(width)
    meta = jnp.pad(meta, ((0, 0), (0, wide - width - meta.shape[1])))
    return pl.pallas_call(
        payload_kernel,
        out_shape=jax.ShapeDtypeStruct((tokens * frames, wide), BF16),
        in_specs=[VMEM_SPEC, VMEM_SPEC],
        out_specs=VMEM_SPEC,
        scratch_shapes=[pltpu.VMEM((wide // LANES, tokens * frames, LANES), F32)],
        compiler_params=params(),
        name="payload",
    )(x, meta)


def prepare_kernel(meta_ref, table_ref, coef_ref, norm_ref, feed_ref, gate_ref, pair_ref, mask_ref):
    groups, here, wide = meta_ref.shape
    frames = groups * here
    levels = table_ref.shape[1]
    meta = meta_ref[...].astype(F32).reshape(frames, wide)
    level = meta[:, 0:1]
    ids = lax.broadcasted_iota(jnp.int32, (frames, levels), 1).astype(F32)
    hot = level == ids
    hot_bf = hot.astype(BF16)
    targets = [(norm_ref, 0), (norm_ref, 1), (feed_ref, 0), (feed_ref, 1), (feed_ref, 2), (gate_ref, 0)]
    for j, (target, at) in enumerate(targets):
        rows = table_ref[j]
        high = rows.astype(BF16)
        rest = rows - high.astype(F32)
        middle = rest.astype(BF16)
        low = (rest - middle.astype(F32)).astype(BF16)
        total = jnp.dot(hot_bf, high, preferred_element_type=F32)
        total += jnp.dot(hot_bf, middle, preferred_element_type=F32)
        total += jnp.dot(hot_bf, low, preferred_element_type=F32)
        target[at] = total
    keep = jnp.sum(jnp.where(hot, coef_ref[0:1, :], 0.0), axis=1, keepdims=True)
    layer = jnp.sum(jnp.where(hot, coef_ref[1:2, :], 0.0), axis=1, keepdims=True)
    lane = lax.broadcasted_iota(jnp.int32, (frames, LANES), 1)
    pair_ref[...] = jnp.where(lane == 0, keep, layer)

    block = mask_ref.shape[0]
    row = lax.broadcasted_iota(jnp.int32, (frames, block), 0)
    column = lax.broadcasted_iota(jnp.int32, (frames, block), 1)
    for t in range(block // frames):
        distance = column - t * frames - row
        inside = (column >= t * frames) & (column < (t + 1) * frames)
        is_open = jnp.zeros((frames, block), F32)
        for o in range(OFFSETS):
            is_open = jnp.where(distance == o - W, meta[:, 1 + o : 2 + o], is_open)
        mask_ref[t * frames : (t + 1) * frames, :] = jnp.where(inside, is_open, 0.0)


def prepare(meta, table, coefs, block):
    groups, here, _ = meta.shape
    frames = groups * here
    features = table.shape[2]
    return pl.pallas_call(
        prepare_kernel,
        out_shape=(
            jax.ShapeDtypeStruct((2, frames, features), F32),
            jax.ShapeDtypeStruct((3, frames, features), F32),
            jax.ShapeDtypeStruct((1, frames, features), F32),
            jax.ShapeDtypeStruct((frames, LANES), F32),
            jax.ShapeDtypeStruct((block, block), F32),
        ),
        in_specs=[VMEM_SPEC] * 3,
        out_specs=(VMEM_SPEC,) * 5,
        compiler_params=params(),
        name="prepare",
    )(meta, table, coefs)


def attend(q, k, v, is_open):
    rows, share = q.shape
    heads = share // HD
    lane = lax.broadcasted_iota(jnp.int32, (1, share), 1)
    scaling = 1.0 / math.sqrt(HD)
    pieces = {}
    for h in range(heads):
        low = HD * h // LANES * LANES
        high = min(share, -(-HD * (h + 1) // LANES) * LANES)
        mine = (lane[:, low:high] >= HD * h) & (lane[:, low:high] < HD * (h + 1))
        qh = jnp.where(mine, q[:, low:high].astype(F32), 0.0).astype(BF16)
        scores = lax.dot_general(
            qh, k[:, low:high], (((1,), (1,)), ((), ())), preferred_element_type=F32
        )
        scores = jnp.where(is_open, scores * scaling, -1e30)
        top = jnp.max(scores, axis=-1, keepdims=True)
        weights = jnp.exp(scores - top)
        probabilities = (weights / jnp.sum(weights, axis=-1, keepdims=True)).astype(BF16)
        mixed = jnp.dot(probabilities, v[:, low:high], preferred_element_type=F32)
        mixed = jnp.where(mine, mixed, 0.0)
        for start in range(low, high, LANES):
            stop = min(start + LANES, high)
            part = mixed[:, start - low : stop - low]
            pieces[start] = part if start not in pieces else pieces[start] + part
    return jnp.concatenate([pieces[s] for s in sorted(pieces)], axis=1).astype(BF16)


def attention_rows(current, norm_ref, mask_ref, weights, out_ref):
    normed = [normalise(rows, norm_ref[0], norm_ref[1]).astype(BF16) for rows in current]
    normed = normed[0] if len(normed) == 1 else jnp.concatenate(normed, axis=0)
    qkv_me, qkv_other, out_me, out_other = weights
    rows_total = normed.shape[0]
    block = mask_ref.shape[0]
    is_open = mask_ref[...] > 0.5
    total = None
    for qkv, w_out in ((qkv_me, out_me), (qkv_other, out_other)):
        q, k, v = (
            lax.dot_general(
                normed, qkv[t], (((1,), (1,)), ((), ())), preferred_element_type=F32
            ).astype(BF16)
            for t in range(3)
        )
        mixed = [
            attend(q[b : b + block], k[b : b + block], v[b : b + block], is_open)
            for b in range(0, rows_total, block)
        ]
        attended = mixed[0] if len(mixed) == 1 else jnp.concatenate(mixed, axis=0)
        part = jnp.dot(attended, w_out[...], preferred_element_type=F32)
        total = part if total is None else total + part
    out_ref[...] = total.astype(BF16)


def shifted_in(rows, fresh_row):
    frames = rows.shape[0]
    first = lax.broadcasted_iota(jnp.int32, (frames, 1), 0) == 0
    return jnp.where(first, fresh_row, pltpu.roll(rows, 1, 0))


def fresh_rows(place_ref, fresh_refs, step, tokens, split):
    me = place_ref[0]
    core = lax.rem(me, 2)
    own = []
    for ref in fresh_refs:
        value = ref[step].astype(F32)
        if split:
            value = jnp.where(core == 0, value[:tokens], value[tokens:])
        own.append(value)
    ordered = []
    for h in range(len(own)):
        pick = own[h]
        for d in range(len(own)):
            pick = jnp.where(lax.bitwise_xor(me, d) == h, own[d], pick)
        ordered.append(pick)
    return jnp.concatenate(ordered, axis=1)


def first_attention_kernel(
    split, chunk, place_ref, mine_ref, other_ref, f0, f1, f2, f3, norm_ref, mask_ref,
    qkv_me, qkv_other, out_me, out_other, cur_ref, part_ref,
):
    groups, cores, rows_here, _ = mine_ref.shape
    frames = norm_ref.shape[1]
    here = frames // groups
    tokens = rows_here // here
    share = qkv_me.shape[1]
    fresh = fresh_rows(place_ref, (f0, f1, f2, f3), 0, tokens, split)
    first_half = place_ref[0] < 2
    start, count = chunk
    at = slice(start * here, (start + count) * here)
    blocks = []
    for g in range(groups):
        mine = [mine_ref[g, c].astype(F32)[at, :share] for c in range(cores)]
        other = [other_ref[g, c].astype(F32)[at, :share] for c in range(cores)]
        left = [jnp.where(first_half, a, b) for a, b in zip(mine, other)]
        right = [jnp.where(first_half, b, a) for a, b in zip(mine, other)]
        blocks.append(jnp.concatenate(left + right, axis=1))
    current = []
    for p in range(count):
        rows = jnp.concatenate([b[p * here : (p + 1) * here] for b in blocks], axis=0)
        rows = shifted_in(rows, fresh[start + p : start + p + 1])
        cur_ref[p * frames : (p + 1) * frames, :] = rows.astype(BF16)
        current.append(rows)
    attention_rows(current, norm_ref, mask_ref, (qkv_me, qkv_other, out_me, out_other), part_ref)


def next_attention_kernel(
    split, chunk, all_tokens, place_ref, old_ref, after_ref, mine_ref, other_ref, f0, f1, f2, f3,
    norm_ref, gate_ref, pair_ref, mask_ref,
    qkv_me, qkv_other, out_me, out_other, cur_ref, part_ref,
):
    frames = norm_ref.shape[1]
    start, count = chunk
    fresh = fresh_rows(place_ref, (f0, f1, f2, f3), 1, all_tokens, split)
    keep, layer = pair_ref[:, 0:1], pair_ref[:, 1:2]
    current = []
    for p in range(count):
        at = slice(p * frames, (p + 1) * frames)
        total = mine_ref[at, :].astype(F32) + other_ref[at, :].astype(F32)
        rows = keep * old_ref[at, :].astype(F32) + layer * (
            after_ref[at, :].astype(F32) + gate_ref[0] * total
        )
        rows = shifted_in(rows, fresh[start + p : start + p + 1]).astype(BF16)
        cur_ref[at, :] = rows
        current.append(rows.astype(F32))
    attention_rows(current, norm_ref, mask_ref, (qkv_me, qkv_other, out_me, out_other), part_ref)


def attention_call(kernel, arrays, rows, features):
    return pl.pallas_call(
        kernel,
        out_shape=(jax.ShapeDtypeStruct((rows, features), BF16),) * 2,
        in_specs=[SMEM_SPEC] + [VMEM_SPEC] * (len(arrays) - 1),
        out_specs=(VMEM_SPEC,) * 2,
        compiler_params=params(),
        name="attention",
    )(*arrays)


def gelu(x):
    inner = math.sqrt(2.0 / math.pi) * (x + 0.044715 * (x * x * x))
    return x * (0.5 * (1.0 + jnp.tanh(inner)))


def pieces_of(width, size):
    return [(s, min(size, width - s)) for s in range(0, width, size)]


def feed_kernel(
    halves, place_ref, cur_ref, mine_ref, other_ref, mod_ref,
    fc1_me, fc1_other, fc2_me, fc2_other, *rest,
):
    outs, hidden_ref = rest[:-1], rest[-1]
    after_ref = outs[0]
    frames = mod_ref.shape[1]
    tokens = cur_ref.shape[0] // frames
    normed = []
    for p in range(tokens):
        at = slice(p * frames, (p + 1) * frames)
        total = mine_ref[at, :].astype(F32) + other_ref[at, :].astype(F32)
        after = (cur_ref[at, :].astype(F32) + mod_ref[0] * total).astype(BF16)
        after_ref[at, :] = after
        normed.append(normalise(after.astype(F32), mod_ref[1], mod_ref[2]).astype(BF16))
    normed = normed[0] if tokens == 1 else jnp.concatenate(normed, axis=0)
    units, features = fc2_me.shape
    for side, w1 in enumerate((fc1_me, fc1_other)):
        for start, size in pieces_of(units, 256):
            hidden = gelu(
                jnp.dot(normed, w1[:, start : start + size], preferred_element_type=F32)
            )
            hidden_ref[:, side * units + start : side * units + start + size] = hidden.astype(BF16)

    def product(at):
        return jnp.dot(
            hidden_ref[:, :units], fc2_me[:, at], preferred_element_type=F32
        ) + jnp.dot(hidden_ref[:, units:], fc2_other[:, at], preferred_element_type=F32)

    if not halves:
        for start, size in pieces_of(features, 256):
            at = slice(start, start + size)
            outs[1][:, at] = product(at).astype(BF16)
        return
    total = product(slice(None))
    left, right = total[:, : features // 2], total[:, features // 2 :]
    first_half = place_ref[0] < 2
    outs[1][...] = jnp.where(first_half, left, right).astype(BF16)
    outs[2][...] = jnp.where(first_half, right, left).astype(BF16)


def feed_call(place, cur, mine, other, mod, weights, halves):
    rows, features = cur.shape
    shape = jax.ShapeDtypeStruct((rows, features), BF16)
    half = jax.ShapeDtypeStruct((rows, features // 2), BF16)
    outs = (shape, half, half) if halves else (shape, shape)
    return pl.pallas_call(
        functools.partial(feed_kernel, halves),
        out_shape=outs,
        in_specs=[SMEM_SPEC] + [VMEM_SPEC] * 8,
        out_specs=(VMEM_SPEC,) * len(outs),
        scratch_shapes=[pltpu.VMEM((rows, 2 * weights[0].shape[1]), BF16)],
        compiler_params=params(),
        name="feed",
    )(place, cur, mine, other, mod, *weights)


def finish_kernel(chunks, place_ref, gate_ref, pair_ref, *refs):
    out_ref = refs[-1]
    groups, cores, _, share = out_ref.shape
    _, frames, features = gate_ref.shape
    here = frames // groups
    half = features // 2
    first_half = place_ref[0] < 2
    keep, layer = pair_ref[:, 0:1], pair_ref[:, 1:2]

    def mine(value):
        return jnp.where(first_half, value[:, :half], value[:, half:])

    gate = mine(gate_ref[0])
    results = []
    for n in range(chunks):
        old_ref, after_ref, mine_ref, other_ref = refs[4 * n : 4 * n + 4]
        for p in range(old_ref.shape[0] // frames):
            at = slice(p * frames, (p + 1) * frames)
            total = mine_ref[at, :].astype(F32) + other_ref[at, :].astype(F32)
            results.append(
                keep * mine(old_ref[at, :].astype(F32))
                + layer * (mine(after_ref[at, :].astype(F32)) + gate * total)
            )
    for c in range(cores):
        shares = [r[:, c * share : (c + 1) * share] for r in results]
        for g in range(groups):
            rows = [s[g * here : (g + 1) * here] for s in shares]
            out_ref[g, c] = jnp.concatenate(rows, axis=0).astype(BF16)


def finish(place, gate, pair, parts, groups):
    features = gate.shape[2]
    rows = sum(part[0].shape[0] for part in parts)
    arrays = [array for part in parts for array in part]
    return pl.pallas_call(
        functools.partial(finish_kernel, len(parts)),
        out_shape=jax.ShapeDtypeStruct((groups, 2, rows // groups, features // 4), BF16),
        in_specs=[SMEM_SPEC] + [VMEM_SPEC] * (2 + len(arrays)),
        out_specs=VMEM_SPEC,
        compiler_params=params(),
        name="finish",
    )(place, gate, pair, *arrays)


def unpack_kernel(rows_ref, out_ref, wide_ref):
    frames, tokens, width = out_ref.shape
    slabs = wide_ref.shape[0]
    for s in range(slabs):
        value = rows_ref[:, s * LANES : min((s + 1) * LANES, width)].astype(F32)
        wide_ref[s, :, : value.shape[1]] = value
    for i in range(frames):
        pieces = [wide_ref[s, pl.ds(i, tokens, stride=frames), :] for s in range(slabs)]
        out_ref[i] = jnp.concatenate(pieces, axis=1)[:, :width].astype(BF16)


def unpack(rows, frames):
    count, width = rows.shape
    wide = -(-width // LANES) * LANES
    return pl.pallas_call(
        unpack_kernel,
        out_shape=jax.ShapeDtypeStruct((frames, count // frames, width), BF16),
        in_specs=[VMEM_SPEC],
        out_specs=VMEM_SPEC,
        scratch_shapes=[pltpu.VMEM((wide // LANES, count, LANES), F32)],
        compiler_params=params(),
        name="unpack",
    )(rows)


SWAP = [(0, 1), (1, 0)]


def on_device(
    latents, fresh, noise_level, window_mask, mod_table, keep_coef, layer_coef,
    w_qkv, w_out, w_fc1, w_fc2,
):
    here, tokens_all, share = latents.shape
    features = mod_table.shape[2]
    groups = lax.axis_size("frame")
    frames = groups * here
    frame_index = lax.axis_index("frame")
    y_index, core_index = lax.axis_index("y"), lax.axis_index("core")
    place = (2 * y_index + core_index).astype(jnp.int32).reshape(1)
    group_tokens = tokens_all // groups
    split = group_tokens % 2 == 0
    tokens = group_tokens // 2 if split else group_tokens
    block = max(frames, LANES)

    positions = (
        frame_index * here
        + jnp.arange(here, dtype=jnp.int32)[:, None]
        + jnp.arange(OFFSETS, dtype=jnp.int32)[None, :]
        - W
    )
    allowed = (window_mask == 1) & (positions >= 0) & (positions < frames)
    meta = jnp.concatenate([noise_level[:, None], allowed.astype(jnp.int32)], axis=1)

    fresh_here = lax.dynamic_slice_in_dim(fresh, frame_index * group_tokens, group_tokens, 1)
    fresh_parts = (
        fresh_here,
        lax.ppermute(fresh_here, "core", SWAP),
        lax.ppermute(fresh_here, "y", SWAP),
        lax.ppermute(fresh_here, ("y", "core"), [(i, i ^ 3) for i in range(4)]),
    )
    swap_core = functools.partial(lax.ppermute, axis_name="core", perm=SWAP)
    swap_y = functools.partial(lax.ppermute, axis_name="y", perm=SWAP)
    w_qkv = jnp.swapaxes(w_qkv, 1, 2)
    attention_weights = (w_qkv, swap_core(w_qkv), w_out, swap_core(w_out))
    feed_weights = (w_fc1, swap_core(w_fc1), w_fc2, swap_core(w_fc2))

    payload = make_payload(latents, meta)
    wide = payload.shape[1]
    if split:
        payload = payload.reshape(groups * 2, tokens * here, wide)
        received = lax.all_to_all(payload, ("frame", "core"), 0, 0, tiled=True)
        received = received.reshape(groups, 2, tokens * here, wide)
    else:
        payload = payload.reshape(groups, tokens * here, wide)
        received = lax.all_to_all(payload, "frame", 0, 0, tiled=True)
        partner = swap_core(received)
        first = core_index == 0
        received = jnp.stack(
            [jnp.where(first, received, partner), jnp.where(first, partner, received)], axis=1
        )
    received_other = swap_y(received)
    norm_mod, feed_mod, gate_mod, pair, mask = prepare(
        received[:, 0, :here, share:],
        jnp.swapaxes(mod_table, 0, 1),
        jnp.stack([keep_coef, layer_coef]),
        block,
    )

    chunk_count = 2 if tokens % 2 == 0 and tokens * frames // 2 % block == 0 else 1
    size = tokens // chunk_count
    chunks = [(n * size, size) for n in range(chunk_count)]
    rows = size * frames

    state = []
    for chunk in chunks:
        current, part = attention_call(
            functools.partial(first_attention_kernel, split, chunk),
            (place, received, received_other) + fresh_parts + (norm_mod, mask) + attention_weights,
            rows, features,
        )
        state.append((current, part, swap_y(part)))
    fed = []
    for current, part, part_other in state:
        after, feed = feed_call(place, current, part, part_other, feed_mod, feed_weights, False)
        fed.append((current, after, feed, swap_y(feed)))
    state = []
    for chunk, arrays in zip(chunks, fed):
        current, part = attention_call(
            functools.partial(next_attention_kernel, split, chunk, tokens),
            (place,) + arrays + fresh_parts + (norm_mod, gate_mod, pair, mask) + attention_weights,
            rows, features,
        )
        state.append((current, part, swap_y(part)))
    parts = []
    for current, part, part_other in state:
        after, feed_here, feed_there = feed_call(
            place, current, part, part_other, feed_mod, feed_weights, True
        )
        parts.append((current, after, feed_here, swap_y(feed_there)))
    result = finish(place, gate_mod, pair, parts, groups)
    if split:
        result = result.reshape(groups * 2, tokens * here, share)
        result = lax.all_to_all(result, ("frame", "core"), 0, 0, tiled=True)
    else:
        result = jnp.where(core_index == 0, result[:, 0], result[:, 1])
        result = lax.all_to_all(result, "frame", 0, 0, tiled=True)
    return unpack(result.reshape(tokens_all * here, share), here)


def solution(mesh):
    groups, heads = mesh.shape["frame"], mesh.shape["head"]
    inner = Mesh(mesh.devices.reshape(groups, heads // 2, 2), ("frame", "y", "core"))
    head = ("y", "core")
    in_specs = (
        P("frame", None, head),
        P(None, None, head),
        P("frame"),
        P("frame", None),
        P(),
        P(),
        P(),
        P(None, None, head),
        P(head, None),
        P(None, head),
        P(head, None),
    )
    return jax.shard_map(
        on_device, mesh=inner, in_specs=in_specs, out_specs=P("frame", None, head), check_vma=False
    )
```

```python
import functools
import math

import jax
import jax.numpy as jnp
from jax import lax
from jax.experimental import pallas as pl
from jax.experimental.pallas import tpu as pltpu
from jax.sharding import Mesh, PartitionSpec as P

HD = 72
W = 8
OFFSETS = 2 * W + 1
EPSILON = 1e-06
F32 = jnp.float32
BF16 = jnp.bfloat16
LANES = 128
VMEM_SPEC = pl.BlockSpec(memory_space=pltpu.VMEM)
SMEM_SPEC = pl.BlockSpec(memory_space=pltpu.SMEM)
HBM_SPEC = pl.BlockSpec(memory_space=pltpu.HBM)


def in_hbm(*arrays):
    return [pltpu.with_memory_space_constraint(array, pltpu.HBM) for array in arrays]


def params(*arrays):
    held = sum(math.prod(a.shape) * jnp.dtype(a.dtype).itemsize for a in arrays)
    return pltpu.CompilerParams(vmem_limit_bytes=held + 8 * 1024 * 1024)


def tiles_of(share):
    return share // LANES, share % LANES


def normalise(values, shift_rows, scale_rows):
    center = values - jnp.mean(values, axis=-1, keepdims=True)
    spread = jnp.mean(center * center, axis=-1, keepdims=True)
    return center * lax.rsqrt(spread + EPSILON) * (1.0 + scale_rows) + shift_rows


def payload_kernel(
    frames, frame_far, level_far, window_far, x_far, fresh_far, out_ref,
    rows_ref, frame_ref, level_ref, window_ref, x_ref, fresh_ref, sems,
):
    fars = (x_far, window_far, level_far, frame_far, fresh_far)
    nears = (x_ref, window_ref, level_ref, frame_ref, fresh_ref)
    copies = [pltpu.make_async_copy(a, b, sems.at[n]) for n, (a, b) in enumerate(zip(fars, nears))]
    for copy in copies:
        copy.start()
    for copy in copies:
        copy.wait()
    here, _, share = x_ref.shape
    targets, chunks, _, _ = out_ref.shape
    full, rest = tiles_of(share)
    size = x_ref.shape[1] // (targets * chunks)
    row = lax.broadcasted_iota(jnp.int32, (here, 1), 0)
    level = jnp.zeros((here, 1), jnp.int32)
    for i in range(here):
        level = jnp.where(row == i, level_ref[i], level)
    offset = lax.broadcasted_iota(jnp.int32, (here, OFFSETS), 1)
    position = frame_ref[0] * here + row + offset - W
    allowed = (window_ref[...] == 1) & (position >= 0) & (position < frames)
    meta = jnp.concatenate([level.astype(F32), allowed.astype(jnp.int32).astype(F32)], axis=1)
    tokens = x_ref.shape[1]
    piece = share // here
    blank = LANES - size * rest - 1 - OFFSETS - piece
    later = fresh_ref[1].astype(F32)
    for j in range(here):
        cut = later[:, j * piece : (j + 1) * piece]
        cut = jnp.concatenate([cut, jnp.zeros((tokens, LANES - piece), F32)], axis=1)
        rows_ref[full + 1, pl.ds(j, tokens, stride=here), :] = cut
    sent = lax.rem(frame_ref[0], size)
    for i in range(here):
        value = x_ref[i].astype(F32)
        if i == here - 1:
            leaves = (frame_ref[0] + 1) * here == frames
            value = jnp.where(leaves, fresh_ref[0].astype(F32), value)
        for t in range(full):
            rows_ref[t, pl.ds(i, tokens, stride=here), :] = value[:, t * LANES : (t + 1) * LANES]
        rows_ref[full, pl.ds(i, tokens, stride=here), :] = jnp.concatenate(
            [value[:, full * LANES :], jnp.zeros((tokens, LANES - rest), F32)], axis=1
        )
    for d in range(targets):
        for n in range(chunks):
            first = (d * chunks + n) * size * here
            pieces = [rows_ref[t, first : first + size * here, :] for t in range(full)]
            tails = [
                rows_ref[full, first + p * here : first + (p + 1) * here, :][:, :rest]
                for p in range(size)
            ]
            cuts = [
                rows_ref[full + 1, first + p * here : first + (p + 1) * here, :][:, :piece]
                for p in range(size)
            ]
            cut = cuts[0]
            for p in range(1, size):
                cut = jnp.where(sent == p, cuts[p], cut)
            tails += [meta, cut]
            if blank:
                tails.append(jnp.zeros((here, blank), F32))
            pieces.append(jnp.concatenate(tails, axis=1))
            out_ref[d, n] = jnp.concatenate(pieces, axis=0).astype(BF16)


def make_payload(frame_index, noise_level, window_mask, x, fresh, frames, targets, chunks):
    here, tokens, share = x.shape
    full, rest = tiles_of(share)
    size = tokens // (targets * chunks)
    out = jax.ShapeDtypeStruct((targets, chunks, (full * size + 1) * here, LANES), BF16)
    scratch = jax.ShapeDtypeStruct((full + 2, tokens * here, LANES), F32)
    return pl.pallas_call(
        functools.partial(payload_kernel, frames),
        out_shape=out,
        in_specs=[HBM_SPEC] * 5,
        out_specs=VMEM_SPEC,
        scratch_shapes=[
            pltpu.VMEM(scratch.shape, F32),
            pltpu.SMEM(frame_index.shape, jnp.int32),
            pltpu.SMEM(noise_level.shape, jnp.int32),
            pltpu.VMEM(window_mask.shape, jnp.int32),
            pltpu.VMEM(x.shape, BF16),
            pltpu.VMEM(fresh.shape, BF16),
            pltpu.SemaphoreType.DMA((5,)),
        ],
        compiler_params=params(x, fresh, out, scratch),
        name="payload",
    )(*in_hbm(frame_index, noise_level, window_mask, x, fresh))


def fresh_piece(block, size, here, share):
    _, rest = tiles_of(share)
    piece = share // here
    first = size * rest + 1 + OFFSETS
    tail = block[-here:, first : first + piece]
    return jnp.concatenate([tail[j : j + 1] for j in range(here)], axis=1)


def chunk_rows(block, size, here, share):
    full, rest = tiles_of(share)
    tail = block[full * size * here :]
    result = []
    for p in range(size):
        pieces = [block[(t * size + p) * here : (t * size + p + 1) * here] for t in range(full)]
        result.append(jnp.concatenate(pieces + [tail[:, p * rest : (p + 1) * rest]], axis=1))
    return result


def prepare_kernel(
    here, lane_at, place_ref, received_ref, table_ref, keep_ref, layer_ref,
    norm_ref, feed_ref, gate_ref, pair_ref, mask_ref, flag_ref,
):
    flag_ref[...] = jnp.where(place_ref[0] < 2, jnp.ones_like(flag_ref), 0.0)
    groups = received_ref.shape[0]
    frames = groups * here
    levels = table_ref.shape[1]
    meta = [received_ref[g, 0].astype(F32)[-here:, lane_at:] for g in range(groups)]
    meta = jnp.concatenate(meta, axis=0)
    level = meta[:, 0:1]
    ids = lax.broadcasted_iota(jnp.int32, (frames, levels), 1).astype(F32)
    hot = level == ids
    hot_bf = hot.astype(BF16)
    targets = [(norm_ref, 0), (norm_ref, 1), (feed_ref, 0), (feed_ref, 1), (feed_ref, 2), (gate_ref, 0)]
    for j, (target, at) in enumerate(targets):
        rows = table_ref[j]
        high = rows.astype(BF16)
        rest = rows - high.astype(F32)
        middle = rest.astype(BF16)
        low = (rest - middle.astype(F32)).astype(BF16)
        total = jnp.dot(hot_bf, high, preferred_element_type=F32)
        total += jnp.dot(hot_bf, middle, preferred_element_type=F32)
        total += jnp.dot(hot_bf, low, preferred_element_type=F32)
        target[at] = total
    keep = jnp.sum(jnp.where(hot, keep_ref[...], 0.0), axis=1, keepdims=True)
    layer = jnp.sum(jnp.where(hot, layer_ref[...], 0.0), axis=1, keepdims=True)
    lane = lax.broadcasted_iota(jnp.int32, (frames, LANES), 1)
    pair_ref[...] = jnp.where(lane == 0, keep, layer)

    block = mask_ref.shape[0]
    row = lax.broadcasted_iota(jnp.int32, (frames, block), 0)
    column = lax.broadcasted_iota(jnp.int32, (frames, block), 1)
    for t in range(block // frames):
        distance = column - t * frames - row
        inside = (column >= t * frames) & (column < (t + 1) * frames)
        is_open = jnp.zeros((frames, block), F32)
        for o in range(OFFSETS):
            is_open = jnp.where(distance == o - W, meta[:, 1 + o : 2 + o], is_open)
        mask_ref[t * frames : (t + 1) * frames, :] = jnp.where(inside, is_open, 0.0)


def prepare(place, received, table, keep, layer, here, lane_at, block):
    frames = received.shape[0] * here
    features = table.shape[2]
    outs = (
        jax.ShapeDtypeStruct((2, frames, features), F32),
        jax.ShapeDtypeStruct((3, frames, features), F32),
        jax.ShapeDtypeStruct((1, frames, features), F32),
        jax.ShapeDtypeStruct((frames, LANES), F32),
        jax.ShapeDtypeStruct((block, block), F32),
        jax.ShapeDtypeStruct((8, LANES), F32),
    )
    return pl.pallas_call(
        functools.partial(prepare_kernel, here, lane_at),
        out_shape=outs,
        in_specs=[SMEM_SPEC] + [VMEM_SPEC] * 4,
        out_specs=(VMEM_SPEC,) * len(outs),
        compiler_params=params(received, table, *outs),
        name="prepare",
    )(place, received, table, keep.reshape(1, -1), layer.reshape(1, -1))


def hold_kernel(places, *refs):
    sources, targets, sems = refs[: len(places)], refs[len(places) : -1], refs[-1]
    copies = []
    for source, (index, start) in zip(sources, places):
        rows = source.shape[0]
        parts = 3 if rows % 48 == 0 or rows % 3 == 0 and len(source.shape) > 2 else 1
        for n in range(parts):
            size = rows // parts
            copies.append(
                pltpu.make_async_copy(
                    source.at[pl.ds(n * size, size)],
                    targets[index].at[pl.ds(start + n * size, size)],
                    sems.at[len(copies)],
                )
            )
            copies[-1].start()
    for copy in copies:
        copy.wait()


def hold(*groups):
    places, outs = [], []
    for index, group in enumerate(groups):
        start = 0
        for array in group:
            places.append((index, start))
            start += array.shape[0]
        outs.append(jax.ShapeDtypeStruct((start,) + group[0].shape[1:], group[0].dtype))
    arrays = [array for group in groups for array in group]
    held = sum(math.prod(o.shape) * jnp.dtype(o.dtype).itemsize for o in outs)
    return pl.pallas_call(
        functools.partial(hold_kernel, tuple(places)),
        out_shape=tuple(outs),
        in_specs=[HBM_SPEC] * len(arrays),
        out_specs=(VMEM_SPEC,) * len(outs),
        scratch_shapes=[pltpu.SemaphoreType.DMA((3 * len(arrays),))],
        compiler_params=params(*outs),
        cost_estimate=pl.CostEstimate(flops=0, bytes_accessed=2 * held, transcendentals=0),
        name="hold",
    )(*in_hbm(*arrays))


def attention_rows(current, norm_ref, mask_ref, weights, out_ref):
    normed = [normalise(rows, norm_ref[0], norm_ref[1]).astype(BF16) for rows in current]
    normed = normed[0] if len(normed) == 1 else jnp.concatenate(normed, axis=0)
    qkv_me, qkv_other = weights
    share = qkv_me.shape[1]
    heads = share // HD
    block = mask_ref.shape[0]
    count = normed.shape[0] // block
    is_open = mask_ref[...] > 0.5
    lane = lax.broadcasted_iota(jnp.int32, (1, share), 1)
    head_lanes = [
        ((lane >= HD * h) & (lane < HD * (h + 1))).astype(jnp.int32).astype(F32).astype(BF16)
        for h in range(heads)
    ]
    scale = math.log2(math.e) / math.sqrt(HD)
    projected = []
    for side, qkv in enumerate((qkv_me, qkv_other)):
        projected.append(
            [
                lax.dot_general(
                    normed, qkv[t], (((1,), (1,)), ((), ())), preferred_element_type=F32
                ).astype(BF16)
                for t in range(3)
            ]
        )
    units = [(side, slice(b * block, (b + 1) * block)) for side in range(2) for b in range(count)]
    scores = []
    for side, at in units:
        query, key = projected[side][0][at], projected[side][1][at]
        keys = jnp.concatenate([key * lanes for lanes in head_lanes], axis=0)
        raw = lax.dot_general(query, keys, (((1,), (1,)), ((), ())), preferred_element_type=F32)
        scores += [
            jnp.where(is_open, raw[:, h * block : (h + 1) * block], -1e30) for h in range(heads)
        ]
    tops = [jnp.max(s, axis=-1, keepdims=True) for s in scores]
    weights_of = [jnp.exp2((s - t) * scale) for s, t in zip(scores, tops)]
    sums = [jnp.sum(w, axis=-1, keepdims=True) for w in weights_of]
    shares = [(w / total).astype(BF16) for w, total in zip(weights_of, sums)]
    attended = []
    for n, (side, at) in enumerate(units):
        value = projected[side][2][at]
        values = jnp.concatenate([value * lanes for lanes in head_lanes], axis=0)
        row = jnp.concatenate(shares[n * heads : (n + 1) * heads], axis=1)
        attended.append(jnp.dot(row, values, preferred_element_type=F32).astype(BF16))
    for n, (side, at) in enumerate(units):
        out_ref[at, side * share : (side + 1) * share] = attended[n]


def shifted_in(rows, fresh_row):
    frames = rows.shape[0]
    first = lax.broadcasted_iota(jnp.int32, (frames, 1), 0) == 0
    return jnp.where(first, fresh_row, pltpu.roll(rows, 1, 0))


def first_attention_kernel(
    count, mine_ref, other_ref, flag_ref, norm_ref, mask_ref,
    qkv_me, qkv_other, cur_ref, part_ref, fresh_ref,
):
    groups, cores = mine_ref.shape[:2]
    frames = norm_ref.shape[1]
    here = frames // groups
    share = qkv_me.shape[1]
    first_half = flag_ref[0:1, :] > 0.5
    blocks = []
    for g in range(groups):
        left, right = [], []
        for c in range(cores):
            mine, other = mine_ref[g, c].astype(F32), other_ref[g, c].astype(F32)
            left.append(jnp.where(first_half, mine, other))
            right.append(jnp.where(first_half, other, mine))
        if g < count:
            cuts = [fresh_piece(block, count, here, share) for block in left + right]
            fresh_ref[g : g + 1, :] = jnp.concatenate(cuts, axis=1)
        blocks.append([chunk_rows(block, count, here, share) for block in left + right])
    current = []
    for p in range(count):
        rows = [jnp.concatenate([part[p] for part in parts], axis=1) for parts in blocks]
        rows = pltpu.roll(jnp.concatenate(rows, axis=0), 1, 0)
        cur_ref[p * frames : (p + 1) * frames, :] = rows.astype(BF16)
        current.append(rows)
    attention_rows(current, norm_ref, mask_ref, (qkv_me, qkv_other), part_ref)


def next_attention_kernel(
    count, old_ref, after_ref, mine_ref, other_ref, fresh_ref, norm_ref, gate_ref, pair_ref,
    mask_ref, qkv_me, qkv_other, cur_ref, part_ref,
):
    frames = norm_ref.shape[1]
    keep, layer = pair_ref[:, 0:1], pair_ref[:, 1:2]
    current = []
    for p in range(count):
        at = slice(p * frames, (p + 1) * frames)
        total = mine_ref[at, :].astype(F32) + other_ref[at, :].astype(F32)
        rows = keep * old_ref[at, :].astype(F32) + layer * (
            after_ref[at, :].astype(F32) + gate_ref[0] * total
        )
        rows = shifted_in(rows, fresh_ref[p : p + 1, :]).astype(BF16)
        cur_ref[at, :] = rows
        current.append(rows.astype(F32))
    attention_rows(current, norm_ref, mask_ref, (qkv_me, qkv_other), part_ref)


def attention_call(kernel, arrays, rows, features, fresh_count=0):
    outs = (
        jax.ShapeDtypeStruct((rows, features), BF16),
        jax.ShapeDtypeStruct((rows, features // 2), BF16),
    )
    if fresh_count:
        outs += (jax.ShapeDtypeStruct((fresh_count, features), F32),)
    return pl.pallas_call(
        kernel,
        out_shape=outs,
        in_specs=[VMEM_SPEC] * len(arrays),
        out_specs=(VMEM_SPEC,) * len(outs),
        compiler_params=params(*arrays, *outs),
        name="attention",
    )(*arrays)


def gelu(x):
    inner = math.sqrt(2.0 / math.pi) * (x + 0.044715 * (x * x * x))
    return x * (0.5 * (1.0 + jnp.tanh(inner)))


def pieces_of(width, size):
    return [(s, min(size, width - s)) for s in range(0, width, size)]


def feed_kernel(
    halves, flag_ref, cur_ref, mine_ref, other_ref, mod_ref,
    out_all, fc1_me, fc1_other, fc2_me, fc2_other, *rest,
):
    outs, hidden_ref = rest[:-1], rest[-1]
    after_ref = outs[0]
    frames = mod_ref.shape[1]
    tokens = cur_ref.shape[0] // frames
    normed = []
    half = mine_ref.shape[1]
    attention_total = jnp.dot(mine_ref[...], out_all[:half], preferred_element_type=F32) + jnp.dot(
        other_ref[...], out_all[half:], preferred_element_type=F32
    )
    for p in range(tokens):
        at = slice(p * frames, (p + 1) * frames)
        after = (cur_ref[at, :].astype(F32) + mod_ref[0] * attention_total[at]).astype(BF16)
        after_ref[at, :] = after
        normed.append(normalise(after.astype(F32), mod_ref[1], mod_ref[2]).astype(BF16))
    normed = normed[0] if tokens == 1 else jnp.concatenate(normed, axis=0)
    units, features = fc2_me.shape
    for side, w1 in enumerate((fc1_me, fc1_other)):
        for start, size in pieces_of(units, 256):
            hidden = gelu(
                jnp.dot(normed, w1[:, start : start + size], preferred_element_type=F32)
            )
            hidden_ref[:, side * units + start : side * units + start + size] = hidden.astype(BF16)

    def product(at):
        return jnp.dot(
            hidden_ref[:, :units], fc2_me[:, at], preferred_element_type=F32
        ) + jnp.dot(hidden_ref[:, units:], fc2_other[:, at], preferred_element_type=F32)

    if not halves:
        for start, size in pieces_of(features, 256):
            at = slice(start, start + size)
            outs[1][:, at] = product(at).astype(BF16)
        return
    total = product(slice(None))
    left, right = total[:, : features // 2], total[:, features // 2 :]
    first_half = flag_ref[0:1, 0:1] > 0.5
    outs[1][...] = jnp.where(first_half, left, right).astype(BF16)
    outs[2][...] = jnp.where(first_half, right, left).astype(BF16)


def feed_call(flag, cur, mine, other, mod, weights, halves):
    rows, features = cur.shape
    shape = jax.ShapeDtypeStruct((rows, features), BF16)
    half = jax.ShapeDtypeStruct((rows, features // 2), BF16)
    outs = (shape, half, half) if halves else (shape, shape)
    return pl.pallas_call(
        functools.partial(feed_kernel, halves),
        out_shape=outs,
        in_specs=[VMEM_SPEC] * 10,
        out_specs=(VMEM_SPEC,) * len(outs),
        scratch_shapes=[pltpu.VMEM((rows, 2 * weights[1].shape[1]), BF16)],
        compiler_params=params(cur, mine, other, mod, *weights, *outs),
        name="feed",
    )(flag, cur, mine, other, mod, *weights)


def finish_kernel(chunks, flag_ref, gate_ref, pair_ref, *refs):
    out_ref = refs[-1]
    groups, cores = out_ref.shape[:2]
    _, frames, features = gate_ref.shape
    here = frames // groups
    half = features // 2
    share = half // cores
    full, rest = tiles_of(share)
    first_half = flag_ref[0:1, 0:1] > 0.5
    keep, layer = pair_ref[:, 0:1], pair_ref[:, 1:2]

    def mine(value):
        return jnp.where(first_half, value[:, :half], value[:, half:])

    gate = mine(gate_ref[0])
    results = []
    for n in range(chunks):
        old_ref, after_ref, mine_ref, other_ref = refs[4 * n : 4 * n + 4]
        for p in range(old_ref.shape[0] // frames):
            at = slice(p * frames, (p + 1) * frames)
            total = mine_ref[at, :].astype(F32) + other_ref[at, :].astype(F32)
            results.append(
                keep * mine(old_ref[at, :].astype(F32))
                + layer * (mine(after_ref[at, :].astype(F32)) + gate * total)
            )
    unused = LANES - len(results) * rest
    for c in range(cores):
        shares = [r[:, c * share : (c + 1) * share] for r in results]
        for g in range(groups):
            rows = [s[g * here : (g + 1) * here] for s in shares]
            pieces = [r[:, t * LANES : (t + 1) * LANES] for t in range(full) for r in rows]
            tails = [r[:, full * LANES :] for r in rows]
            if unused:
                tails.append(jnp.zeros((here, unused), F32))
            pieces.append(jnp.concatenate(tails, axis=1))
            out_ref[g, c] = jnp.concatenate(pieces, axis=0).astype(BF16)


def finish(flag, gate, pair, parts, groups):
    _, frames, features = gate.shape
    tokens = sum(part[0].shape[0] for part in parts) // frames
    full, _ = tiles_of(features // 4)
    arrays = [array for part in parts for array in part]
    out = jax.ShapeDtypeStruct((groups, 2, (full * tokens + 1) * (frames // groups), LANES), BF16)
    return pl.pallas_call(
        functools.partial(finish_kernel, len(parts)),
        out_shape=out,
        in_specs=[VMEM_SPEC] * (3 + len(arrays)),
        out_specs=VMEM_SPEC,
        compiler_params=params(gate, pair, out, *arrays),
        name="finish",
    )(flag, gate, pair, *arrays)


def unpack_kernel(rows_ref, out_ref, wide_ref):
    here, tokens, share = out_ref.shape
    sources = rows_ref.shape[0]
    size = tokens // sources
    full, rest = tiles_of(share)
    for d in range(sources):
        block = rows_ref[d].astype(F32)
        first = d * size * here
        for t in range(full):
            wide_ref[t, first : first + size * here, :] = block[t * size * here : (t + 1) * size * here]
        tail = block[full * size * here :]
        for p in range(size):
            wide_ref[full, first + p * here : first + (p + 1) * here, :rest] = tail[
                :, p * rest : (p + 1) * rest
            ]
    for i in range(here):
        pieces = [wide_ref[t, pl.ds(i, tokens, stride=here), :] for t in range(full + 1)]
        out_ref[i] = jnp.concatenate(pieces, axis=1)[:, :share].astype(BF16)


def unpack(rows, here, tokens, share):
    full, _ = tiles_of(share)
    out = jax.ShapeDtypeStruct((here, tokens, share), BF16)
    scratch = jax.ShapeDtypeStruct((full + 1, tokens * here, LANES), F32)
    return pl.pallas_call(
        unpack_kernel,
        out_shape=out,
        in_specs=[VMEM_SPEC],
        out_specs=VMEM_SPEC,
        scratch_shapes=[pltpu.VMEM(scratch.shape, F32)],
        compiler_params=params(rows, out, scratch),
        name="unpack",
    )(rows)


SWAP = [(0, 1), (1, 0)]


def on_device(
    latents, fresh, noise_level, window_mask, mod_table, keep_coef, layer_coef,
    w_qkv, w_out, w_fc1, w_fc2,
):
    here, tokens_all, share = latents.shape
    features = mod_table.shape[2]
    groups = lax.axis_size("frame")
    frames = groups * here
    frame_index = lax.axis_index("frame")
    y_index, core_index = lax.axis_index("y"), lax.axis_index("core")
    place = (2 * y_index + core_index).astype(jnp.int32).reshape(1)
    group_tokens = tokens_all // groups
    split = group_tokens % 2 == 0
    tokens = group_tokens // 2 if split else group_tokens
    block = max(frames, LANES)
    chunk_count = 2 if tokens % 2 == 0 and tokens * frames // 2 % block == 0 else 1
    size = tokens // chunk_count
    rows = size * frames

    swap_core = functools.partial(lax.ppermute, axis_name="core", perm=SWAP)
    swap_y = functools.partial(lax.ppermute, axis_name="y", perm=SWAP)
    w_qkv = jnp.swapaxes(w_qkv, 1, 2)
    out_far = swap_y(w_out)
    table, w_qkv, qkv_other, fc2_other, out_all = hold(
        (jnp.swapaxes(mod_table, 0, 1),),
        (w_qkv,),
        (swap_core(w_qkv),),
        (swap_core(w_fc2),),
        (w_out, swap_core(w_out), out_far, swap_core(out_far)),
    )
    attention_weights = (w_qkv, qkv_other)
    feed_weights = (out_all, w_fc1, swap_core(w_fc1), w_fc2, fc2_other)

    payload = make_payload(
        frame_index.astype(jnp.int32).reshape(1), noise_level, window_mask, latents, fresh,
        frames, tokens_all // tokens, chunk_count,
    )
    if split:
        received = lax.all_to_all(payload, ("frame", "core"), 0, 0, tiled=True)
        received = received.reshape((groups, 2) + received.shape[1:])
    else:
        received = lax.all_to_all(payload, "frame", 0, 0, tiled=True)
        partner = swap_core(received)
        first = core_index == 0
        received = jnp.stack(
            [jnp.where(first, received, partner), jnp.where(first, partner, received)], axis=1
        )
    arrived = [received[:, :, n] for n in range(chunk_count)]
    arrived_other = [swap_y(part) for part in arrived]
    norm_mod, feed_mod, gate_mod, pair, mask, flag = prepare(
        place, arrived[0], table, keep_coef, layer_coef, here, size * tiles_of(share)[1], block
    )

    state = []
    for mine, other in zip(arrived, arrived_other):
        current, part, later = attention_call(
            functools.partial(first_attention_kernel, size),
            (mine, other, flag, norm_mod, mask) + attention_weights,
            rows, features, size,
        )
        state.append((current, part, swap_y(part), later))
    fed = []
    for current, part, part_other, later in state:
        after, feed = feed_call(flag, current, part, part_other, feed_mod, feed_weights, False)
        fed.append((current, after, feed, swap_y(feed), later))
    state = []
    for arrays in fed:
        current, part = attention_call(
            functools.partial(next_attention_kernel, size),
            arrays + (norm_mod, gate_mod, pair, mask) + attention_weights,
            rows, features,
        )
        state.append((current, part, swap_y(part)))
    parts = []
    for current, part, part_other in state:
        after, feed_here, feed_there = feed_call(
            flag, current, part, part_other, feed_mod, feed_weights, True
        )
        parts.append((current, after, feed_here, swap_y(feed_there)))
    result = finish(flag, gate_mod, pair, parts, groups)
    if split:
        result = result.reshape((groups * 2,) + result.shape[2:])
        result = lax.all_to_all(result, ("frame", "core"), 0, 0, tiled=True)
    else:
        result = jnp.where(core_index == 0, result[:, 0], result[:, 1])
        result = lax.all_to_all(result, "frame", 0, 0, tiled=True)
    return unpack(result, here, tokens_all, share)


def solution(mesh):
    groups, heads = mesh.shape["frame"], mesh.shape["head"]
    inner = Mesh(mesh.devices.reshape(groups, heads // 2, 2), ("frame", "y", "core"))
    head = ("y", "core")
    in_specs = (
        P("frame", None, head),
        P(None, None, head),
        P("frame"),
        P("frame", None),
        P(),
        P(),
        P(),
        P(None, None, head),
        P(head, None),
        P(None, head),
        P(head, None),
    )
    return jax.shard_map(
        on_device, mesh=inner, in_specs=in_specs, out_specs=P("frame", None, head), check_vma=False
    )
```

```python
import functools
import math

import jax
import jax.numpy as jnp
from jax import lax
from jax.experimental import pallas as pl
from jax.experimental.pallas import tpu as pltpu
from jax.sharding import Mesh, PartitionSpec as P

HD = 72
W = 8
OFFSETS = 2 * W + 1
EPSILON = 1e-06
F32 = jnp.float32
BF16 = jnp.bfloat16
LANES = 128
VMEM_SPEC = pl.BlockSpec(memory_space=pltpu.VMEM)
SMEM_SPEC = pl.BlockSpec(memory_space=pltpu.SMEM)
HBM_SPEC = pl.BlockSpec(memory_space=pltpu.HBM)


def in_hbm(*arrays):
    return [pltpu.with_memory_space_constraint(array, pltpu.HBM) for array in arrays]


def params(*arrays):
    held = sum(math.prod(a.shape) * jnp.dtype(a.dtype).itemsize for a in arrays)
    return pltpu.CompilerParams(vmem_limit_bytes=held + 8 * 1024 * 1024)


def takes(microseconds):
    return pl.CostEstimate(
        flops=0, bytes_accessed=int(microseconds * 3.3e6), transcendentals=0
    )


def tiles_of(share):
    return share // LANES, share % LANES


def normalise(values, shift_rows, scale_rows):
    center = values - jnp.mean(values, axis=-1, keepdims=True)
    spread = jnp.mean(center * center, axis=-1, keepdims=True)
    return center * lax.rsqrt(spread + EPSILON) * (1.0 + scale_rows) + shift_rows


def payload_kernel(
    frames, frame_far, level_far, window_far, x_far, fresh_far, out_ref,
    rows_ref, frame_ref, level_ref, window_ref, x_ref, fresh_ref, sems,
):
    fars = (x_far, window_far, level_far, frame_far, fresh_far)
    nears = (x_ref, window_ref, level_ref, frame_ref, fresh_ref)
    copies = [pltpu.make_async_copy(a, b, sems.at[n]) for n, (a, b) in enumerate(zip(fars, nears))]
    for copy in copies:
        copy.start()
    for copy in copies:
        copy.wait()
    here, _, share = x_ref.shape
    targets, chunks, _, _ = out_ref.shape
    full, rest = tiles_of(share)
    size = x_ref.shape[1] // (targets * chunks)
    row = lax.broadcasted_iota(jnp.int32, (here, 1), 0)
    level = jnp.zeros((here, 1), jnp.int32)
    for i in range(here):
        level = jnp.where(row == i, level_ref[i], level)
    offset = lax.broadcasted_iota(jnp.int32, (here, OFFSETS), 1)
    position = frame_ref[0] * here + row + offset - W
    allowed = (window_ref[...] == 1) & (position >= 0) & (position < frames)
    meta = jnp.concatenate([level.astype(F32), allowed.astype(jnp.int32).astype(F32)], axis=1)
    tokens = x_ref.shape[1]
    piece = share // here
    blank = LANES - size * rest - 1 - OFFSETS - piece
    later = fresh_ref[1].astype(F32)
    for j in range(here):
        cut = later[:, j * piece : (j + 1) * piece]
        cut = jnp.concatenate([cut, jnp.zeros((tokens, LANES - piece), F32)], axis=1)
        rows_ref[full + 1, pl.ds(j, tokens, stride=here), :] = cut
    sent = lax.rem(frame_ref[0], size)
    for i in range(here):
        value = x_ref[i].astype(F32)
        if i == here - 1:
            leaves = (frame_ref[0] + 1) * here == frames
            value = jnp.where(leaves, fresh_ref[0].astype(F32), value)
        for t in range(full):
            rows_ref[t, pl.ds(i, tokens, stride=here), :] = value[:, t * LANES : (t + 1) * LANES]
        rows_ref[full, pl.ds(i, tokens, stride=here), :] = jnp.concatenate(
            [value[:, full * LANES :], jnp.zeros((tokens, LANES - rest), F32)], axis=1
        )
    for d in range(targets):
        for n in range(chunks):
            first = (d * chunks + n) * size * here
            pieces = [rows_ref[t, first : first + size * here, :] for t in range(full)]
            tails = [
                rows_ref[full, first + p * here : first + (p + 1) * here, :][:, :rest]
                for p in range(size)
            ]
            cuts = [
                rows_ref[full + 1, first + p * here : first + (p + 1) * here, :][:, :piece]
                for p in range(size)
            ]
            cut = cuts[0]
            for p in range(1, size):
                cut = jnp.where(sent == p, cuts[p], cut)
            tails += [meta, cut]
            if blank:
                tails.append(jnp.zeros((here, blank), F32))
            pieces.append(jnp.concatenate(tails, axis=1))
            out_ref[d, n] = jnp.concatenate(pieces, axis=0).astype(BF16)


def make_payload(frame_index, noise_level, window_mask, x, fresh, frames, targets, chunks):
    here, tokens, share = x.shape
    full, rest = tiles_of(share)
    size = tokens // (targets * chunks)
    out = jax.ShapeDtypeStruct((targets, chunks, (full * size + 1) * here, LANES), BF16)
    scratch = jax.ShapeDtypeStruct((full + 2, tokens * here, LANES), F32)
    return pl.pallas_call(
        functools.partial(payload_kernel, frames),
        out_shape=out,
        in_specs=[HBM_SPEC] * 5,
        out_specs=VMEM_SPEC,
        scratch_shapes=[
            pltpu.VMEM(scratch.shape, F32),
            pltpu.SMEM(frame_index.shape, jnp.int32),
            pltpu.SMEM(noise_level.shape, jnp.int32),
            pltpu.VMEM(window_mask.shape, jnp.int32),
            pltpu.VMEM(x.shape, BF16),
            pltpu.VMEM(fresh.shape, BF16),
            pltpu.SemaphoreType.DMA((5,)),
        ],
        compiler_params=params(x, fresh, out, scratch),
        cost_estimate=takes(2),
        name="payload",
    )(*in_hbm(frame_index, noise_level, window_mask, x, fresh))


def fresh_piece(block, size, here, share):
    _, rest = tiles_of(share)
    piece = share // here
    first = size * rest + 1 + OFFSETS
    tail = block[-here:, first : first + piece]
    return jnp.concatenate([tail[j : j + 1] for j in range(here)], axis=1)


def chunk_rows(block, size, here, share):
    full, rest = tiles_of(share)
    tail = block[full * size * here :]
    result = []
    for p in range(size):
        pieces = [block[(t * size + p) * here : (t * size + p + 1) * here] for t in range(full)]
        result.append(jnp.concatenate(pieces + [tail[:, p * rest : (p + 1) * rest]], axis=1))
    return result


def prepare_kernel(
    here, lane_at, places, place_ref, received_ref, table_far, keep_ref, layer_ref, *refs
):
    sources, refs = refs[: len(places)], refs[len(places) :]
    norm_ref, feed_ref, gate_ref, pair_ref, mask_ref, flag_ref = refs[:6]
    held, (table_ref, table_sems, sems) = refs[6:-3], refs[-3:]
    table_copies = start_copies(
        (table_far,), [(0, 0, 0, table_far.shape[0])], (table_ref,), table_sems
    )
    copies = start_copies(sources, places, held, sems)
    flag_ref[...] = jnp.where(place_ref[0] < 2, jnp.ones_like(flag_ref), 0.0)
    groups = received_ref.shape[0]
    frames = groups * here
    levels = table_ref.shape[1]
    meta = [received_ref[g, 0].astype(F32)[-here:, lane_at:] for g in range(groups)]
    meta = jnp.concatenate(meta, axis=0)
    level = meta[:, 0:1]
    ids = lax.broadcasted_iota(jnp.int32, (frames, levels), 1).astype(F32)
    hot = level == ids
    hot_bf = hot.astype(BF16)
    for copy in table_copies:
        copy.wait()
    targets = [(norm_ref, 0), (norm_ref, 1), (feed_ref, 0), (feed_ref, 1), (feed_ref, 2), (gate_ref, 0)]
    for j, (target, at) in enumerate(targets):
        rows = table_ref[j]
        high = rows.astype(BF16)
        rest = rows - high.astype(F32)
        middle = rest.astype(BF16)
        low = (rest - middle.astype(F32)).astype(BF16)
        total = jnp.dot(hot_bf, high, preferred_element_type=F32)
        total += jnp.dot(hot_bf, middle, preferred_element_type=F32)
        total += jnp.dot(hot_bf, low, preferred_element_type=F32)
        target[at] = total
    keep = jnp.sum(jnp.where(hot, keep_ref[...], 0.0), axis=1, keepdims=True)
    layer = jnp.sum(jnp.where(hot, layer_ref[...], 0.0), axis=1, keepdims=True)
    lane = lax.broadcasted_iota(jnp.int32, (frames, LANES), 1)
    pair_ref[...] = jnp.where(lane == 0, keep, layer)

    block = mask_ref.shape[0]
    row = lax.broadcasted_iota(jnp.int32, (frames, block), 0)
    column = lax.broadcasted_iota(jnp.int32, (frames, block), 1)
    for t in range(block // frames):
        distance = column - t * frames - row
        inside = (column >= t * frames) & (column < (t + 1) * frames)
        is_open = jnp.zeros((frames, block), F32)
        for o in range(OFFSETS):
            is_open = jnp.where(distance == o - W, meta[:, 1 + o : 2 + o], is_open)
        mask_ref[t * frames : (t + 1) * frames, :] = jnp.where(inside, is_open, 0.0)
    for copy in copies:
        copy.wait()


def prepare(place, received, table, keep, layer, weights, places, held, here, lane_at, block):
    frames = received.shape[0] * here
    features = table.shape[2]
    outs = (
        jax.ShapeDtypeStruct((2, frames, features), F32),
        jax.ShapeDtypeStruct((3, frames, features), F32),
        jax.ShapeDtypeStruct((1, frames, features), F32),
        jax.ShapeDtypeStruct((frames, LANES), F32),
        jax.ShapeDtypeStruct((block, block), F32),
        jax.ShapeDtypeStruct((8, LANES), F32),
    ) + tuple(jax.ShapeDtypeStruct(shape, BF16) for shape in held)
    (table,) = in_hbm(table)
    return pl.pallas_call(
        functools.partial(prepare_kernel, here, lane_at, tuple(places)),
        out_shape=outs,
        in_specs=[SMEM_SPEC, VMEM_SPEC, HBM_SPEC, VMEM_SPEC, VMEM_SPEC]
        + [HBM_SPEC] * len(weights),
        out_specs=(VMEM_SPEC,) * len(outs),
        scratch_shapes=[
            pltpu.VMEM(table.shape, F32),
            pltpu.SemaphoreType.DMA((3,)),
            pltpu.SemaphoreType.DMA((3 * len(weights),)),
        ],
        compiler_params=params(received, table, *outs),
        cost_estimate=takes(5),
        name="prepare",
    )(place, received, table, keep.reshape(1, -1), layer.reshape(1, -1), *in_hbm(*weights))


def start_copies(sources, places, targets, sems):
    copies = []
    for source, (index, to, at, rows) in zip(sources, places):
        parts = 3 if rows % 48 == 0 or rows % 3 == 0 and len(source.shape) > 2 else 1
        for n in range(parts):
            size = rows // parts
            copies.append(
                pltpu.make_async_copy(
                    source.at[pl.ds(at + n * size, size)],
                    targets[index].at[pl.ds(to + n * size, size)],
                    sems.at[len(copies)],
                )
            )
            copies[-1].start()
    return copies


def attention_rows(current, norm_ref, mask_ref, weights, out_ref):
    normed = [normalise(rows, norm_ref[0], norm_ref[1]).astype(BF16) for rows in current]
    normed = normed[0] if len(normed) == 1 else jnp.concatenate(normed, axis=0)
    qkv_me, qkv_other = weights
    share = qkv_me.shape[1]
    heads = share // HD
    block = mask_ref.shape[0]
    count = normed.shape[0] // block
    is_open = mask_ref[...] > 0.5
    lane = lax.broadcasted_iota(jnp.int32, (1, share), 1)
    head_lanes = [
        ((lane >= HD * h) & (lane < HD * (h + 1))).astype(jnp.int32).astype(F32).astype(BF16)
        for h in range(heads)
    ]
    scale = math.log2(math.e) / math.sqrt(HD)
    projected = []
    for side, qkv in enumerate((qkv_me, qkv_other)):
        projected.append(
            [
                lax.dot_general(
                    normed, qkv[t], (((1,), (1,)), ((), ())), preferred_element_type=F32
                ).astype(BF16)
                for t in range(3)
            ]
        )
    units = [(side, slice(b * block, (b + 1) * block)) for side in range(2) for b in range(count)]
    scores = []
    for side, at in units:
        query, key = projected[side][0][at], projected[side][1][at]
        keys = jnp.concatenate([key * lanes for lanes in head_lanes], axis=0)
        raw = lax.dot_general(query, keys, (((1,), (1,)), ((), ())), preferred_element_type=F32)
        scores += [
            jnp.where(is_open, raw[:, h * block : (h + 1) * block], -1e30) for h in range(heads)
        ]
    tops = [jnp.max(s, axis=-1, keepdims=True) for s in scores]
    weights_of = [jnp.exp2((s - t) * scale) for s, t in zip(scores, tops)]
    sums = [jnp.sum(w, axis=-1, keepdims=True) for w in weights_of]
    shares = [(w / total).astype(BF16) for w, total in zip(weights_of, sums)]
    attended = []
    for n, (side, at) in enumerate(units):
        value = projected[side][2][at]
        values = jnp.concatenate([value * lanes for lanes in head_lanes], axis=0)
        row = jnp.concatenate(shares[n * heads : (n + 1) * heads], axis=1)
        attended.append(jnp.dot(row, values, preferred_element_type=F32).astype(BF16))
    sides = [attended[side * count : (side + 1) * count] for side in range(2)]
    sides = [x[0] if count == 1 else jnp.concatenate(x, axis=0) for x in sides]
    full, _ = tiles_of(share)
    tiles = [x[:, t * LANES : (t + 1) * LANES] for x in sides for t in range(full)]
    pack_half(out_ref, tiles, jnp.concatenate([x[:, full * LANES :] for x in sides], axis=1))


def shifted_in(rows, fresh_row):
    frames = rows.shape[0]
    first = lax.broadcasted_iota(jnp.int32, (frames, 1), 0) == 0
    return jnp.where(first, fresh_row, pltpu.roll(rows, 1, 0))


def first_attention_kernel(
    count, mine_ref, other_ref, flag_ref, norm_ref, mask_ref,
    qkv_me, qkv_other, cur_ref, part_ref, fresh_ref,
):
    groups, cores = mine_ref.shape[:2]
    frames = norm_ref.shape[1]
    here = frames // groups
    share = qkv_me.shape[1]
    first_half = flag_ref[0:1, :] > 0.5
    blocks = []
    for g in range(groups):
        left, right = [], []
        for c in range(cores):
            mine, other = mine_ref[g, c].astype(F32), other_ref[g, c].astype(F32)
            left.append(jnp.where(first_half, mine, other))
            right.append(jnp.where(first_half, other, mine))
        if g < count:
            cuts = [fresh_piece(block, count, here, share) for block in left + right]
            fresh_ref[g : g + 1, :] = jnp.concatenate(cuts, axis=1)
        blocks.append([chunk_rows(block, count, here, share) for block in left + right])
    current = []
    for p in range(count):
        rows = [jnp.concatenate([part[p] for part in parts], axis=1) for parts in blocks]
        rows = pltpu.roll(jnp.concatenate(rows, axis=0), 1, 0)
        cur_ref[p * frames : (p + 1) * frames, :] = rows.astype(BF16)
        current.append(rows)
    attention_rows(current, norm_ref, mask_ref, (qkv_me, qkv_other), part_ref)


def next_attention_kernel(
    count, old_ref, after_ref, mine_ref, other_ref, fresh_ref, norm_ref, gate_ref, pair_ref,
    mask_ref, qkv_me, qkv_other, cur_ref, part_ref,
):
    frames = norm_ref.shape[1]
    keep, layer = pair_ref[:, 0:1], pair_ref[:, 1:2]
    current = []
    for p in range(count):
        at = slice(p * frames, (p + 1) * frames)
        total = mine_ref[at, :].astype(F32) + other_ref[at, :].astype(F32)
        rows = keep * old_ref[at, :].astype(F32) + layer * (
            after_ref[at, :].astype(F32) + gate_ref[0] * total
        )
        rows = shifted_in(rows, fresh_ref[p : p + 1, :]).astype(BF16)
        cur_ref[at, :] = rows
        current.append(rows.astype(F32))
    attention_rows(current, norm_ref, mask_ref, (qkv_me, qkv_other), part_ref)


def attention_call(kernel, arrays, rows, features, fresh_count=0):
    outs = (
        jax.ShapeDtypeStruct((rows, features), BF16),
        jax.ShapeDtypeStruct((rows * features // 2 // LANES, LANES), BF16),
    )
    if fresh_count:
        outs += (jax.ShapeDtypeStruct((fresh_count, features), F32),)
    return pl.pallas_call(
        kernel,
        out_shape=outs,
        in_specs=[VMEM_SPEC] * len(arrays),
        out_specs=(VMEM_SPEC,) * len(outs),
        compiler_params=params(*arrays, *outs),
        cost_estimate=takes(2.8),
        name="attention",
    )(*arrays)


def pack_half(ref, tiles, tail):
    rows = tail.shape[0]
    for n, tile in enumerate(tiles):
        ref[n * rows : (n + 1) * rows, :] = tile
    ref[len(tiles) * rows :, :] = jnp.concatenate([tail[: rows // 2], tail[rows // 2 :]], axis=1)


def pick_half(first_half, value):
    middle = value.shape[1] // 2 // LANES
    tiles = []
    for t in range(middle):
        left, right = (value[:, n * LANES : (n + 1) * LANES] for n in (t, t + middle + 1))
        tiles.append(jnp.where(first_half, left, right))
    split = value[:, middle * LANES : (middle + 1) * LANES]
    cut = LANES // 2
    return tiles, jnp.where(first_half[:, :cut], split[:, :cut], split[:, cut:])


def unpack_half(ref, rows):
    count = ref.shape[0] // rows
    tail = ref[count * rows :, :]
    tail = jnp.concatenate([tail[:, : LANES // 2], tail[:, LANES // 2 :]], axis=0)
    tiles = [ref[n * rows : (n + 1) * rows, :] for n in range(count)]
    return jnp.concatenate(tiles, axis=1), tail


def gelu(x):
    inner = math.sqrt(2.0 / math.pi) * (x + 0.044715 * (x * x * x))
    return x * (0.5 * (1.0 + jnp.tanh(inner)))


def pieces_of(width, size):
    return [(s, min(size, width - s)) for s in range(0, width, size)]


def feed_kernel(
    halves, flag_ref, cur_ref, mine_ref, other_ref, mod_ref,
    out_all, fc1_me, fc1_other, fc2_me, fc2_other, *rest,
):
    outs, hidden_ref = (rest[:-2], rest[-2]) if halves else (rest[:-1], rest[-1])
    after_ref = outs[0]
    frames = mod_ref.shape[1]
    tokens = cur_ref.shape[0] // frames
    normed = []
    rows, half = cur_ref.shape[0], out_all.shape[0] // 2
    attention_total = None
    for n, ref in enumerate((mine_ref, other_ref)):
        main, tail = unpack_half(ref, rows)
        middle = n * half + main.shape[1]
        part = jnp.dot(main, out_all[n * half : middle], preferred_element_type=F32)
        part += jnp.dot(tail, out_all[middle : (n + 1) * half], preferred_element_type=F32)
        attention_total = part if n == 0 else attention_total + part
    for p in range(tokens):
        at = slice(p * frames, (p + 1) * frames)
        after = (cur_ref[at, :].astype(F32) + mod_ref[0] * attention_total[at]).astype(BF16)
        after_ref[at, :] = after
        normed.append(normalise(after.astype(F32), mod_ref[1], mod_ref[2]).astype(BF16))
    normed = normed[0] if tokens == 1 else jnp.concatenate(normed, axis=0)
    units, features = fc2_me.shape
    for side, w1 in enumerate((fc1_me, fc1_other)):
        for start, size in pieces_of(units, 256):
            hidden = gelu(
                jnp.dot(normed, w1[:, start : start + size], preferred_element_type=F32)
            )
            hidden_ref[:, side * units + start : side * units + start + size] = hidden.astype(BF16)

    def product(at):
        return jnp.dot(
            hidden_ref[:, :units], fc2_me[:, at], preferred_element_type=F32
        ) + jnp.dot(hidden_ref[:, units:], fc2_other[:, at], preferred_element_type=F32)

    target = rest[-1] if halves else outs[1]
    for start, size in pieces_of(features, 256):
        at = slice(start, start + size)
        target[:, at] = product(at).astype(BF16)
    if not halves:
        return
    first_half = flag_ref[0:1, :] > 0.5
    pack_half(outs[1], *pick_half(first_half, target[...]))
    pack_half(outs[2], *pick_half(jnp.logical_not(first_half), target[...]))


def feed_call(flag, cur, mine, other, mod, weights, halves):
    rows, features = cur.shape
    shape = jax.ShapeDtypeStruct((rows, features), BF16)
    packed = jax.ShapeDtypeStruct((rows * features // 2 // LANES, LANES), BF16)
    outs = (shape, packed, packed) if halves else (shape, shape)
    return pl.pallas_call(
        functools.partial(feed_kernel, halves),
        out_shape=outs,
        in_specs=[VMEM_SPEC] * 10,
        out_specs=(VMEM_SPEC,) * len(outs),
        scratch_shapes=[pltpu.VMEM((rows, 2 * weights[1].shape[1]), BF16)]
        + ([pltpu.VMEM((rows, features), BF16)] if halves else []),
        compiler_params=params(cur, mine, other, mod, *weights, *outs),
        cost_estimate=takes(2.8),
        name="feed",
    )(flag, cur, mine, other, mod, *weights)


def finish_kernel(chunks, flag_ref, gate_ref, pair_ref, *refs):
    out_ref = refs[-1]
    groups, cores = out_ref.shape[:2]
    _, frames, features = gate_ref.shape
    here = frames // groups
    half = features // 2
    share = half // cores
    full, rest = tiles_of(share)
    first_half = flag_ref[0:1, :] > 0.5
    keep, layer = pair_ref[:, 0:1], pair_ref[:, 1:2]
    gates = pick_half(first_half, gate_ref[0])
    gates = gates[0] + [gates[1]]
    results = []
    for n in range(chunks):
        old_ref, after_ref, mine_ref, other_ref = refs[4 * n : 4 * n + 4]
        rows = old_ref.shape[0]
        (mine, mine_tail), (theirs, their_tail) = (
            unpack_half(ref, rows) for ref in (mine_ref, other_ref)
        )
        main = mine.astype(F32) + theirs.astype(F32)
        main_tail = mine_tail.astype(F32) + their_tail.astype(F32)
        for p in range(rows // frames):
            at = slice(p * frames, (p + 1) * frames)
            old, after = (
                pick_half(first_half, ref[at, :].astype(F32)) for ref in (old_ref, after_ref)
            )
            old, after = old[0] + [old[1]], after[0] + [after[1]]
            total = [main[at, t * LANES : (t + 1) * LANES] for t in range(len(old) - 1)]
            total.append(main_tail[at])
            done = [
                keep * o + layer * (a + g * t) for o, a, g, t in zip(old, after, gates, total)
            ]
            left, right = jnp.concatenate(done, axis=1), jnp.concatenate(done[-1:] + done[:-1], axis=1)
            results.append(jnp.where(first_half[:, 0:1], left, right))
    unused = LANES - len(results) * rest
    for c in range(cores):
        shares = [r[:, c * share : (c + 1) * share] for r in results]
        for g in range(groups):
            rows = [s[g * here : (g + 1) * here] for s in shares]
            pieces = [r[:, t * LANES : (t + 1) * LANES] for t in range(full) for r in rows]
            tails = [r[:, full * LANES :] for r in rows]
            if unused:
                tails.append(jnp.zeros((here, unused), F32))
            pieces.append(jnp.concatenate(tails, axis=1))
            out_ref[g, c] = jnp.concatenate(pieces, axis=0).astype(BF16)


def finish(flag, gate, pair, parts, groups):
    _, frames, features = gate.shape
    tokens = sum(part[0].shape[0] for part in parts) // frames
    full, _ = tiles_of(features // 4)
    arrays = [array for part in parts for array in part]
    out = jax.ShapeDtypeStruct((groups, 2, (full * tokens + 1) * (frames // groups), LANES), BF16)
    return pl.pallas_call(
        functools.partial(finish_kernel, len(parts)),
        out_shape=out,
        in_specs=[VMEM_SPEC] * (3 + len(arrays)),
        out_specs=VMEM_SPEC,
        compiler_params=params(gate, pair, out, *arrays),
        cost_estimate=takes(0.8),
        name="finish",
    )(flag, gate, pair, *arrays)


def unpack_kernel(rows_ref, out_ref, wide_ref):
    here, tokens, share = out_ref.shape
    sources = rows_ref.shape[0]
    size = tokens // sources
    full, rest = tiles_of(share)
    for d in range(sources):
        block = rows_ref[d].astype(F32)
        first = d * size * here
        for t in range(full):
            wide_ref[t, first : first + size * here, :] = block[t * size * here : (t + 1) * size * here]
        tail = block[full * size * here :]
        for p in range(size):
            wide_ref[full, first + p * here : first + (p + 1) * here, :rest] = tail[
                :, p * rest : (p + 1) * rest
            ]
    for i in range(here):
        pieces = [wide_ref[t, pl.ds(i, tokens, stride=here), :] for t in range(full + 1)]
        out_ref[i] = jnp.concatenate(pieces, axis=1)[:, :share].astype(BF16)


def unpack(rows, here, tokens, share):
    full, _ = tiles_of(share)
    out = jax.ShapeDtypeStruct((here, tokens, share), BF16)
    scratch = jax.ShapeDtypeStruct((full + 1, tokens * here, LANES), F32)
    return pl.pallas_call(
        unpack_kernel,
        out_shape=out,
        in_specs=[VMEM_SPEC],
        out_specs=VMEM_SPEC,
        scratch_shapes=[pltpu.VMEM(scratch.shape, F32)],
        compiler_params=params(rows, out, scratch),
        cost_estimate=takes(0.9),
        name="unpack",
    )(rows)


SWAP = [(0, 1), (1, 0)]


def on_device(
    latents, fresh, noise_level, window_mask, mod_table, keep_coef, layer_coef,
    w_qkv, w_out, w_fc1, w_fc2,
):
    here, tokens_all, share = latents.shape
    features = mod_table.shape[2]
    groups = lax.axis_size("frame")
    frames = groups * here
    frame_index = lax.axis_index("frame")
    y_index, core_index = lax.axis_index("y"), lax.axis_index("core")
    place = (2 * y_index + core_index).astype(jnp.int32).reshape(1)
    group_tokens = tokens_all // groups
    split = group_tokens % 2 == 0
    tokens = group_tokens // 2 if split else group_tokens
    block = max(frames, LANES)
    chunk_count = 2 if tokens % 2 == 0 and tokens * frames // 2 % block == 0 else 1
    size = tokens // chunk_count
    rows = size * frames

    swap_core = functools.partial(lax.ppermute, axis_name="core", perm=SWAP)
    swap_y = functools.partial(lax.ppermute, axis_name="y", perm=SWAP)
    w_qkv = jnp.swapaxes(w_qkv, 1, 2)
    qkv_other = swap_core(w_qkv)
    out_far = swap_y(w_out)
    out_core, out_corner, fc2_other = swap_core(w_out), swap_core(out_far), swap_core(w_fc2)
    payload = make_payload(
        frame_index.astype(jnp.int32).reshape(1), noise_level, window_mask, latents, fresh,
        frames, tokens_all // tokens, chunk_count,
    )
    if split:
        received = lax.all_to_all(payload, ("frame", "core"), 0, 0, tiled=True)
        received = received.reshape((groups, 2) + received.shape[1:])
    else:
        received = lax.all_to_all(payload, "frame", 0, 0, tiled=True)
        partner = swap_core(received)
        first = core_index == 0
        received = jnp.stack(
            [jnp.where(first, received, partner), jnp.where(first, partner, received)], axis=1
        )
    received, qkv_other, out_core, out_far, fc2_other = lax.optimization_barrier(
        (received, qkv_other, out_core, out_far, fc2_other)
    )
    full, rest = tiles_of(share)
    arrived = [received[:, :, n] for n in range(chunk_count)]
    arrived_other = [swap_y(part) for part in arrived]
    weights = [w_qkv, qkv_other]
    places = [(n, 0, 0, w_qkv.shape[0]) for n in range(2)]
    for n in range(2):
        first, second = ((w_out, out_core), (out_far, out_corner))[n]
        weights += [first, second, first, second]
        to = 2 * n * share
        places += [(2, to, 0, full * LANES), (2, to + full * LANES, 0, full * LANES)]
        to += 2 * full * LANES
        places += [(2, to, full * LANES, rest), (2, to + rest, full * LANES, rest)]
    weights.append(fc2_other)
    places.append((3, 0, 0, w_fc2.shape[0]))
    held = (w_qkv.shape, w_qkv.shape, (4 * share, features), w_fc2.shape)
    norm_mod, feed_mod, gate_mod, pair, mask, flag, w_qkv, qkv_other, out_all, fc2_other = prepare(
        place, arrived[0], jnp.swapaxes(mod_table, 0, 1), keep_coef, layer_coef,
        weights, places, held, here, size * rest, block,
    )
    attention_weights = (w_qkv, qkv_other)

    state = []
    for n in range(chunk_count):
        results = attention_call(
            functools.partial(first_attention_kernel, size),
            (arrived[n], arrived_other[n], flag, norm_mod, mask) + attention_weights,
            rows, features, size,
        )
        current, part, later = results
        state.append((current, part, swap_y(part), later))
    feed_weights = (out_all, w_fc1, swap_core(w_fc1), w_fc2, fc2_other)
    fed = []
    for current, part, part_other, later in state:
        after, feed = feed_call(flag, current, part, part_other, feed_mod, feed_weights, False)
        fed.append((current, after, feed, swap_y(feed), later))
    state = []
    for arrays in fed:
        current, part = attention_call(
            functools.partial(next_attention_kernel, size),
            arrays + (norm_mod, gate_mod, pair, mask) + attention_weights,
            rows, features,
        )
        state.append((current, part, swap_y(part)))
    parts = []
    for current, part, part_other in state:
        after, feed_here, feed_there = feed_call(
            flag, current, part, part_other, feed_mod, feed_weights, True
        )
        parts.append((current, after, feed_here, swap_y(feed_there)))
    result = finish(flag, gate_mod, pair, parts, groups)
    if split:
        result = result.reshape((groups * 2,) + result.shape[2:])
        result = lax.all_to_all(result, ("frame", "core"), 0, 0, tiled=True)
    else:
        result = jnp.where(core_index == 0, result[:, 0], result[:, 1])
        result = lax.all_to_all(result, "frame", 0, 0, tiled=True)
    return unpack(result, here, tokens_all, share)


def solution(mesh):
    groups, heads = mesh.shape["frame"], mesh.shape["head"]
    inner = Mesh(mesh.devices.reshape(groups, heads // 2, 2), ("frame", "y", "core"))
    head = ("y", "core")
    in_specs = (
        P("frame", None, head),
        P(None, None, head),
        P("frame"),
        P("frame", None),
        P(),
        P(),
        P(),
        P(None, None, head),
        P(head, None),
        P(None, head),
        P(head, None),
    )
    return jax.shard_map(
        on_device, mesh=inner, in_specs=in_specs, out_specs=P("frame", None, head), check_vma=False
    )
```

```python
import functools
import math

import jax
import jax.numpy as jnp
from jax import lax
from jax.experimental import pallas as pl
from jax.experimental.pallas import tpu as pltpu
from jax.sharding import Mesh, PartitionSpec as P

HD = 72
W = 8
OFFSETS = 2 * W + 1
EPSILON = 1e-06
F32 = jnp.float32
BF16 = jnp.bfloat16
LANES = 128
VMEM_SPEC = pl.BlockSpec(memory_space=pltpu.VMEM)
SMEM_SPEC = pl.BlockSpec(memory_space=pltpu.SMEM)
HBM_SPEC = pl.BlockSpec(memory_space=pltpu.HBM)


def in_hbm(*arrays):
    return [pltpu.with_memory_space_constraint(array, pltpu.HBM) for array in arrays]


def params(*arrays):
    held = sum(math.prod(a.shape) * jnp.dtype(a.dtype).itemsize for a in arrays)
    return pltpu.CompilerParams(vmem_limit_bytes=held + 8 * 1024 * 1024)


def takes(microseconds):
    return pl.CostEstimate(
        flops=0, bytes_accessed=int(microseconds * 3.3e6), transcendentals=0
    )


def tiles_of(share):
    return share // LANES, share % LANES


def normalise(values, shift_rows, scale_rows):
    center = values - jnp.mean(values, axis=-1, keepdims=True)
    spread = jnp.mean(center * center, axis=-1, keepdims=True)
    return center * lax.rsqrt(spread + EPSILON) * (1.0 + scale_rows) + shift_rows


def payload_kernel(
    frames, frame_far, level_far, window_far, x_far, fresh_far, out_ref,
    rows_ref, frame_ref, level_ref, window_ref, x_ref, fresh_ref, sems,
):
    fars = (x_far, window_far, level_far, frame_far, fresh_far)
    nears = (x_ref, window_ref, level_ref, frame_ref, fresh_ref)
    copies = [pltpu.make_async_copy(a, b, sems.at[n]) for n, (a, b) in enumerate(zip(fars, nears))]
    for copy in copies:
        copy.start()
    for copy in copies:
        copy.wait()
    here, _, share = x_ref.shape
    targets, chunks, _, _ = out_ref.shape
    full, rest = tiles_of(share)
    size = x_ref.shape[1] // (targets * chunks)
    row = lax.broadcasted_iota(jnp.int32, (here, 1), 0)
    level = jnp.zeros((here, 1), jnp.int32)
    for i in range(here):
        level = jnp.where(row == i, level_ref[i], level)
    offset = lax.broadcasted_iota(jnp.int32, (here, OFFSETS), 1)
    position = frame_ref[0] * here + row + offset - W
    allowed = (window_ref[...] == 1) & (position >= 0) & (position < frames)
    meta = jnp.concatenate([level.astype(F32), allowed.astype(jnp.int32).astype(F32)], axis=1)
    tokens = x_ref.shape[1]
    piece = share // here
    blank = LANES - size * rest - 1 - OFFSETS - piece
    later = fresh_ref[1].astype(F32)
    for j in range(here):
        cut = later[:, j * piece : (j + 1) * piece]
        cut = jnp.concatenate([cut, jnp.zeros((tokens, LANES - piece), F32)], axis=1)
        rows_ref[full + 1, pl.ds(j, tokens, stride=here), :] = cut
    sent = lax.rem(frame_ref[0], size)
    for i in range(here):
        value = x_ref[i].astype(F32)
        if i == here - 1:
            leaves = (frame_ref[0] + 1) * here == frames
            value = jnp.where(leaves, fresh_ref[0].astype(F32), value)
        for t in range(full):
            rows_ref[t, pl.ds(i, tokens, stride=here), :] = value[:, t * LANES : (t + 1) * LANES]
        rows_ref[full, pl.ds(i, tokens, stride=here), :] = jnp.concatenate(
            [value[:, full * LANES :], jnp.zeros((tokens, LANES - rest), F32)], axis=1
        )
    for d in range(targets):
        for n in range(chunks):
            first = (d * chunks + n) * size * here
            pieces = [rows_ref[t, first : first + size * here, :] for t in range(full)]
            tails = [
                rows_ref[full, first + p * here : first + (p + 1) * here, :][:, :rest]
                for p in range(size)
            ]
            cuts = [
                rows_ref[full + 1, first + p * here : first + (p + 1) * here, :][:, :piece]
                for p in range(size)
            ]
            cut = cuts[0]
            for p in range(1, size):
                cut = jnp.where(sent == p, cuts[p], cut)
            tails += [meta, cut]
            if blank:
                tails.append(jnp.zeros((here, blank), F32))
            pieces.append(jnp.concatenate(tails, axis=1))
            out_ref[d, n] = jnp.concatenate(pieces, axis=0).astype(BF16)


def make_payload(frame_index, noise_level, window_mask, x, fresh, frames, targets, chunks):
    here, tokens, share = x.shape
    full, rest = tiles_of(share)
    size = tokens // (targets * chunks)
    out = jax.ShapeDtypeStruct((targets, chunks, (full * size + 1) * here, LANES), BF16)
    scratch = jax.ShapeDtypeStruct((full + 2, tokens * here, LANES), F32)
    return pl.pallas_call(
        functools.partial(payload_kernel, frames),
        out_shape=out,
        in_specs=[HBM_SPEC] * 5,
        out_specs=VMEM_SPEC,
        scratch_shapes=[
            pltpu.VMEM(scratch.shape, F32),
            pltpu.SMEM(frame_index.shape, jnp.int32),
            pltpu.SMEM(noise_level.shape, jnp.int32),
            pltpu.VMEM(window_mask.shape, jnp.int32),
            pltpu.VMEM(x.shape, BF16),
            pltpu.VMEM(fresh.shape, BF16),
            pltpu.SemaphoreType.DMA((5,)),
        ],
        compiler_params=params(x, fresh, out, scratch),
        cost_estimate=takes(2),
        name="payload",
    )(*in_hbm(frame_index, noise_level, window_mask, x, fresh))


def fresh_piece(block, size, here, share):
    _, rest = tiles_of(share)
    piece = share // here
    first = size * rest + 1 + OFFSETS
    tail = block[-here:, first : first + piece]
    return jnp.concatenate([tail[j : j + 1] for j in range(here)], axis=1)


def chunk_rows(block, size, here, share):
    full, rest = tiles_of(share)
    tail = block[full * size * here :]
    result = []
    for p in range(size):
        pieces = [block[(t * size + p) * here : (t * size + p + 1) * here] for t in range(full)]
        result.append(jnp.concatenate(pieces + [tail[:, p * rest : (p + 1) * rest]], axis=1))
    return result


def prepare_kernel(
    here, lane_at, places, place_ref, received_ref, table_far, keep_ref, layer_ref, *refs
):
    sources, refs = refs[: len(places)], refs[len(places) :]
    norm_ref, feed_ref, gate_ref, pair_ref, mask_ref, flag_ref = refs[:6]
    held, (table_ref, table_sems, sems) = refs[6:-3], refs[-3:]
    table_copies = start_copies(
        (table_far,), [(0, 0, 0, table_far.shape[0])], (table_ref,), table_sems
    )
    copies = start_copies(sources, places, held, sems)
    flag_ref[...] = jnp.where(place_ref[0] < 2, jnp.ones_like(flag_ref), 0.0)
    groups = received_ref.shape[0]
    frames = groups * here
    levels = table_ref.shape[1]
    meta = [received_ref[g, 0].astype(F32)[-here:, lane_at:] for g in range(groups)]
    meta = jnp.concatenate(meta, axis=0)
    level = meta[:, 0:1]
    ids = lax.broadcasted_iota(jnp.int32, (frames, levels), 1).astype(F32)
    hot = level == ids
    hot_bf = hot.astype(BF16)
    for copy in table_copies:
        copy.wait()
    targets = [(norm_ref, 0), (norm_ref, 1), (feed_ref, 0), (feed_ref, 1), (feed_ref, 2), (gate_ref, 0)]
    for j, (target, at) in enumerate(targets):
        rows = table_ref[j]
        high = rows.astype(BF16)
        rest = rows - high.astype(F32)
        middle = rest.astype(BF16)
        low = (rest - middle.astype(F32)).astype(BF16)
        total = jnp.dot(hot_bf, high, preferred_element_type=F32)
        total += jnp.dot(hot_bf, middle, preferred_element_type=F32)
        total += jnp.dot(hot_bf, low, preferred_element_type=F32)
        target[at] = total
    keep = jnp.sum(jnp.where(hot, keep_ref[...], 0.0), axis=1, keepdims=True)
    layer = jnp.sum(jnp.where(hot, layer_ref[...], 0.0), axis=1, keepdims=True)
    lane = lax.broadcasted_iota(jnp.int32, (frames, LANES), 1)
    pair_ref[...] = jnp.where(lane == 0, keep, layer)

    block = mask_ref.shape[0]
    row = lax.broadcasted_iota(jnp.int32, (frames, block), 0)
    column = lax.broadcasted_iota(jnp.int32, (frames, block), 1)
    for t in range(block // frames):
        distance = column - t * frames - row
        inside = (column >= t * frames) & (column < (t + 1) * frames)
        is_open = jnp.zeros((frames, block), F32)
        for o in range(OFFSETS):
            is_open = jnp.where(distance == o - W, meta[:, 1 + o : 2 + o], is_open)
        is_open = jnp.where(inside, is_open, 0.0)
        mask_ref[t * frames : (t + 1) * frames, :] = jnp.where(is_open > 0.5, 0.0, -1e30)
    for copy in copies:
        copy.wait()


def prepare(place, received, table, keep, layer, weights, places, held, here, lane_at, block):
    frames = received.shape[0] * here
    features = table.shape[2]
    outs = (
        jax.ShapeDtypeStruct((2, frames, features), F32),
        jax.ShapeDtypeStruct((3, frames, features), F32),
        jax.ShapeDtypeStruct((1, frames, features), F32),
        jax.ShapeDtypeStruct((frames, LANES), F32),
        jax.ShapeDtypeStruct((block, block), F32),
        jax.ShapeDtypeStruct((8, LANES), F32),
    ) + tuple(jax.ShapeDtypeStruct(shape, BF16) for shape in held)
    (table,) = in_hbm(table)
    return pl.pallas_call(
        functools.partial(prepare_kernel, here, lane_at, tuple(places)),
        out_shape=outs,
        in_specs=[SMEM_SPEC, VMEM_SPEC, HBM_SPEC, VMEM_SPEC, VMEM_SPEC]
        + [HBM_SPEC] * len(weights),
        out_specs=(VMEM_SPEC,) * len(outs),
        scratch_shapes=[
            pltpu.VMEM(table.shape, F32),
            pltpu.SemaphoreType.DMA((3,)),
            pltpu.SemaphoreType.DMA((3 * len(weights),)),
        ],
        compiler_params=params(received, table, *outs),
        cost_estimate=takes(5),
        name="prepare",
    )(place, received, table, keep.reshape(1, -1), layer.reshape(1, -1), *in_hbm(*weights))


def start_copies(sources, places, targets, sems):
    copies = []
    for source, (index, to, at, rows) in zip(sources, places):
        parts = 3 if rows % 48 == 0 or rows % 3 == 0 and len(source.shape) > 2 else 1
        for n in range(parts):
            size = rows // parts
            copies.append(
                pltpu.make_async_copy(
                    source.at[pl.ds(at + n * size, size)],
                    targets[index].at[pl.ds(to + n * size, size)],
                    sems.at[len(copies)],
                )
            )
            copies[-1].start()
    return copies


def attention_rows(current, norm_ref, mask_ref, weights, out_ref):
    normed = [normalise(rows, norm_ref[0], norm_ref[1]).astype(BF16) for rows in current]
    normed = normed[0] if len(normed) == 1 else jnp.concatenate(normed, axis=0)
    qkv_me, qkv_other = weights
    share = qkv_me.shape[1]
    heads = share // HD
    block = mask_ref.shape[0]
    count = normed.shape[0] // block
    bias = mask_ref[...]
    lane = lax.broadcasted_iota(jnp.int32, (1, share), 1)
    head_lanes = [
        ((lane >= HD * h) & (lane < HD * (h + 1))).astype(jnp.int32).astype(F32).astype(BF16)
        for h in range(heads)
    ]
    scale = math.log2(math.e) / math.sqrt(HD)
    projected = []
    for side, qkv in enumerate((qkv_me, qkv_other)):
        projected.append(
            [
                lax.dot_general(
                    normed, qkv[t], (((1,), (1,)), ((), ())), preferred_element_type=F32
                ).astype(BF16)
                for t in range(3)
            ]
        )
    units = [(side, slice(b * block, (b + 1) * block)) for side in range(2) for b in range(count)]
    scores = []
    for side, at in units:
        query, key = projected[side][0][at], projected[side][1][at]
        keys = jnp.concatenate([key * lanes for lanes in head_lanes], axis=0)
        raw = lax.dot_general(query, keys, (((1,), (1,)), ((), ())), preferred_element_type=F32)
        scores += [
            raw[:, h * block : (h + 1) * block] + bias for h in range(heads)
        ]
    tops = [jnp.max(s, axis=-1, keepdims=True) for s in scores]
    weights_of = [jnp.exp2((s - t) * scale) for s, t in zip(scores, tops)]
    parts = [1.0 / jnp.sum(w, axis=-1, keepdims=True) for w in weights_of]
    shares = [(w * part).astype(BF16) for w, part in zip(weights_of, parts)]
    attended = []
    for n, (side, at) in enumerate(units):
        value = projected[side][2][at]
        values = jnp.concatenate([value * lanes for lanes in head_lanes], axis=0)
        row = jnp.concatenate(shares[n * heads : (n + 1) * heads], axis=1)
        attended.append(jnp.dot(row, values, preferred_element_type=F32).astype(BF16))
    sides = [attended[side * count : (side + 1) * count] for side in range(2)]
    sides = [x[0] if count == 1 else jnp.concatenate(x, axis=0) for x in sides]
    full, _ = tiles_of(share)
    tiles = [x[:, t * LANES : (t + 1) * LANES] for x in sides for t in range(full)]
    pack_half(out_ref, tiles, jnp.concatenate([x[:, full * LANES :] for x in sides], axis=1))


def shifted_in(rows, fresh_row):
    frames = rows.shape[0]
    first = lax.broadcasted_iota(jnp.int32, (frames, 1), 0) == 0
    return jnp.where(first, fresh_row, pltpu.roll(rows, 1, 0))


def first_attention_kernel(
    count, mine_ref, other_ref, flag_ref, norm_ref, mask_ref,
    qkv_me, qkv_other, cur_ref, part_ref, fresh_ref,
):
    groups, cores = mine_ref.shape[:2]
    frames = norm_ref.shape[1]
    here = frames // groups
    share = qkv_me.shape[1]
    first_half = flag_ref[0:1, :] > 0.5
    blocks = []
    for g in range(groups):
        left, right = [], []
        for c in range(cores):
            mine, other = mine_ref[g, c].astype(F32), other_ref[g, c].astype(F32)
            left.append(jnp.where(first_half, mine, other))
            right.append(jnp.where(first_half, other, mine))
        if g < count:
            cuts = [fresh_piece(block, count, here, share) for block in left + right]
            fresh_ref[g : g + 1, :] = jnp.concatenate(cuts, axis=1)
        blocks.append([chunk_rows(block, count, here, share) for block in left + right])
    current = []
    for p in range(count):
        rows = [jnp.concatenate([part[p] for part in parts], axis=1) for parts in blocks]
        rows = pltpu.roll(jnp.concatenate(rows, axis=0), 1, 0)
        cur_ref[p * frames : (p + 1) * frames, :] = rows.astype(BF16)
        current.append(rows)
    attention_rows(current, norm_ref, mask_ref, (qkv_me, qkv_other), part_ref)


def next_attention_kernel(
    count, old_ref, after_ref, mine_ref, other_ref, fresh_ref, norm_ref, gate_ref, pair_ref,
    mask_ref, qkv_me, qkv_other, cur_ref, part_ref,
):
    frames = norm_ref.shape[1]
    keep, layer = pair_ref[:, 0:1], pair_ref[:, 1:2]
    current = []
    for p in range(count):
        at = slice(p * frames, (p + 1) * frames)
        total = mine_ref[at, :].astype(F32) + other_ref[at, :].astype(F32)
        rows = keep * old_ref[at, :].astype(F32) + layer * (
            after_ref[at, :].astype(F32) + gate_ref[0] * total
        )
        rows = shifted_in(rows, fresh_ref[p : p + 1, :]).astype(BF16)
        cur_ref[at, :] = rows
        current.append(rows.astype(F32))
    attention_rows(current, norm_ref, mask_ref, (qkv_me, qkv_other), part_ref)


def attention_call(kernel, arrays, rows, features, fresh_count=0):
    outs = (
        jax.ShapeDtypeStruct((rows, features), BF16),
        jax.ShapeDtypeStruct((rows * features // 2 // LANES, LANES), BF16),
    )
    if fresh_count:
        outs += (jax.ShapeDtypeStruct((fresh_count, features), F32),)
    return pl.pallas_call(
        kernel,
        out_shape=outs,
        in_specs=[VMEM_SPEC] * len(arrays),
        out_specs=(VMEM_SPEC,) * len(outs),
        compiler_params=params(*arrays, *outs),
        cost_estimate=takes(2.8),
        name="attention",
    )(*arrays)


def pack_half(ref, tiles, tail):
    rows = tail.shape[0]
    for n, tile in enumerate(tiles):
        ref[n * rows : (n + 1) * rows, :] = tile
    ref[len(tiles) * rows :, :] = jnp.concatenate([tail[: rows // 2], tail[rows // 2 :]], axis=1)


def pick_half(first_half, value):
    middle = value.shape[1] // 2 // LANES
    tiles = []
    for t in range(middle):
        left, right = (value[:, n * LANES : (n + 1) * LANES] for n in (t, t + middle + 1))
        tiles.append(jnp.where(first_half, left, right))
    split = value[:, middle * LANES : (middle + 1) * LANES]
    cut = LANES // 2
    return tiles, jnp.where(first_half[:, :cut], split[:, :cut], split[:, cut:])


def unpack_half(ref, rows):
    count = ref.shape[0] // rows
    tail = ref[count * rows :, :]
    tail = jnp.concatenate([tail[:, : LANES // 2], tail[:, LANES // 2 :]], axis=0)
    tiles = [ref[n * rows : (n + 1) * rows, :] for n in range(count)]
    return jnp.concatenate(tiles, axis=1), tail


def gelu(x):
    scale = math.sqrt(2.0 / math.pi)
    half = 0.5 * x
    return half + half * jnp.tanh(x * (scale + (0.044715 * scale) * (x * x)))


def pieces_of(width, size):
    return [(s, min(size, width - s)) for s in range(0, width, size)]


def feed_kernel(
    halves, flag_ref, cur_ref, mine_ref, other_ref, mod_ref,
    out_all, fc1_me, fc1_other, fc2_me, fc2_other, *rest,
):
    outs, hidden_ref = (rest[:-2], rest[-2]) if halves else (rest[:-1], rest[-1])
    after_ref = outs[0]
    frames = mod_ref.shape[1]
    tokens = cur_ref.shape[0] // frames
    normed = []
    rows, half = cur_ref.shape[0], out_all.shape[0] // 2
    attention_total = None
    for n, ref in enumerate((mine_ref, other_ref)):
        main, tail = unpack_half(ref, rows)
        middle = n * half + main.shape[1]
        part = jnp.dot(main, out_all[n * half : middle], preferred_element_type=F32)
        part += jnp.dot(tail, out_all[middle : (n + 1) * half], preferred_element_type=F32)
        attention_total = part if n == 0 else attention_total + part
    for p in range(tokens):
        at = slice(p * frames, (p + 1) * frames)
        after = (cur_ref[at, :].astype(F32) + mod_ref[0] * attention_total[at]).astype(BF16)
        after_ref[at, :] = after
        normed.append(normalise(after.astype(F32), mod_ref[1], mod_ref[2]).astype(BF16))
    normed = normed[0] if tokens == 1 else jnp.concatenate(normed, axis=0)
    units, features = fc2_me.shape
    for side, w1 in enumerate((fc1_me, fc1_other)):
        for start, size in pieces_of(units, 256):
            hidden = gelu(
                jnp.dot(normed, w1[:, start : start + size], preferred_element_type=F32)
            )
            hidden_ref[:, side * units + start : side * units + start + size] = hidden.astype(BF16)

    def product(at):
        return jnp.dot(
            hidden_ref[:, :units], fc2_me[:, at], preferred_element_type=F32
        ) + jnp.dot(hidden_ref[:, units:], fc2_other[:, at], preferred_element_type=F32)

    target = rest[-1] if halves else outs[1]
    for start, size in pieces_of(features, 256):
        at = slice(start, start + size)
        target[:, at] = product(at).astype(BF16)
    if not halves:
        return
    first_half = flag_ref[0:1, :] > 0.5
    pack_half(outs[1], *pick_half(first_half, target[...]))
    pack_half(outs[2], *pick_half(jnp.logical_not(first_half), target[...]))


def feed_call(flag, cur, mine, other, mod, weights, halves):
    rows, features = cur.shape
    shape = jax.ShapeDtypeStruct((rows, features), BF16)
    packed = jax.ShapeDtypeStruct((rows * features // 2 // LANES, LANES), BF16)
    outs = (shape, packed, packed) if halves else (shape, shape)
    return pl.pallas_call(
        functools.partial(feed_kernel, halves),
        out_shape=outs,
        in_specs=[VMEM_SPEC] * 10,
        out_specs=(VMEM_SPEC,) * len(outs),
        scratch_shapes=[pltpu.VMEM((rows, 2 * weights[1].shape[1]), BF16)]
        + ([pltpu.VMEM((rows, features), BF16)] if halves else []),
        compiler_params=params(cur, mine, other, mod, *weights, *outs),
        cost_estimate=takes(2.8),
        name="feed",
    )(flag, cur, mine, other, mod, *weights)


def finish_kernel(chunks, flag_ref, gate_ref, pair_ref, *refs):
    out_ref = refs[-1]
    groups, cores = out_ref.shape[:2]
    _, frames, features = gate_ref.shape
    here = frames // groups
    half = features // 2
    share = half // cores
    full, rest = tiles_of(share)
    first_half = flag_ref[0:1, :] > 0.5
    keep, layer = pair_ref[:, 0:1], pair_ref[:, 1:2]
    gates = pick_half(first_half, gate_ref[0])
    gates = gates[0] + [gates[1]]
    results = []
    for n in range(chunks):
        old_ref, after_ref, mine_ref, other_ref = refs[4 * n : 4 * n + 4]
        rows = old_ref.shape[0]
        (mine, mine_tail), (theirs, their_tail) = (
            unpack_half(ref, rows) for ref in (mine_ref, other_ref)
        )
        main = mine.astype(F32) + theirs.astype(F32)
        main_tail = mine_tail.astype(F32) + their_tail.astype(F32)
        for p in range(rows // frames):
            at = slice(p * frames, (p + 1) * frames)
            old, after = (
                pick_half(first_half, ref[at, :].astype(F32)) for ref in (old_ref, after_ref)
            )
            old, after = old[0] + [old[1]], after[0] + [after[1]]
            total = [main[at, t * LANES : (t + 1) * LANES] for t in range(len(old) - 1)]
            total.append(main_tail[at])
            done = [
                keep * o + layer * (a + g * t) for o, a, g, t in zip(old, after, gates, total)
            ]
            left, right = jnp.concatenate(done, axis=1), jnp.concatenate(done[-1:] + done[:-1], axis=1)
            results.append(jnp.where(first_half[:, 0:1], left, right))
    unused = LANES - len(results) * rest
    for c in range(cores):
        shares = [r[:, c * share : (c + 1) * share] for r in results]
        for g in range(groups):
            rows = [s[g * here : (g + 1) * here] for s in shares]
            pieces = [r[:, t * LANES : (t + 1) * LANES] for t in range(full) for r in rows]
            tails = [r[:, full * LANES :] for r in rows]
            if unused:
                tails.append(jnp.zeros((here, unused), F32))
            pieces.append(jnp.concatenate(tails, axis=1))
            out_ref[g, c] = jnp.concatenate(pieces, axis=0).astype(BF16)


def finish(flag, gate, pair, parts, groups):
    _, frames, features = gate.shape
    tokens = sum(part[0].shape[0] for part in parts) // frames
    full, _ = tiles_of(features // 4)
    arrays = [array for part in parts for array in part]
    out = jax.ShapeDtypeStruct((groups, 2, (full * tokens + 1) * (frames // groups), LANES), BF16)
    return pl.pallas_call(
        functools.partial(finish_kernel, len(parts)),
        out_shape=out,
        in_specs=[VMEM_SPEC] * (3 + len(arrays)),
        out_specs=VMEM_SPEC,
        compiler_params=params(gate, pair, out, *arrays),
        cost_estimate=takes(0.8),
        name="finish",
    )(flag, gate, pair, *arrays)


def unpack_kernel(rows_ref, out_ref, wide_ref):
    here, tokens, share = out_ref.shape
    sources = rows_ref.shape[0]
    size = tokens // sources
    full, rest = tiles_of(share)
    for d in range(sources):
        block = rows_ref[d].astype(F32)
        first = d * size * here
        for t in range(full):
            wide_ref[t, first : first + size * here, :] = block[t * size * here : (t + 1) * size * here]
        tail = block[full * size * here :]
        for p in range(size):
            wide_ref[full, first + p * here : first + (p + 1) * here, :rest] = tail[
                :, p * rest : (p + 1) * rest
            ]
    for i in range(here):
        pieces = [wide_ref[t, pl.ds(i, tokens, stride=here), :] for t in range(full + 1)]
        out_ref[i] = jnp.concatenate(pieces, axis=1)[:, :share].astype(BF16)


def unpack(rows, here, tokens, share):
    full, _ = tiles_of(share)
    out = jax.ShapeDtypeStruct((here, tokens, share), BF16)
    scratch = jax.ShapeDtypeStruct((full + 1, tokens * here, LANES), F32)
    return pl.pallas_call(
        unpack_kernel,
        out_shape=out,
        in_specs=[VMEM_SPEC],
        out_specs=VMEM_SPEC,
        scratch_shapes=[pltpu.VMEM(scratch.shape, F32)],
        compiler_params=params(rows, out, scratch),
        cost_estimate=takes(0.9),
        name="unpack",
    )(rows)


SWAP = [(0, 1), (1, 0)]


def on_device(
    latents, fresh, noise_level, window_mask, mod_table, keep_coef, layer_coef,
    w_qkv, w_out, w_fc1, w_fc2,
):
    here, tokens_all, share = latents.shape
    features = mod_table.shape[2]
    groups = lax.axis_size("frame")
    frames = groups * here
    frame_index = lax.axis_index("frame")
    y_index, core_index = lax.axis_index("y"), lax.axis_index("core")
    place = (2 * y_index + core_index).astype(jnp.int32).reshape(1)
    group_tokens = tokens_all // groups
    split = group_tokens % 2 == 0
    tokens = group_tokens // 2 if split else group_tokens
    block = max(frames, LANES)
    chunk_count = 2 if tokens % 2 == 0 and tokens * frames // 2 % block == 0 else 1
    size = tokens // chunk_count
    rows = size * frames

    swap_core = functools.partial(lax.ppermute, axis_name="core", perm=SWAP)
    swap_y = functools.partial(lax.ppermute, axis_name="y", perm=SWAP)
    w_qkv = jnp.swapaxes(w_qkv, 1, 2)
    qkv_other = swap_core(w_qkv)
    out_far = swap_y(w_out)
    out_core, out_corner, fc2_other = swap_core(w_out), swap_core(out_far), swap_core(w_fc2)
    payload = make_payload(
        frame_index.astype(jnp.int32).reshape(1), noise_level, window_mask, latents, fresh,
        frames, tokens_all // tokens, chunk_count,
    )
    if split:
        received = lax.all_to_all(payload, ("frame", "core"), 0, 0, tiled=True)
        received = received.reshape((groups, 2) + received.shape[1:])
    else:
        received = lax.all_to_all(payload, "frame", 0, 0, tiled=True)
        partner = swap_core(received)
        first = core_index == 0
        received = jnp.stack(
            [jnp.where(first, received, partner), jnp.where(first, partner, received)], axis=1
        )
    received, qkv_other, out_core, out_far, fc2_other = lax.optimization_barrier(
        (received, qkv_other, out_core, out_far, fc2_other)
    )
    full, rest = tiles_of(share)
    arrived = [received[:, :, n] for n in range(chunk_count)]
    arrived_other = [swap_y(part) for part in arrived]
    weights = [qkv_other]
    places = [(0, 0, 0, w_qkv.shape[0])]
    for n in range(2):
        first, second = ((w_out, out_core), (out_far, out_corner))[n]
        weights += [first, second, first, second]
        to = 2 * n * share
        places += [(1, to, 0, full * LANES), (1, to + full * LANES, 0, full * LANES)]
        to += 2 * full * LANES
        places += [(1, to, full * LANES, rest), (1, to + rest, full * LANES, rest)]
    weights.append(fc2_other)
    places.append((2, 0, 0, w_fc2.shape[0]))
    held = (w_qkv.shape, (4 * share, features), w_fc2.shape)
    norm_mod, feed_mod, gate_mod, pair, mask, flag, qkv_other, out_all, fc2_other = prepare(
        place, arrived[0], jnp.swapaxes(mod_table, 0, 1), keep_coef, layer_coef,
        weights, places, held, here, size * rest, block,
    )
    attention_weights = (w_qkv, qkv_other)

    state = []
    for n in range(chunk_count):
        results = attention_call(
            functools.partial(first_attention_kernel, size),
            (arrived[n], arrived_other[n], flag, norm_mod, mask) + attention_weights,
            rows, features, size,
        )
        current, part, later = results
        state.append((current, part, swap_y(part), later))
    feed_weights = (out_all, w_fc1, swap_core(w_fc1), w_fc2, fc2_other)
    fed = []
    for current, part, part_other, later in state:
        after, feed = feed_call(flag, current, part, part_other, feed_mod, feed_weights, False)
        fed.append((current, after, feed, swap_y(feed), later))
    state = []
    for arrays in fed:
        current, part = attention_call(
            functools.partial(next_attention_kernel, size),
            arrays + (norm_mod, gate_mod, pair, mask) + attention_weights,
            rows, features,
        )
        state.append((current, part, swap_y(part)))
    parts = []
    for current, part, part_other in state:
        after, feed_here, feed_there = feed_call(
            flag, current, part, part_other, feed_mod, feed_weights, True
        )
        parts.append((current, after, feed_here, swap_y(feed_there)))
    result = finish(flag, gate_mod, pair, parts, groups)
    if split:
        result = result.reshape((groups * 2,) + result.shape[2:])
        result = lax.all_to_all(result, ("frame", "core"), 0, 0, tiled=True)
    else:
        result = jnp.where(core_index == 0, result[:, 0], result[:, 1])
        result = lax.all_to_all(result, "frame", 0, 0, tiled=True)
    return unpack(result, here, tokens_all, share)


def solution(mesh):
    groups, heads = mesh.shape["frame"], mesh.shape["head"]
    inner = Mesh(mesh.devices.reshape(groups, heads // 2, 2), ("frame", "y", "core"))
    head = ("y", "core")
    in_specs = (
        P("frame", None, head),
        P(None, None, head),
        P("frame"),
        P("frame", None),
        P(),
        P(),
        P(),
        P(None, None, head),
        P(head, None),
        P(None, head),
        P(head, None),
    )
    return jax.shard_map(
        on_device, mesh=inner, in_specs=in_specs, out_specs=P("frame", None, head), check_vma=False
    )
```

```python
import functools
import math

import jax
import jax.numpy as jnp
from jax import lax
from jax.experimental import pallas as pl
from jax.experimental.pallas import tpu as pltpu
from jax.sharding import Mesh, PartitionSpec as P

HD = 72
W = 8
OFFSETS = 2 * W + 1
EPSILON = 1e-06
F32 = jnp.float32
BF16 = jnp.bfloat16
LANES = 128
VMEM_SPEC = pl.BlockSpec(memory_space=pltpu.VMEM)
SMEM_SPEC = pl.BlockSpec(memory_space=pltpu.SMEM)
HBM_SPEC = pl.BlockSpec(memory_space=pltpu.HBM)


def in_hbm(*arrays):
    return [pltpu.with_memory_space_constraint(array, pltpu.HBM) for array in arrays]


def params(*arrays):
    held = sum(math.prod(a.shape) * jnp.dtype(a.dtype).itemsize for a in arrays)
    return pltpu.CompilerParams(vmem_limit_bytes=held + 8 * 1024 * 1024)


def takes(microseconds):
    return pl.CostEstimate(
        flops=0, bytes_accessed=int(microseconds * 3.3e6), transcendentals=0
    )


def tiles_of(share):
    return share // LANES, share % LANES


def normalise(values, shift_rows, scale_rows):
    center = values - jnp.mean(values, axis=-1, keepdims=True)
    spread = jnp.mean(center * center, axis=-1, keepdims=True)
    return center * lax.rsqrt(spread + EPSILON) * (1.0 + scale_rows) + shift_rows


def payload_kernel(
    frames, x_ref, frame_far, level_far, window_far, fresh_far, out_ref,
    rows_ref, frame_ref, level_ref, window_ref, fresh_ref, sems,
):
    fars = (window_far, level_far, frame_far, fresh_far)
    nears = (window_ref, level_ref, frame_ref, fresh_ref)
    copies = [pltpu.make_async_copy(a, b, sems.at[n]) for n, (a, b) in enumerate(zip(fars, nears))]
    for copy in copies:
        copy.start()
    for copy in copies:
        copy.wait()
    here, _, share = x_ref.shape
    targets, chunks, _, _ = out_ref.shape
    full, rest = tiles_of(share)
    size = x_ref.shape[1] // (targets * chunks)
    row = lax.broadcasted_iota(jnp.int32, (here, 1), 0)
    level = jnp.zeros((here, 1), jnp.int32)
    for i in range(here):
        level = jnp.where(row == i, level_ref[i], level)
    offset = lax.broadcasted_iota(jnp.int32, (here, OFFSETS), 1)
    position = frame_ref[0] * here + row + offset - W
    allowed = (window_ref[...] == 1) & (position >= 0) & (position < frames)
    meta = jnp.concatenate([level.astype(F32), allowed.astype(jnp.int32).astype(F32)], axis=1)
    tokens = x_ref.shape[1]
    piece = share // here
    blank = LANES - size * rest - 1 - OFFSETS - piece
    later = fresh_ref[1].astype(F32)
    for j in range(here):
        cut = later[:, j * piece : (j + 1) * piece]
        cut = jnp.concatenate([cut, jnp.zeros((tokens, LANES - piece), F32)], axis=1)
        rows_ref[full + 1, pl.ds(j, tokens, stride=here), :] = cut
    sent = lax.rem(frame_ref[0], size)
    for i in range(here):
        value = x_ref[i].astype(F32)
        if i == here - 1:
            leaves = (frame_ref[0] + 1) * here == frames
            value = jnp.where(leaves, fresh_ref[0].astype(F32), value)
        for t in range(full):
            rows_ref[t, pl.ds(i, tokens, stride=here), :] = value[:, t * LANES : (t + 1) * LANES]
        rows_ref[full, pl.ds(i, tokens, stride=here), :] = jnp.concatenate(
            [value[:, full * LANES :], jnp.zeros((tokens, LANES - rest), F32)], axis=1
        )
    for d in range(targets):
        for n in range(chunks):
            first = (d * chunks + n) * size * here
            pieces = [rows_ref[t, first : first + size * here, :] for t in range(full)]
            tails = [
                rows_ref[full, first + p * here : first + (p + 1) * here, :][:, :rest]
                for p in range(size)
            ]
            cuts = [
                rows_ref[full + 1, first + p * here : first + (p + 1) * here, :][:, :piece]
                for p in range(size)
            ]
            cut = cuts[0]
            for p in range(1, size):
                cut = jnp.where(sent == p, cuts[p], cut)
            tails += [meta, cut]
            if blank:
                tails.append(jnp.zeros((here, blank), F32))
            pieces.append(jnp.concatenate(tails, axis=1))
            out_ref[d, n] = jnp.concatenate(pieces, axis=0).astype(BF16)


def make_payload(frame_index, noise_level, window_mask, x, fresh, frames, targets, chunks):
    here, tokens, share = x.shape
    full, rest = tiles_of(share)
    size = tokens // (targets * chunks)
    out = jax.ShapeDtypeStruct((targets, chunks, (full * size + 1) * here, LANES), BF16)
    scratch = jax.ShapeDtypeStruct((full + 2, tokens * here, LANES), F32)
    return pl.pallas_call(
        functools.partial(payload_kernel, frames),
        out_shape=out,
        in_specs=[VMEM_SPEC] + [HBM_SPEC] * 4,
        out_specs=VMEM_SPEC,
        scratch_shapes=[
            pltpu.VMEM(scratch.shape, F32),
            pltpu.SMEM(frame_index.shape, jnp.int32),
            pltpu.SMEM(noise_level.shape, jnp.int32),
            pltpu.VMEM(window_mask.shape, jnp.int32),
            pltpu.VMEM(fresh.shape, BF16),
            pltpu.SemaphoreType.DMA((4,)),
        ],
        compiler_params=params(x, fresh, out, scratch),
        cost_estimate=takes(2),
        name="payload",
    )(x, *in_hbm(frame_index, noise_level, window_mask, fresh))


def fresh_piece(block, size, here, share):
    _, rest = tiles_of(share)
    piece = share // here
    first = size * rest + 1 + OFFSETS
    tail = block[-here:, first : first + piece]
    return jnp.concatenate([tail[j : j + 1] for j in range(here)], axis=1)


def chunk_rows(block, size, here, share):
    full, rest = tiles_of(share)
    tail = block[full * size * here :]
    result = []
    for p in range(size):
        pieces = [block[(t * size + p) * here : (t * size + p + 1) * here] for t in range(full)]
        result.append(jnp.concatenate(pieces + [tail[:, p * rest : (p + 1) * rest]], axis=1))
    return result


def prepare_kernel(
    here, lane_at, places, place_ref, received_ref, table_far, keep_ref, layer_ref, *refs
):
    sources, refs = refs[: len(places)], refs[len(places) :]
    norm_ref, feed_ref, gate_ref, pair_ref, mask_ref, flag_ref = refs[:6]
    held, (table_ref, table_sems, sems) = refs[6:-3], refs[-3:]
    table_copies = start_copies(
        (table_far,), [(0, 0, 0, table_far.shape[0])], (table_ref,), table_sems
    )
    copies = start_copies(sources, places, held, sems)
    flag_ref[...] = jnp.where(place_ref[0] < 2, jnp.ones_like(flag_ref), 0.0)
    groups = received_ref.shape[0]
    frames = groups * here
    levels = table_ref.shape[1]
    meta = [received_ref[g, 0].astype(F32)[-here:, lane_at:] for g in range(groups)]
    meta = jnp.concatenate(meta, axis=0)
    level = meta[:, 0:1]
    ids = lax.broadcasted_iota(jnp.int32, (frames, levels), 1).astype(F32)
    hot = level == ids
    hot_bf = hot.astype(BF16)
    for copy in table_copies:
        copy.wait()
    targets = [(norm_ref, 0), (norm_ref, 1), (feed_ref, 0), (feed_ref, 1), (feed_ref, 2), (gate_ref, 0)]
    for j, (target, at) in enumerate(targets):
        rows = table_ref[j]
        high = rows.astype(BF16)
        rest = rows - high.astype(F32)
        middle = rest.astype(BF16)
        low = (rest - middle.astype(F32)).astype(BF16)
        total = jnp.dot(hot_bf, high, preferred_element_type=F32)
        total += jnp.dot(hot_bf, middle, preferred_element_type=F32)
        total += jnp.dot(hot_bf, low, preferred_element_type=F32)
        target[at] = total
    keep = jnp.sum(jnp.where(hot, keep_ref[...], 0.0), axis=1, keepdims=True)
    layer = jnp.sum(jnp.where(hot, layer_ref[...], 0.0), axis=1, keepdims=True)
    lane = lax.broadcasted_iota(jnp.int32, (frames, LANES), 1)
    pair_ref[...] = jnp.where(lane == 0, keep, layer)

    block = mask_ref.shape[0]
    row = lax.broadcasted_iota(jnp.int32, (frames, block), 0)
    column = lax.broadcasted_iota(jnp.int32, (frames, block), 1)
    for t in range(block // frames):
        distance = column - t * frames - row
        inside = (column >= t * frames) & (column < (t + 1) * frames)
        is_open = jnp.zeros((frames, block), F32)
        for o in range(OFFSETS):
            is_open = jnp.where(distance == o - W, meta[:, 1 + o : 2 + o], is_open)
        is_open = jnp.where(inside, is_open, 0.0)
        mask_ref[t * frames : (t + 1) * frames, :] = jnp.where(is_open > 0.5, 0.0, -1e30)
    for copy in copies:
        copy.wait()


def prepare(place, received, table, keep, layer, weights, places, held, here, lane_at, block):
    frames = received.shape[0] * here
    features = table.shape[2]
    outs = (
        jax.ShapeDtypeStruct((2, frames, features), F32),
        jax.ShapeDtypeStruct((3, frames, features), F32),
        jax.ShapeDtypeStruct((1, frames, features), F32),
        jax.ShapeDtypeStruct((frames, LANES), F32),
        jax.ShapeDtypeStruct((block, block), F32),
        jax.ShapeDtypeStruct((8, LANES), F32),
    ) + tuple(jax.ShapeDtypeStruct(shape, BF16) for shape in held)
    (table,) = in_hbm(table)
    return pl.pallas_call(
        functools.partial(prepare_kernel, here, lane_at, tuple(places)),
        out_shape=outs,
        in_specs=[SMEM_SPEC, VMEM_SPEC, HBM_SPEC, VMEM_SPEC, VMEM_SPEC]
        + [HBM_SPEC] * len(weights),
        out_specs=(VMEM_SPEC,) * len(outs),
        scratch_shapes=[
            pltpu.VMEM(table.shape, F32),
            pltpu.SemaphoreType.DMA((3,)),
            pltpu.SemaphoreType.DMA((3 * len(weights),)),
        ],
        compiler_params=params(received, table, *outs),
        cost_estimate=takes(5),
        name="prepare",
    )(place, received, table, keep.reshape(1, -1), layer.reshape(1, -1), *in_hbm(*weights))


def start_copies(sources, places, targets, sems):
    copies = []
    for source, (index, to, at, rows) in zip(sources, places):
        parts = 3 if rows % 48 == 0 or rows % 3 == 0 and len(source.shape) > 2 else 1
        for n in range(parts):
            size = rows // parts
            copies.append(
                pltpu.make_async_copy(
                    source.at[pl.ds(at + n * size, size)],
                    targets[index].at[pl.ds(to + n * size, size)],
                    sems.at[len(copies)],
                )
            )
            copies[-1].start()
    return copies


def attention_rows(current, norm_ref, mask_ref, weights, out_ref):
    normed = [normalise(rows, norm_ref[0], norm_ref[1]).astype(BF16) for rows in current]
    normed = normed[0] if len(normed) == 1 else jnp.concatenate(normed, axis=0)
    qkv_me, qkv_other = weights
    share = qkv_me.shape[1]
    heads = share // HD
    block = mask_ref.shape[0]
    count = normed.shape[0] // block
    bias = mask_ref[...]
    lane = lax.broadcasted_iota(jnp.int32, (1, share), 1)
    head_lanes = [
        ((lane >= HD * h) & (lane < HD * (h + 1))).astype(jnp.int32).astype(F32).astype(BF16)
        for h in range(heads)
    ]
    scale = math.log2(math.e) / math.sqrt(HD)
    projected = []
    for side, qkv in enumerate((qkv_me, qkv_other)):
        projected.append(
            [
                lax.dot_general(
                    normed, qkv[t], (((1,), (1,)), ((), ())), preferred_element_type=F32
                ).astype(BF16)
                for t in range(3)
            ]
        )
    units = [(side, slice(b * block, (b + 1) * block)) for side in range(2) for b in range(count)]
    scores = []
    for side, at in units:
        query, key = projected[side][0][at], projected[side][1][at]
        keys = jnp.concatenate([key * lanes for lanes in head_lanes], axis=0)
        raw = lax.dot_general(query, keys, (((1,), (1,)), ((), ())), preferred_element_type=F32)
        scores += [
            raw[:, h * block : (h + 1) * block] + bias for h in range(heads)
        ]
    tops = [jnp.max(s, axis=-1, keepdims=True) for s in scores]
    weights_of = [jnp.exp2((s - t) * scale) for s, t in zip(scores, tops)]
    parts = [1.0 / jnp.sum(w, axis=-1, keepdims=True) for w in weights_of]
    shares = [(w * part).astype(BF16) for w, part in zip(weights_of, parts)]
    attended = []
    for n, (side, at) in enumerate(units):
        value = projected[side][2][at]
        values = jnp.concatenate([value * lanes for lanes in head_lanes], axis=0)
        row = jnp.concatenate(shares[n * heads : (n + 1) * heads], axis=1)
        attended.append(jnp.dot(row, values, preferred_element_type=F32).astype(BF16))
    sides = [attended[side * count : (side + 1) * count] for side in range(2)]
    sides = [x[0] if count == 1 else jnp.concatenate(x, axis=0) for x in sides]
    full, _ = tiles_of(share)
    tiles = [x[:, t * LANES : (t + 1) * LANES] for x in sides for t in range(full)]
    pack_half(out_ref, tiles, jnp.concatenate([x[:, full * LANES :] for x in sides], axis=1))


def shifted_in(rows, fresh_row):
    frames = rows.shape[0]
    first = lax.broadcasted_iota(jnp.int32, (frames, 1), 0) == 0
    return jnp.where(first, fresh_row, pltpu.roll(rows, 1, 0))


def first_attention_kernel(
    count, mine_ref, other_ref, flag_ref, norm_ref, mask_ref,
    qkv_me, qkv_other, cur_ref, part_ref, fresh_ref,
):
    groups, cores = mine_ref.shape[:2]
    frames = norm_ref.shape[1]
    here = frames // groups
    share = qkv_me.shape[1]
    first_half = flag_ref[0:1, :] > 0.5
    blocks = []
    for g in range(groups):
        left, right = [], []
        for c in range(cores):
            mine, other = mine_ref[g, c].astype(F32), other_ref[g, c].astype(F32)
            left.append(jnp.where(first_half, mine, other))
            right.append(jnp.where(first_half, other, mine))
        if g < count:
            cuts = [fresh_piece(block, count, here, share) for block in left + right]
            fresh_ref[g : g + 1, :] = jnp.concatenate(cuts, axis=1)
        blocks.append([chunk_rows(block, count, here, share) for block in left + right])
    current = []
    for p in range(count):
        rows = [jnp.concatenate([part[p] for part in parts], axis=1) for parts in blocks]
        rows = pltpu.roll(jnp.concatenate(rows, axis=0), 1, 0)
        cur_ref[p * frames : (p + 1) * frames, :] = rows.astype(BF16)
        current.append(rows)
    attention_rows(current, norm_ref, mask_ref, (qkv_me, qkv_other), part_ref)


def next_attention_kernel(
    count, old_ref, after_ref, mine_ref, other_ref, fresh_ref, norm_ref, gate_ref, pair_ref,
    mask_ref, qkv_me, qkv_other, cur_ref, part_ref,
):
    frames = norm_ref.shape[1]
    keep, layer = pair_ref[:, 0:1], pair_ref[:, 1:2]
    current = []
    for p in range(count):
        at = slice(p * frames, (p + 1) * frames)
        total = mine_ref[at, :].astype(F32) + other_ref[at, :].astype(F32)
        rows = keep * old_ref[at, :].astype(F32) + layer * (
            after_ref[at, :].astype(F32) + gate_ref[0] * total
        )
        rows = shifted_in(rows, fresh_ref[p : p + 1, :]).astype(BF16)
        cur_ref[at, :] = rows
        current.append(rows.astype(F32))
    attention_rows(current, norm_ref, mask_ref, (qkv_me, qkv_other), part_ref)


def attention_call(kernel, arrays, rows, features, fresh_count=0):
    outs = (
        jax.ShapeDtypeStruct((rows, features), BF16),
        jax.ShapeDtypeStruct((rows * features // 2 // LANES, LANES), BF16),
    )
    if fresh_count:
        outs += (jax.ShapeDtypeStruct((fresh_count, features), F32),)
    return pl.pallas_call(
        kernel,
        out_shape=outs,
        in_specs=[VMEM_SPEC] * len(arrays),
        out_specs=(VMEM_SPEC,) * len(outs),
        compiler_params=params(*arrays, *outs),
        cost_estimate=takes(2.8),
        name="attention",
    )(*arrays)


def pack_half(ref, tiles, tail):
    rows = tail.shape[0]
    for n, tile in enumerate(tiles):
        ref[n * rows : (n + 1) * rows, :] = tile
    ref[len(tiles) * rows :, :] = jnp.concatenate([tail[: rows // 2], tail[rows // 2 :]], axis=1)


def pick_half(first_half, value):
    middle = value.shape[1] // 2 // LANES
    tiles = []
    for t in range(middle):
        left, right = (value[:, n * LANES : (n + 1) * LANES] for n in (t, t + middle + 1))
        tiles.append(jnp.where(first_half, left, right))
    split = value[:, middle * LANES : (middle + 1) * LANES]
    cut = LANES // 2
    return tiles, jnp.where(first_half[:, :cut], split[:, :cut], split[:, cut:])


def unpack_half(ref, rows):
    count = ref.shape[0] // rows
    tail = ref[count * rows :, :]
    tail = jnp.concatenate([tail[:, : LANES // 2], tail[:, LANES // 2 :]], axis=0)
    tiles = [ref[n * rows : (n + 1) * rows, :] for n in range(count)]
    return jnp.concatenate(tiles, axis=1), tail


def gelu(x):
    scale = math.sqrt(2.0 / math.pi)
    half = 0.5 * x
    return half + half * jnp.tanh(x * (scale + (0.044715 * scale) * (x * x)))


def pieces_of(width, size):
    return [(s, min(size, width - s)) for s in range(0, width, size)]


def feed_kernel(
    halves, flag_ref, cur_ref, mine_ref, other_ref, mod_ref,
    out_all, fc1_me, fc1_other, fc2_me, fc2_other, *rest,
):
    outs, hidden_ref = (rest[:-2], rest[-2]) if halves else (rest[:-1], rest[-1])
    after_ref = outs[0]
    frames = mod_ref.shape[1]
    tokens = cur_ref.shape[0] // frames
    normed = []
    rows, half = cur_ref.shape[0], out_all.shape[0] // 2
    attention_total = None
    for n, ref in enumerate((mine_ref, other_ref)):
        main, tail = unpack_half(ref, rows)
        middle = n * half + main.shape[1]
        part = jnp.dot(main, out_all[n * half : middle], preferred_element_type=F32)
        part += jnp.dot(tail, out_all[middle : (n + 1) * half], preferred_element_type=F32)
        attention_total = part if n == 0 else attention_total + part
    for p in range(tokens):
        at = slice(p * frames, (p + 1) * frames)
        after = (cur_ref[at, :].astype(F32) + mod_ref[0] * attention_total[at]).astype(BF16)
        after_ref[at, :] = after
        normed.append(normalise(after.astype(F32), mod_ref[1], mod_ref[2]).astype(BF16))
    normed = normed[0] if tokens == 1 else jnp.concatenate(normed, axis=0)
    units, features = fc2_me.shape
    for side, w1 in enumerate((fc1_me, fc1_other)):
        for start, size in pieces_of(units, 256):
            hidden = gelu(
                jnp.dot(normed, w1[:, start : start + size], preferred_element_type=F32)
            )
            hidden_ref[:, side * units + start : side * units + start + size] = hidden.astype(BF16)

    def product(at):
        return jnp.dot(
            hidden_ref[:, :units], fc2_me[:, at], preferred_element_type=F32
        ) + jnp.dot(hidden_ref[:, units:], fc2_other[:, at], preferred_element_type=F32)

    target = rest[-1] if halves else outs[1]
    for start, size in pieces_of(features, 256):
        at = slice(start, start + size)
        target[:, at] = product(at).astype(BF16)
    if not halves:
        return
    first_half = flag_ref[0:1, :] > 0.5
    pack_half(outs[1], *pick_half(first_half, target[...]))
    pack_half(outs[2], *pick_half(jnp.logical_not(first_half), target[...]))


def feed_call(flag, cur, mine, other, mod, weights, halves):
    rows, features = cur.shape
    shape = jax.ShapeDtypeStruct((rows, features), BF16)
    packed = jax.ShapeDtypeStruct((rows * features // 2 // LANES, LANES), BF16)
    outs = (shape, packed, packed) if halves else (shape, shape)
    return pl.pallas_call(
        functools.partial(feed_kernel, halves),
        out_shape=outs,
        in_specs=[VMEM_SPEC] * 10,
        out_specs=(VMEM_SPEC,) * len(outs),
        scratch_shapes=[pltpu.VMEM((rows, 2 * weights[1].shape[1]), BF16)]
        + ([pltpu.VMEM((rows, features), BF16)] if halves else []),
        compiler_params=params(cur, mine, other, mod, *weights, *outs),
        cost_estimate=takes(2.8),
        name="feed",
    )(flag, cur, mine, other, mod, *weights)


def finish_kernel(chunks, flag_ref, gate_ref, pair_ref, *refs):
    out_ref = refs[-1]
    groups, cores = out_ref.shape[:2]
    _, frames, features = gate_ref.shape
    here = frames // groups
    half = features // 2
    share = half // cores
    full, rest = tiles_of(share)
    first_half = flag_ref[0:1, :] > 0.5
    keep, layer = pair_ref[:, 0:1], pair_ref[:, 1:2]
    gates = pick_half(first_half, gate_ref[0])
    gates = gates[0] + [gates[1]]
    results = []
    for n in range(chunks):
        old_ref, after_ref, mine_ref, other_ref = refs[4 * n : 4 * n + 4]
        rows = old_ref.shape[0]
        (mine, mine_tail), (theirs, their_tail) = (
            unpack_half(ref, rows) for ref in (mine_ref, other_ref)
        )
        main = mine.astype(F32) + theirs.astype(F32)
        main_tail = mine_tail.astype(F32) + their_tail.astype(F32)
        for p in range(rows // frames):
            at = slice(p * frames, (p + 1) * frames)
            old, after = (
                pick_half(first_half, ref[at, :].astype(F32)) for ref in (old_ref, after_ref)
            )
            old, after = old[0] + [old[1]], after[0] + [after[1]]
            total = [main[at, t * LANES : (t + 1) * LANES] for t in range(len(old) - 1)]
            total.append(main_tail[at])
            done = [
                keep * o + layer * (a + g * t) for o, a, g, t in zip(old, after, gates, total)
            ]
            left, right = jnp.concatenate(done, axis=1), jnp.concatenate(done[-1:] + done[:-1], axis=1)
            results.append(jnp.where(first_half[:, 0:1], left, right))
    unused = LANES - len(results) * rest
    for c in range(cores):
        shares = [r[:, c * share : (c + 1) * share] for r in results]
        for g in range(groups):
            rows = [s[g * here : (g + 1) * here] for s in shares]
            pieces = [r[:, t * LANES : (t + 1) * LANES] for t in range(full) for r in rows]
            tails = [r[:, full * LANES :] for r in rows]
            if unused:
                tails.append(jnp.zeros((here, unused), F32))
            pieces.append(jnp.concatenate(tails, axis=1))
            out_ref[g, c] = jnp.concatenate(pieces, axis=0).astype(BF16)


def finish(flag, gate, pair, parts, groups):
    _, frames, features = gate.shape
    tokens = sum(part[0].shape[0] for part in parts) // frames
    full, _ = tiles_of(features // 4)
    arrays = [array for part in parts for array in part]
    out = jax.ShapeDtypeStruct((groups, 2, (full * tokens + 1) * (frames // groups), LANES), BF16)
    return pl.pallas_call(
        functools.partial(finish_kernel, len(parts)),
        out_shape=out,
        in_specs=[VMEM_SPEC] * (3 + len(arrays)),
        out_specs=VMEM_SPEC,
        compiler_params=params(gate, pair, out, *arrays),
        cost_estimate=takes(0.8),
        name="finish",
    )(flag, gate, pair, *arrays)


def unpack_kernel(rows_ref, out_ref, wide_ref):
    here, tokens, share = out_ref.shape
    sources = rows_ref.shape[0]
    size = tokens // sources
    full, rest = tiles_of(share)
    for d in range(sources):
        block = rows_ref[d].astype(F32)
        first = d * size * here
        for t in range(full):
            wide_ref[t, first : first + size * here, :] = block[t * size * here : (t + 1) * size * here]
        tail = block[full * size * here :]
        for p in range(size):
            wide_ref[full, first + p * here : first + (p + 1) * here, :rest] = tail[
                :, p * rest : (p + 1) * rest
            ]
    for i in range(here):
        pieces = [wide_ref[t, pl.ds(i, tokens, stride=here), :] for t in range(full + 1)]
        out_ref[i] = jnp.concatenate(pieces, axis=1)[:, :share].astype(BF16)


def unpack(rows, here, tokens, share):
    full, _ = tiles_of(share)
    out = jax.ShapeDtypeStruct((here, tokens, share), BF16)
    scratch = jax.ShapeDtypeStruct((full + 1, tokens * here, LANES), F32)
    return pl.pallas_call(
        unpack_kernel,
        out_shape=out,
        in_specs=[VMEM_SPEC],
        out_specs=VMEM_SPEC,
        scratch_shapes=[pltpu.VMEM(scratch.shape, F32)],
        compiler_params=params(rows, out, scratch),
        cost_estimate=takes(0.9),
        name="unpack",
    )(rows)


SWAP = [(0, 1), (1, 0)]


def on_device(
    latents, fresh, noise_level, window_mask, mod_table, keep_coef, layer_coef,
    w_qkv, w_out, w_fc1, w_fc2,
):
    here, tokens_all, share = latents.shape
    features = mod_table.shape[2]
    groups = lax.axis_size("frame")
    frames = groups * here
    frame_index = lax.axis_index("frame")
    y_index, core_index = lax.axis_index("y"), lax.axis_index("core")
    place = (2 * y_index + core_index).astype(jnp.int32).reshape(1)
    group_tokens = tokens_all // groups
    split = group_tokens % 2 == 0
    tokens = group_tokens // 2 if split else group_tokens
    block = max(frames, LANES)
    chunk_count = 2 if tokens % 2 == 0 and tokens * frames // 2 % block == 0 else 1
    size = tokens // chunk_count
    rows = size * frames

    swap_core = functools.partial(lax.ppermute, axis_name="core", perm=SWAP)
    swap_y = functools.partial(lax.ppermute, axis_name="y", perm=SWAP)
    w_qkv = jnp.swapaxes(w_qkv, 1, 2)
    qkv_other = swap_core(w_qkv)
    out_far = swap_y(w_out)
    out_core, out_corner, fc2_other = swap_core(w_out), swap_core(out_far), swap_core(w_fc2)
    payload = make_payload(
        frame_index.astype(jnp.int32).reshape(1), noise_level, window_mask, latents, fresh,
        frames, tokens_all // tokens, chunk_count,
    )
    if split:
        received = lax.all_to_all(payload, ("frame", "core"), 0, 0, tiled=True)
        received = received.reshape((groups, 2) + received.shape[1:])
    else:
        received = lax.all_to_all(payload, "frame", 0, 0, tiled=True)
        partner = swap_core(received)
        first = core_index == 0
        received = jnp.stack(
            [jnp.where(first, received, partner), jnp.where(first, partner, received)], axis=1
        )
    received, qkv_other, out_core, out_far, fc2_other = lax.optimization_barrier(
        (received, qkv_other, out_core, out_far, fc2_other)
    )
    full, rest = tiles_of(share)
    arrived = [received[:, :, n] for n in range(chunk_count)]
    arrived_other = [swap_y(part) for part in arrived]
    weights = [qkv_other]
    places = [(0, 0, 0, w_qkv.shape[0])]
    for n in range(2):
        first, second = ((w_out, out_core), (out_far, out_corner))[n]
        weights += [first, second, first, second]
        to = 2 * n * share
        places += [(1, to, 0, full * LANES), (1, to + full * LANES, 0, full * LANES)]
        to += 2 * full * LANES
        places += [(1, to, full * LANES, rest), (1, to + rest, full * LANES, rest)]
    weights.append(fc2_other)
    places.append((2, 0, 0, w_fc2.shape[0]))
    held = (w_qkv.shape, (4 * share, features), w_fc2.shape)
    norm_mod, feed_mod, gate_mod, pair, mask, flag, qkv_other, out_all, fc2_other = prepare(
        place, arrived[0], jnp.swapaxes(mod_table, 0, 1), keep_coef, layer_coef,
        weights, places, held, here, size * rest, block,
    )
    attention_weights = (w_qkv, qkv_other)

    state = []
    for n in range(chunk_count):
        results = attention_call(
            functools.partial(first_attention_kernel, size),
            (arrived[n], arrived_other[n], flag, norm_mod, mask) + attention_weights,
            rows, features, size,
        )
        current, part, later = results
        state.append((current, part, swap_y(part), later))
    feed_weights = (out_all, w_fc1, swap_core(w_fc1), w_fc2, fc2_other)
    fed = []
    for current, part, part_other, later in state:
        after, feed = feed_call(flag, current, part, part_other, feed_mod, feed_weights, False)
        fed.append((current, after, feed, swap_y(feed), later))
    state = []
    for arrays in fed:
        current, part = attention_call(
            functools.partial(next_attention_kernel, size),
            arrays + (norm_mod, gate_mod, pair, mask) + attention_weights,
            rows, features,
        )
        state.append((current, part, swap_y(part)))
    parts = []
    for current, part, part_other in state:
        after, feed_here, feed_there = feed_call(
            flag, current, part, part_other, feed_mod, feed_weights, True
        )
        parts.append((current, after, feed_here, swap_y(feed_there)))
    result = finish(flag, gate_mod, pair, parts, groups)
    if split:
        result = result.reshape((groups * 2,) + result.shape[2:])
        result = lax.all_to_all(result, ("frame", "core"), 0, 0, tiled=True)
    else:
        result = jnp.where(core_index == 0, result[:, 0], result[:, 1])
        result = lax.all_to_all(result, "frame", 0, 0, tiled=True)
    return unpack(result, here, tokens_all, share)


def solution(mesh):
    groups, heads = mesh.shape["frame"], mesh.shape["head"]
    inner = Mesh(mesh.devices.reshape(groups, heads // 2, 2), ("frame", "y", "core"))
    head = ("y", "core")
    in_specs = (
        P("frame", None, head),
        P(None, None, head),
        P("frame"),
        P("frame", None),
        P(),
        P(),
        P(),
        P(None, None, head),
        P(head, None),
        P(None, head),
        P(head, None),
    )
    return jax.shard_map(
        on_device, mesh=inner, in_specs=in_specs, out_specs=P("frame", None, head), check_vma=False
    )
```

```python
import functools
import math

import jax
import jax.numpy as jnp
from jax import lax
from jax.experimental import pallas as pl
from jax.experimental.pallas import tpu as pltpu
from jax.sharding import Mesh, PartitionSpec as P

HD = 72
W = 8
OFFSETS = 2 * W + 1
EPSILON = 1e-06
F32 = jnp.float32
BF16 = jnp.bfloat16
LANES = 128
VMEM_SPEC = pl.BlockSpec(memory_space=pltpu.VMEM)
SMEM_SPEC = pl.BlockSpec(memory_space=pltpu.SMEM)
HBM_SPEC = pl.BlockSpec(memory_space=pltpu.HBM)


def in_hbm(*arrays):
    return [pltpu.with_memory_space_constraint(array, pltpu.HBM) for array in arrays]


def params(*arrays):
    held = sum(math.prod(a.shape) * jnp.dtype(a.dtype).itemsize for a in arrays)
    return pltpu.CompilerParams(vmem_limit_bytes=held + 8 * 1024 * 1024)


def takes(microseconds):
    return pl.CostEstimate(
        flops=0, bytes_accessed=int(microseconds * 3.3e6), transcendentals=0
    )


def tiles_of(share):
    return share // LANES, share % LANES


def normalise(values, shift_rows, scale_rows):
    center = values - jnp.mean(values, axis=-1, keepdims=True)
    spread = jnp.mean(center * center, axis=-1, keepdims=True)
    return center * lax.rsqrt(spread + EPSILON) * (1.0 + scale_rows) + shift_rows


def payload_kernel(
    frames, x_ref, frame_far, level_far, window_far, fresh_far, out_ref,
    rows_ref, frame_ref, level_ref, window_ref, fresh_ref, sems,
):
    fars = (window_far, level_far, frame_far, fresh_far)
    nears = (window_ref, level_ref, frame_ref, fresh_ref)
    copies = [pltpu.make_async_copy(a, b, sems.at[n]) for n, (a, b) in enumerate(zip(fars, nears))]
    for copy in copies:
        copy.start()
    for copy in copies:
        copy.wait()
    here, _, share = x_ref.shape
    targets, chunks, _, _ = out_ref.shape
    full, rest = tiles_of(share)
    size = x_ref.shape[1] // (targets * chunks)
    row = lax.broadcasted_iota(jnp.int32, (here, 1), 0)
    level = jnp.zeros((here, 1), jnp.int32)
    for i in range(here):
        level = jnp.where(row == i, level_ref[i], level)
    offset = lax.broadcasted_iota(jnp.int32, (here, OFFSETS), 1)
    position = frame_ref[0] * here + row + offset - W
    allowed = (window_ref[...] == 1) & (position >= 0) & (position < frames)
    meta = jnp.concatenate([level.astype(F32), allowed.astype(jnp.int32).astype(F32)], axis=1)
    tokens = x_ref.shape[1]
    piece = share // here
    blank = LANES - size * rest - 1 - OFFSETS - piece
    later = fresh_ref[1].astype(F32)
    for j in range(here):
        cut = later[:, j * piece : (j + 1) * piece]
        cut = jnp.concatenate([cut, jnp.zeros((tokens, LANES - piece), F32)], axis=1)
        rows_ref[full + 1, pl.ds(j, tokens, stride=here), :] = cut
    sent = lax.rem(frame_ref[0], size)
    for i in range(here):
        value = x_ref[i].astype(F32)
        if i == here - 1:
            leaves = (frame_ref[0] + 1) * here == frames
            value = jnp.where(leaves, fresh_ref[0].astype(F32), value)
        for t in range(full):
            rows_ref[t, pl.ds(i, tokens, stride=here), :] = value[:, t * LANES : (t + 1) * LANES]
        rows_ref[full, pl.ds(i, tokens, stride=here), :] = jnp.concatenate(
            [value[:, full * LANES :], jnp.zeros((tokens, LANES - rest), F32)], axis=1
        )
    for d in range(targets):
        for n in range(chunks):
            first = (d * chunks + n) * size * here
            pieces = [rows_ref[t, first : first + size * here, :] for t in range(full)]
            tails = [
                rows_ref[full, first + p * here : first + (p + 1) * here, :][:, :rest]
                for p in range(size)
            ]
            cuts = [
                rows_ref[full + 1, first + p * here : first + (p + 1) * here, :][:, :piece]
                for p in range(size)
            ]
            cut = cuts[0]
            for p in range(1, size):
                cut = jnp.where(sent == p, cuts[p], cut)
            tails += [meta, cut]
            if blank:
                tails.append(jnp.zeros((here, blank), F32))
            pieces.append(jnp.concatenate(tails, axis=1))
            out_ref[d, n] = jnp.concatenate(pieces, axis=0).astype(BF16)


def make_payload(frame_index, noise_level, window_mask, x, fresh, frames, targets, chunks):
    here, tokens, share = x.shape
    full, rest = tiles_of(share)
    size = tokens // (targets * chunks)
    out = jax.ShapeDtypeStruct((targets, chunks, (full * size + 1) * here, LANES), BF16)
    scratch = jax.ShapeDtypeStruct((full + 2, tokens * here, LANES), F32)
    return pl.pallas_call(
        functools.partial(payload_kernel, frames),
        out_shape=out,
        in_specs=[VMEM_SPEC] + [HBM_SPEC] * 4,
        out_specs=VMEM_SPEC,
        scratch_shapes=[
            pltpu.VMEM(scratch.shape, F32),
            pltpu.SMEM(frame_index.shape, jnp.int32),
            pltpu.SMEM(noise_level.shape, jnp.int32),
            pltpu.VMEM(window_mask.shape, jnp.int32),
            pltpu.VMEM(fresh.shape, BF16),
            pltpu.SemaphoreType.DMA((4,)),
        ],
        compiler_params=params(x, fresh, out, scratch),
        cost_estimate=takes(2),
        name="payload",
    )(x, *in_hbm(frame_index, noise_level, window_mask, fresh))


def fresh_piece(block, size, here, share):
    _, rest = tiles_of(share)
    piece = share // here
    first = size * rest + 1 + OFFSETS
    tail = block[-here:, first : first + piece]
    return jnp.concatenate([tail[j : j + 1] for j in range(here)], axis=1)


def chunk_rows(block, size, here, share):
    full, rest = tiles_of(share)
    tail = block[full * size * here :]
    result = []
    for p in range(size):
        pieces = [block[(t * size + p) * here : (t * size + p + 1) * here] for t in range(full)]
        result.append(jnp.concatenate(pieces + [tail[:, p * rest : (p + 1) * rest]], axis=1))
    return result


def prepare_kernel(
    here, lane_at, places, place_ref, received_ref, table_far, keep_ref, layer_ref, *refs
):
    sources, refs = refs[: len(places)], refs[len(places) :]
    norm_ref, feed_ref, gate_ref, pair_ref, mask_ref, flag_ref = refs[:6]
    held, (table_ref, table_sems, sems) = refs[6:-3], refs[-3:]
    table_copies = start_copies(
        (table_far,), [(0, 0, 0, table_far.shape[0])], (table_ref,), table_sems
    )
    copies = start_copies(sources, places, held, sems)
    flag_ref[...] = jnp.where(place_ref[0] < 2, jnp.ones_like(flag_ref), 0.0)
    groups = received_ref.shape[0]
    frames = groups * here
    levels = table_ref.shape[1]
    meta = [received_ref[g, 0].astype(F32)[-here:, lane_at:] for g in range(groups)]
    meta = jnp.concatenate(meta, axis=0)
    level = meta[:, 0:1]
    ids = lax.broadcasted_iota(jnp.int32, (frames, levels), 1).astype(F32)
    hot = level == ids
    hot_bf = hot.astype(BF16)
    for copy in table_copies:
        copy.wait()
    targets = [(norm_ref, 0), (norm_ref, 1), (feed_ref, 0), (feed_ref, 1), (feed_ref, 2), (gate_ref, 0)]
    for j, (target, at) in enumerate(targets):
        rows = table_ref[j]
        high = rows.astype(BF16)
        rest = rows - high.astype(F32)
        middle = rest.astype(BF16)
        low = (rest - middle.astype(F32)).astype(BF16)
        total = jnp.dot(hot_bf, high, preferred_element_type=F32)
        total += jnp.dot(hot_bf, middle, preferred_element_type=F32)
        total += jnp.dot(hot_bf, low, preferred_element_type=F32)
        target[at] = total
    keep = jnp.sum(jnp.where(hot, keep_ref[...], 0.0), axis=1, keepdims=True)
    layer = jnp.sum(jnp.where(hot, layer_ref[...], 0.0), axis=1, keepdims=True)
    lane = lax.broadcasted_iota(jnp.int32, (frames, LANES), 1)
    pair_ref[...] = jnp.where(lane == 0, keep, layer)

    block = mask_ref.shape[0]
    row = lax.broadcasted_iota(jnp.int32, (frames, block), 0)
    column = lax.broadcasted_iota(jnp.int32, (frames, block), 1)
    for t in range(block // frames):
        distance = column - t * frames - row
        inside = (column >= t * frames) & (column < (t + 1) * frames)
        is_open = jnp.zeros((frames, block), F32)
        for o in range(OFFSETS):
            is_open = jnp.where(distance == o - W, meta[:, 1 + o : 2 + o], is_open)
        is_open = jnp.where(inside, is_open, 0.0)
        mask_ref[t * frames : (t + 1) * frames, :] = jnp.where(is_open > 0.5, 0.0, -1e30)
    for copy in copies:
        copy.wait()


def prepare(place, received, table, keep, layer, weights, places, held, here, lane_at, block):
    frames = received.shape[0] * here
    features = table.shape[2]
    outs = (
        jax.ShapeDtypeStruct((2, frames, features), F32),
        jax.ShapeDtypeStruct((3, frames, features), F32),
        jax.ShapeDtypeStruct((1, frames, features), F32),
        jax.ShapeDtypeStruct((frames, LANES), F32),
        jax.ShapeDtypeStruct((block, block), F32),
        jax.ShapeDtypeStruct((8, LANES), F32),
    ) + tuple(jax.ShapeDtypeStruct(shape, BF16) for shape in held)
    (table,) = in_hbm(table)
    return pl.pallas_call(
        functools.partial(prepare_kernel, here, lane_at, tuple(places)),
        out_shape=outs,
        in_specs=[SMEM_SPEC, VMEM_SPEC, HBM_SPEC, VMEM_SPEC, VMEM_SPEC]
        + [HBM_SPEC] * len(weights),
        out_specs=(VMEM_SPEC,) * len(outs),
        scratch_shapes=[
            pltpu.VMEM(table.shape, F32),
            pltpu.SemaphoreType.DMA((3,)),
            pltpu.SemaphoreType.DMA((3 * len(weights),)),
        ],
        compiler_params=params(received, table, *outs),
        cost_estimate=takes(5),
        name="prepare",
    )(place, received, table, keep.reshape(1, -1), layer.reshape(1, -1), *in_hbm(*weights))


def start_copies(sources, places, targets, sems):
    copies = []
    for source, (index, to, at, rows) in zip(sources, places):
        parts = 3 if rows % 48 == 0 or rows % 3 == 0 and len(source.shape) > 2 else 1
        for n in range(parts):
            size = rows // parts
            copies.append(
                pltpu.make_async_copy(
                    source.at[pl.ds(at + n * size, size)],
                    targets[index].at[pl.ds(to + n * size, size)],
                    sems.at[len(copies)],
                )
            )
            copies[-1].start()
    return copies


def attention_rows(current, norm_ref, mask_ref, weights, out_ref):
    normed = [normalise(rows, norm_ref[0], norm_ref[1]).astype(BF16) for rows in current]
    normed = normed[0] if len(normed) == 1 else jnp.concatenate(normed, axis=0)
    qkv_me, qkv_other = weights
    share = qkv_me.shape[1]
    heads = share // HD
    block = mask_ref.shape[0]
    count = normed.shape[0] // block
    bias = mask_ref[...]
    lane = lax.broadcasted_iota(jnp.int32, (1, share), 1)
    head_lanes = [
        ((lane >= HD * h) & (lane < HD * (h + 1))).astype(jnp.int32).astype(F32).astype(BF16)
        for h in range(heads)
    ]
    scale = math.log2(math.e) / math.sqrt(HD)
    projected = []
    for side, qkv in enumerate((qkv_me, qkv_other)):
        projected.append(
            [
                lax.dot_general(
                    normed, qkv[t], (((1,), (1,)), ((), ())), preferred_element_type=F32
                ).astype(BF16)
                for t in range(3)
            ]
        )
    units = [(side, slice(b * block, (b + 1) * block)) for side in range(2) for b in range(count)]
    scores = []
    for side, at in units:
        query, key = projected[side][0][at], projected[side][1][at]
        keys = jnp.concatenate([key * lanes for lanes in head_lanes], axis=0)
        raw = lax.dot_general(query, keys, (((1,), (1,)), ((), ())), preferred_element_type=F32)
        scores += [
            raw[:, h * block : (h + 1) * block] + bias for h in range(heads)
        ]
    tops = [jnp.max(s, axis=-1, keepdims=True) for s in scores]
    weights_of = [jnp.exp2((s - t) * scale) for s, t in zip(scores, tops)]
    parts = [1.0 / jnp.sum(w, axis=-1, keepdims=True) for w in weights_of]
    shares = [(w * part).astype(BF16) for w, part in zip(weights_of, parts)]
    attended = []
    for n, (side, at) in enumerate(units):
        value = projected[side][2][at]
        values = jnp.concatenate([value * lanes for lanes in head_lanes], axis=0)
        row = jnp.concatenate(shares[n * heads : (n + 1) * heads], axis=1)
        attended.append(jnp.dot(row, values, preferred_element_type=F32).astype(BF16))
    sides = [attended[side * count : (side + 1) * count] for side in range(2)]
    sides = [x[0] if count == 1 else jnp.concatenate(x, axis=0) for x in sides]
    full, _ = tiles_of(share)
    tiles = [x[:, t * LANES : (t + 1) * LANES] for x in sides for t in range(full)]
    pack_half(out_ref, tiles, jnp.concatenate([x[:, full * LANES :] for x in sides], axis=1))


def shifted_in(rows, fresh_row):
    frames = rows.shape[0]
    first = lax.broadcasted_iota(jnp.int32, (frames, 1), 0) == 0
    return jnp.where(first, fresh_row, pltpu.roll(rows, 1, 0))


def first_attention_kernel(
    count, mine_ref, other_ref, flag_ref, norm_ref, mask_ref,
    qkv_me, qkv_other, cur_ref, part_ref, fresh_ref,
):
    groups, cores = mine_ref.shape[:2]
    frames = norm_ref.shape[1]
    here = frames // groups
    share = qkv_me.shape[1]
    first_half = flag_ref[0:1, :] > 0.5
    blocks = []
    for g in range(groups):
        left, right = [], []
        for c in range(cores):
            mine, other = mine_ref[g, c].astype(F32), other_ref[g, c].astype(F32)
            left.append(jnp.where(first_half, mine, other))
            right.append(jnp.where(first_half, other, mine))
        if g < count:
            cuts = [fresh_piece(block, count, here, share) for block in left + right]
            fresh_ref[g : g + 1, :] = jnp.concatenate(cuts, axis=1)
        blocks.append([chunk_rows(block, count, here, share) for block in left + right])
    current = []
    for p in range(count):
        rows = [jnp.concatenate([part[p] for part in parts], axis=1) for parts in blocks]
        rows = pltpu.roll(jnp.concatenate(rows, axis=0), 1, 0)
        cur_ref[p * frames : (p + 1) * frames, :] = rows.astype(BF16)
        current.append(rows)
    attention_rows(current, norm_ref, mask_ref, (qkv_me, qkv_other), part_ref)


def next_attention_kernel(
    count, old_ref, after_ref, mine_ref, other_ref, fresh_ref, norm_ref, gate_ref, pair_ref,
    mask_ref, qkv_me, qkv_other, cur_ref, part_ref,
):
    frames = norm_ref.shape[1]
    keep, layer = pair_ref[:, 0:1], pair_ref[:, 1:2]
    current = []
    for p in range(count):
        at = slice(p * frames, (p + 1) * frames)
        total = mine_ref[at, :].astype(F32) + other_ref[at, :].astype(F32)
        rows = keep * old_ref[at, :].astype(F32) + layer * (
            after_ref[at, :].astype(F32) + gate_ref[0] * total
        )
        rows = shifted_in(rows, fresh_ref[p : p + 1, :]).astype(BF16)
        cur_ref[at, :] = rows
        current.append(rows.astype(F32))
    attention_rows(current, norm_ref, mask_ref, (qkv_me, qkv_other), part_ref)


def attention_call(kernel, arrays, rows, features, fresh_count=0):
    outs = (
        jax.ShapeDtypeStruct((rows, features), BF16),
        jax.ShapeDtypeStruct((rows * features // 2 // LANES, LANES), BF16),
    )
    if fresh_count:
        outs += (jax.ShapeDtypeStruct((fresh_count, features), F32),)
    return pl.pallas_call(
        kernel,
        out_shape=outs,
        in_specs=[VMEM_SPEC] * len(arrays),
        out_specs=(VMEM_SPEC,) * len(outs),
        compiler_params=params(*arrays, *outs),
        name="attention",
    )(*arrays)


def pack_half(ref, tiles, tail):
    rows = tail.shape[0]
    for n, tile in enumerate(tiles):
        ref[n * rows : (n + 1) * rows, :] = tile
    ref[len(tiles) * rows :, :] = jnp.concatenate([tail[: rows // 2], tail[rows // 2 :]], axis=1)


def pick_half(first_half, value):
    middle = value.shape[1] // 2 // LANES
    tiles = []
    for t in range(middle):
        left, right = (value[:, n * LANES : (n + 1) * LANES] for n in (t, t + middle + 1))
        tiles.append(jnp.where(first_half, left, right))
    split = value[:, middle * LANES : (middle + 1) * LANES]
    cut = LANES // 2
    return tiles, jnp.where(first_half[:, :cut], split[:, :cut], split[:, cut:])


def unpack_half(ref, rows):
    count = ref.shape[0] // rows
    tail = ref[count * rows :, :]
    tail = jnp.concatenate([tail[:, : LANES // 2], tail[:, LANES // 2 :]], axis=0)
    tiles = [ref[n * rows : (n + 1) * rows, :] for n in range(count)]
    return jnp.concatenate(tiles, axis=1), tail


def gelu(x):
    scale = math.sqrt(2.0 / math.pi)
    half = 0.5 * x
    return half + half * jnp.tanh(x * (scale + (0.044715 * scale) * (x * x)))


def pieces_of(width, size):
    return [(s, min(size, width - s)) for s in range(0, width, size)]


def feed_kernel(
    halves, flag_ref, cur_ref, mine_ref, other_ref, mod_ref,
    out_all, fc1_me, fc1_other, fc2_me, fc2_other, *rest,
):
    outs, hidden_ref = (rest[:-2], rest[-2]) if halves else (rest[:-1], rest[-1])
    after_ref = outs[0]
    frames = mod_ref.shape[1]
    tokens = cur_ref.shape[0] // frames
    normed = []
    rows, half = cur_ref.shape[0], out_all.shape[0] // 2
    attention_total = None
    for n, ref in enumerate((mine_ref, other_ref)):
        main, tail = unpack_half(ref, rows)
        middle = n * half + main.shape[1]
        part = jnp.dot(main, out_all[n * half : middle], preferred_element_type=F32)
        part += jnp.dot(tail, out_all[middle : (n + 1) * half], preferred_element_type=F32)
        attention_total = part if n == 0 else attention_total + part
    for p in range(tokens):
        at = slice(p * frames, (p + 1) * frames)
        after = (cur_ref[at, :].astype(F32) + mod_ref[0] * attention_total[at]).astype(BF16)
        after_ref[at, :] = after
        normed.append(normalise(after.astype(F32), mod_ref[1], mod_ref[2]).astype(BF16))
    normed = normed[0] if tokens == 1 else jnp.concatenate(normed, axis=0)
    units, features = fc2_me.shape
    for side, w1 in enumerate((fc1_me, fc1_other)):
        for start, size in pieces_of(units, 256):
            hidden = gelu(
                jnp.dot(normed, w1[:, start : start + size], preferred_element_type=F32)
            )
            hidden_ref[:, side * units + start : side * units + start + size] = hidden.astype(BF16)

    def product(at):
        return jnp.dot(
            hidden_ref[:, :units], fc2_me[:, at], preferred_element_type=F32
        ) + jnp.dot(hidden_ref[:, units:], fc2_other[:, at], preferred_element_type=F32)

    target = rest[-1] if halves else outs[1]
    for start, size in pieces_of(features, 256):
        at = slice(start, start + size)
        target[:, at] = product(at).astype(BF16)
    if not halves:
        return
    first_half = flag_ref[0:1, :] > 0.5
    pack_half(outs[1], *pick_half(first_half, target[...]))
    pack_half(outs[2], *pick_half(jnp.logical_not(first_half), target[...]))


def feed_call(flag, cur, mine, other, mod, weights, halves):
    rows, features = cur.shape
    shape = jax.ShapeDtypeStruct((rows, features), BF16)
    packed = jax.ShapeDtypeStruct((rows * features // 2 // LANES, LANES), BF16)
    outs = (shape, packed, packed) if halves else (shape, shape)
    return pl.pallas_call(
        functools.partial(feed_kernel, halves),
        out_shape=outs,
        in_specs=[VMEM_SPEC] * 10,
        out_specs=(VMEM_SPEC,) * len(outs),
        scratch_shapes=[pltpu.VMEM((rows, 2 * weights[1].shape[1]), BF16)]
        + ([pltpu.VMEM((rows, features), BF16)] if halves else []),
        compiler_params=params(cur, mine, other, mod, *weights, *outs),
        name="feed",
    )(flag, cur, mine, other, mod, *weights)


def finish_kernel(chunks, flag_ref, gate_ref, pair_ref, *refs):
    out_ref = refs[-1]
    groups, cores = out_ref.shape[:2]
    _, frames, features = gate_ref.shape
    here = frames // groups
    half = features // 2
    share = half // cores
    full, rest = tiles_of(share)
    first_half = flag_ref[0:1, :] > 0.5
    keep, layer = pair_ref[:, 0:1], pair_ref[:, 1:2]
    gates = pick_half(first_half, gate_ref[0])
    gates = gates[0] + [gates[1]]
    results = []
    for n in range(chunks):
        old_ref, after_ref, mine_ref, other_ref = refs[4 * n : 4 * n + 4]
        rows = old_ref.shape[0]
        (mine, mine_tail), (theirs, their_tail) = (
            unpack_half(ref, rows) for ref in (mine_ref, other_ref)
        )
        main = mine.astype(F32) + theirs.astype(F32)
        main_tail = mine_tail.astype(F32) + their_tail.astype(F32)
        for p in range(rows // frames):
            at = slice(p * frames, (p + 1) * frames)
            old, after = (
                pick_half(first_half, ref[at, :].astype(F32)) for ref in (old_ref, after_ref)
            )
            old, after = old[0] + [old[1]], after[0] + [after[1]]
            total = [main[at, t * LANES : (t + 1) * LANES] for t in range(len(old) - 1)]
            total.append(main_tail[at])
            done = [
                keep * o + layer * (a + g * t) for o, a, g, t in zip(old, after, gates, total)
            ]
            left, right = jnp.concatenate(done, axis=1), jnp.concatenate(done[-1:] + done[:-1], axis=1)
            results.append(jnp.where(first_half[:, 0:1], left, right))
    unused = LANES - len(results) * rest
    for c in range(cores):
        shares = [r[:, c * share : (c + 1) * share] for r in results]
        for g in range(groups):
            rows = [s[g * here : (g + 1) * here] for s in shares]
            pieces = [r[:, t * LANES : (t + 1) * LANES] for t in range(full) for r in rows]
            tails = [r[:, full * LANES :] for r in rows]
            if unused:
                tails.append(jnp.zeros((here, unused), F32))
            pieces.append(jnp.concatenate(tails, axis=1))
            out_ref[g, c] = jnp.concatenate(pieces, axis=0).astype(BF16)


def finish(flag, gate, pair, parts, groups):
    _, frames, features = gate.shape
    tokens = sum(part[0].shape[0] for part in parts) // frames
    full, _ = tiles_of(features // 4)
    arrays = [array for part in parts for array in part]
    out = jax.ShapeDtypeStruct((groups, 2, (full * tokens + 1) * (frames // groups), LANES), BF16)
    return pl.pallas_call(
        functools.partial(finish_kernel, len(parts)),
        out_shape=out,
        in_specs=[VMEM_SPEC] * (3 + len(arrays)),
        out_specs=VMEM_SPEC,
        compiler_params=params(gate, pair, out, *arrays),
        cost_estimate=takes(0.8),
        name="finish",
    )(flag, gate, pair, *arrays)


def unpack_kernel(rows_ref, out_ref, wide_ref):
    here, tokens, share = out_ref.shape
    sources = rows_ref.shape[0]
    size = tokens // sources
    full, rest = tiles_of(share)
    for d in range(sources):
        block = rows_ref[d].astype(F32)
        first = d * size * here
        for t in range(full):
            wide_ref[t, first : first + size * here, :] = block[t * size * here : (t + 1) * size * here]
        tail = block[full * size * here :]
        for p in range(size):
            wide_ref[full, first + p * here : first + (p + 1) * here, :rest] = tail[
                :, p * rest : (p + 1) * rest
            ]
    for i in range(here):
        pieces = [wide_ref[t, pl.ds(i, tokens, stride=here), :] for t in range(full + 1)]
        out_ref[i] = jnp.concatenate(pieces, axis=1)[:, :share].astype(BF16)


def unpack(rows, here, tokens, share):
    full, _ = tiles_of(share)
    out = jax.ShapeDtypeStruct((here, tokens, share), BF16)
    scratch = jax.ShapeDtypeStruct((full + 1, tokens * here, LANES), F32)
    return pl.pallas_call(
        unpack_kernel,
        out_shape=out,
        in_specs=[VMEM_SPEC],
        out_specs=VMEM_SPEC,
        scratch_shapes=[pltpu.VMEM(scratch.shape, F32)],
        compiler_params=params(rows, out, scratch),
        cost_estimate=takes(0.9),
        name="unpack",
    )(rows)


SWAP = [(0, 1), (1, 0)]


def on_device(
    latents, fresh, noise_level, window_mask, mod_table, keep_coef, layer_coef,
    w_qkv, w_out, w_fc1, w_fc2,
):
    here, tokens_all, share = latents.shape
    features = mod_table.shape[2]
    groups = lax.axis_size("frame")
    frames = groups * here
    frame_index = lax.axis_index("frame")
    y_index, core_index = lax.axis_index("y"), lax.axis_index("core")
    place = (2 * y_index + core_index).astype(jnp.int32).reshape(1)
    group_tokens = tokens_all // groups
    split = group_tokens % 2 == 0
    tokens = group_tokens // 2 if split else group_tokens
    block = max(frames, LANES)
    chunk_count = 2 if tokens % 2 == 0 and tokens * frames // 2 % block == 0 else 1
    size = tokens // chunk_count
    rows = size * frames

    swap_core = functools.partial(lax.ppermute, axis_name="core", perm=SWAP)
    swap_y = functools.partial(lax.ppermute, axis_name="y", perm=SWAP)
    w_qkv = jnp.swapaxes(w_qkv, 1, 2)
    qkv_other = swap_core(w_qkv)
    out_far = swap_y(w_out)
    out_core, out_corner, fc2_other = swap_core(w_out), swap_core(out_far), swap_core(w_fc2)
    payload = make_payload(
        frame_index.astype(jnp.int32).reshape(1), noise_level, window_mask, latents, fresh,
        frames, tokens_all // tokens, chunk_count,
    )
    if split:
        received = lax.all_to_all(payload, ("frame", "core"), 0, 0, tiled=True)
        received = received.reshape((groups, 2) + received.shape[1:])
    else:
        received = lax.all_to_all(payload, "frame", 0, 0, tiled=True)
        partner = swap_core(received)
        first = core_index == 0
        received = jnp.stack(
            [jnp.where(first, received, partner), jnp.where(first, partner, received)], axis=1
        )
    received, qkv_other, out_core, out_far, fc2_other = lax.optimization_barrier(
        (received, qkv_other, out_core, out_far, fc2_other)
    )
    full, rest = tiles_of(share)
    arrived = [received[:, :, n] for n in range(chunk_count)]
    arrived_other = [swap_y(part) for part in arrived]
    weights = [qkv_other]
    places = [(0, 0, 0, w_qkv.shape[0])]
    for n in range(2):
        first, second = ((w_out, out_core), (out_far, out_corner))[n]
        weights += [first, second, first, second]
        to = 2 * n * share
        places += [(1, to, 0, full * LANES), (1, to + full * LANES, 0, full * LANES)]
        to += 2 * full * LANES
        places += [(1, to, full * LANES, rest), (1, to + rest, full * LANES, rest)]
    weights.append(fc2_other)
    places.append((2, 0, 0, w_fc2.shape[0]))
    held = (w_qkv.shape, (4 * share, features), w_fc2.shape)
    norm_mod, feed_mod, gate_mod, pair, mask, flag, qkv_other, out_all, fc2_other = prepare(
        place, arrived[0], jnp.swapaxes(mod_table, 0, 1), keep_coef, layer_coef,
        weights, places, held, here, size * rest, block,
    )
    attention_weights = (w_qkv, qkv_other)

    state = []
    for n in range(chunk_count):
        results = attention_call(
            functools.partial(first_attention_kernel, size),
            (arrived[n], arrived_other[n], flag, norm_mod, mask) + attention_weights,
            rows, features, size,
        )
        current, part, later = results
        state.append((current, part, swap_y(part), later))
    feed_weights = (out_all, w_fc1, swap_core(w_fc1), w_fc2, fc2_other)
    fed = []
    for current, part, part_other, later in state:
        after, feed = feed_call(flag, current, part, part_other, feed_mod, feed_weights, False)
        fed.append((current, after, feed, swap_y(feed), later))
    state = []
    for arrays in fed:
        current, part = attention_call(
            functools.partial(next_attention_kernel, size),
            arrays + (norm_mod, gate_mod, pair, mask) + attention_weights,
            rows, features,
        )
        state.append((current, part, swap_y(part)))
    parts = []
    for current, part, part_other in state:
        after, feed_here, feed_there = feed_call(
            flag, current, part, part_other, feed_mod, feed_weights, True
        )
        parts.append((current, after, feed_here, swap_y(feed_there)))
    result = finish(flag, gate_mod, pair, parts, groups)
    if split:
        result = result.reshape((groups * 2,) + result.shape[2:])
        result = lax.all_to_all(result, ("frame", "core"), 0, 0, tiled=True)
    else:
        result = jnp.where(core_index == 0, result[:, 0], result[:, 1])
        result = lax.all_to_all(result, "frame", 0, 0, tiled=True)
    return unpack(result, here, tokens_all, share)


def solution(mesh):
    groups, heads = mesh.shape["frame"], mesh.shape["head"]
    inner = Mesh(mesh.devices.reshape(groups, heads // 2, 2), ("frame", "y", "core"))
    head = ("y", "core")
    in_specs = (
        P("frame", None, head),
        P(None, None, head),
        P("frame"),
        P("frame", None),
        P(),
        P(),
        P(),
        P(None, None, head),
        P(head, None),
        P(None, head),
        P(head, None),
    )
    return jax.shard_map(
        on_device, mesh=inner, in_specs=in_specs, out_specs=P("frame", None, head), check_vma=False
    )
```

```python
import functools
import math

import jax
import jax.numpy as jnp
from jax import lax
from jax.experimental import pallas as pl
from jax.experimental.pallas import tpu as pltpu
from jax.sharding import Mesh, PartitionSpec as P

HD = 72
W = 8
OFFSETS = 2 * W + 1
EPSILON = 1e-06
F32 = jnp.float32
BF16 = jnp.bfloat16
LANES = 128
VMEM_SPEC = pl.BlockSpec(memory_space=pltpu.VMEM)
SMEM_SPEC = pl.BlockSpec(memory_space=pltpu.SMEM)
HBM_SPEC = pl.BlockSpec(memory_space=pltpu.HBM)


def in_hbm(*arrays):
    return [pltpu.with_memory_space_constraint(array, pltpu.HBM) for array in arrays]


def params(*arrays):
    held = sum(math.prod(a.shape) * jnp.dtype(a.dtype).itemsize for a in arrays)
    return pltpu.CompilerParams(vmem_limit_bytes=held + 8 * 1024 * 1024)


def takes(microseconds):
    return pl.CostEstimate(
        flops=0, bytes_accessed=int(microseconds * 3.3e6), transcendentals=0
    )


def tiles_of(share):
    return share // LANES, share % LANES


def normalise(values, shift_rows, scale_rows):
    center = values - jnp.mean(values, axis=-1, keepdims=True)
    spread = jnp.mean(center * center, axis=-1, keepdims=True)
    return center * lax.rsqrt(spread + EPSILON) * (1.0 + scale_rows) + shift_rows


def payload_kernel(
    frames, x_ref, frame_far, level_far, window_far, fresh_far, out_ref,
    rows_ref, frame_ref, level_ref, window_ref, fresh_ref, sems,
):
    fars = (window_far, level_far, frame_far, fresh_far)
    nears = (window_ref, level_ref, frame_ref, fresh_ref)
    copies = [pltpu.make_async_copy(a, b, sems.at[n]) for n, (a, b) in enumerate(zip(fars, nears))]
    for copy in copies:
        copy.start()
    for copy in copies:
        copy.wait()
    here, _, share = x_ref.shape
    targets, chunks, _, _ = out_ref.shape
    full, rest = tiles_of(share)
    size = x_ref.shape[1] // (targets * chunks)
    row = lax.broadcasted_iota(jnp.int32, (here, 1), 0)
    level = jnp.zeros((here, 1), jnp.int32)
    for i in range(here):
        level = jnp.where(row == i, level_ref[i], level)
    offset = lax.broadcasted_iota(jnp.int32, (here, OFFSETS), 1)
    position = frame_ref[0] * here + row + offset - W
    allowed = (window_ref[...] == 1) & (position >= 0) & (position < frames)
    meta = jnp.concatenate([level.astype(F32), allowed.astype(jnp.int32).astype(F32)], axis=1)
    tokens = x_ref.shape[1]
    piece = share // here
    blank = LANES - size * rest - 1 - OFFSETS - piece
    later = fresh_ref[1].astype(F32)
    for j in range(here):
        cut = later[:, j * piece : (j + 1) * piece]
        cut = jnp.concatenate([cut, jnp.zeros((tokens, LANES - piece), F32)], axis=1)
        rows_ref[full + 1, pl.ds(j, tokens, stride=here), :] = cut
    sent = lax.rem(frame_ref[0], size)
    for i in range(here):
        value = x_ref[i].astype(F32)
        if i == here - 1:
            leaves = (frame_ref[0] + 1) * here == frames
            value = jnp.where(leaves, fresh_ref[0].astype(F32), value)
        for t in range(full):
            rows_ref[t, pl.ds(i, tokens, stride=here), :] = value[:, t * LANES : (t + 1) * LANES]
        rows_ref[full, pl.ds(i, tokens, stride=here), :] = jnp.concatenate(
            [value[:, full * LANES :], jnp.zeros((tokens, LANES - rest), F32)], axis=1
        )
    for d in range(targets):
        for n in range(chunks):
            first = (d * chunks + n) * size * here
            pieces = [rows_ref[t, first : first + size * here, :] for t in range(full)]
            tails = [
                rows_ref[full, first + p * here : first + (p + 1) * here, :][:, :rest]
                for p in range(size)
            ]
            cuts = [
                rows_ref[full + 1, first + p * here : first + (p + 1) * here, :][:, :piece]
                for p in range(size)
            ]
            cut = cuts[0]
            for p in range(1, size):
                cut = jnp.where(sent == p, cuts[p], cut)
            tails += [meta, cut]
            if blank:
                tails.append(jnp.zeros((here, blank), F32))
            pieces.append(jnp.concatenate(tails, axis=1))
            out_ref[d, n] = jnp.concatenate(pieces, axis=0).astype(BF16)


def make_payload(frame_index, noise_level, window_mask, x, fresh, frames, targets, chunks):
    here, tokens, share = x.shape
    full, rest = tiles_of(share)
    size = tokens // (targets * chunks)
    out = jax.ShapeDtypeStruct((targets, chunks, (full * size + 1) * here, LANES), BF16)
    scratch = jax.ShapeDtypeStruct((full + 2, tokens * here, LANES), F32)
    return pl.pallas_call(
        functools.partial(payload_kernel, frames),
        out_shape=out,
        in_specs=[VMEM_SPEC] + [HBM_SPEC] * 4,
        out_specs=VMEM_SPEC,
        scratch_shapes=[
            pltpu.VMEM(scratch.shape, F32),
            pltpu.SMEM(frame_index.shape, jnp.int32),
            pltpu.SMEM(noise_level.shape, jnp.int32),
            pltpu.VMEM(window_mask.shape, jnp.int32),
            pltpu.VMEM(fresh.shape, BF16),
            pltpu.SemaphoreType.DMA((4,)),
        ],
        compiler_params=params(x, fresh, out, scratch),
        cost_estimate=takes(2),
        name="payload",
    )(x, *in_hbm(frame_index, noise_level, window_mask, fresh))


def fresh_piece(block, size, here, share):
    _, rest = tiles_of(share)
    piece = share // here
    first = size * rest + 1 + OFFSETS
    tail = block[-here:, first : first + piece]
    return jnp.concatenate([tail[j : j + 1] for j in range(here)], axis=1)


def chunk_rows(block, size, here, share):
    full, rest = tiles_of(share)
    tail = block[full * size * here :]
    result = []
    for p in range(size):
        pieces = [block[(t * size + p) * here : (t * size + p + 1) * here] for t in range(full)]
        result.append(jnp.concatenate(pieces + [tail[:, p * rest : (p + 1) * rest]], axis=1))
    return result


def prepare_kernel(
    here, lane_at, places, place_ref, received_ref, table_far, keep_ref, layer_ref, *refs
):
    sources, refs = refs[: len(places)], refs[len(places) :]
    norm_ref, feed_ref, gate_ref, pair_ref, mask_ref, flag_ref = refs[:6]
    held, (table_ref, table_sems, sems) = refs[6:-3], refs[-3:]
    table_copies = start_copies(
        (table_far,), [(0, 0, 0, table_far.shape[0])], (table_ref,), table_sems
    )
    copies = start_copies(sources, places, held, sems)
    flag_ref[...] = jnp.where(place_ref[0] < 2, jnp.ones_like(flag_ref), 0.0)
    groups = received_ref.shape[0]
    frames = groups * here
    levels = table_ref.shape[1]
    meta = [received_ref[g, 0].astype(F32)[-here:, lane_at:] for g in range(groups)]
    meta = jnp.concatenate(meta, axis=0)
    level = meta[:, 0:1]
    ids = lax.broadcasted_iota(jnp.int32, (frames, levels), 1).astype(F32)
    hot = level == ids
    hot_bf = hot.astype(BF16)
    for copy in table_copies:
        copy.wait()
    targets = [(norm_ref, 0), (norm_ref, 1), (feed_ref, 0), (feed_ref, 1), (feed_ref, 2), (gate_ref, 0)]
    for j, (target, at) in enumerate(targets):
        rows = table_ref[j]
        high = rows.astype(BF16)
        rest = rows - high.astype(F32)
        middle = rest.astype(BF16)
        low = (rest - middle.astype(F32)).astype(BF16)
        total = jnp.dot(hot_bf, high, preferred_element_type=F32)
        total += jnp.dot(hot_bf, middle, preferred_element_type=F32)
        total += jnp.dot(hot_bf, low, preferred_element_type=F32)
        target[at] = total
    keep = jnp.sum(jnp.where(hot, keep_ref[...], 0.0), axis=1, keepdims=True)
    layer = jnp.sum(jnp.where(hot, layer_ref[...], 0.0), axis=1, keepdims=True)
    lane = lax.broadcasted_iota(jnp.int32, (frames, LANES), 1)
    pair_ref[...] = jnp.where(lane == 0, keep, layer)

    block = mask_ref.shape[0]
    row = lax.broadcasted_iota(jnp.int32, (frames, block), 0)
    column = lax.broadcasted_iota(jnp.int32, (frames, block), 1)
    for t in range(block // frames):
        distance = column - t * frames - row
        inside = (column >= t * frames) & (column < (t + 1) * frames)
        is_open = jnp.zeros((frames, block), F32)
        for o in range(OFFSETS):
            is_open = jnp.where(distance == o - W, meta[:, 1 + o : 2 + o], is_open)
        is_open = jnp.where(inside, is_open, 0.0)
        mask_ref[t * frames : (t + 1) * frames, :] = jnp.where(is_open > 0.5, 0.0, -1e30)
    for copy in copies:
        copy.wait()


def prepare(place, received, table, keep, layer, weights, places, held, here, lane_at, block):
    frames = received.shape[0] * here
    features = table.shape[2]
    outs = (
        jax.ShapeDtypeStruct((2, frames, features), F32),
        jax.ShapeDtypeStruct((3, frames, features), F32),
        jax.ShapeDtypeStruct((1, frames, features), F32),
        jax.ShapeDtypeStruct((frames, LANES), F32),
        jax.ShapeDtypeStruct((block, block), F32),
        jax.ShapeDtypeStruct((8, LANES), F32),
    ) + tuple(jax.ShapeDtypeStruct(shape, BF16) for shape in held)
    (table,) = in_hbm(table)
    return pl.pallas_call(
        functools.partial(prepare_kernel, here, lane_at, tuple(places)),
        out_shape=outs,
        in_specs=[SMEM_SPEC, VMEM_SPEC, HBM_SPEC, VMEM_SPEC, VMEM_SPEC]
        + [HBM_SPEC] * len(weights),
        out_specs=(VMEM_SPEC,) * len(outs),
        scratch_shapes=[
            pltpu.VMEM(table.shape, F32),
            pltpu.SemaphoreType.DMA((3,)),
            pltpu.SemaphoreType.DMA((3 * len(weights),)),
        ],
        compiler_params=params(received, table, *outs),
        cost_estimate=takes(5),
        name="prepare",
    )(place, received, table, keep.reshape(1, -1), layer.reshape(1, -1), *in_hbm(*weights))


def start_copies(sources, places, targets, sems):
    copies = []
    for source, (index, to, at, rows) in zip(sources, places):
        parts = 3 if rows % 48 == 0 or rows % 3 == 0 and len(source.shape) > 2 else 1
        for n in range(parts):
            size = rows // parts
            copies.append(
                pltpu.make_async_copy(
                    source.at[pl.ds(at + n * size, size)],
                    targets[index].at[pl.ds(to + n * size, size)],
                    sems.at[len(copies)],
                )
            )
            copies[-1].start()
    return copies


def attention_rows(current, norm_ref, mask_ref, weights, out_ref):
    normed = [normalise(rows, norm_ref[0], norm_ref[1]).astype(BF16) for rows in current]
    normed = normed[0] if len(normed) == 1 else jnp.concatenate(normed, axis=0)
    qkv_me, qkv_other = weights
    share = qkv_me.shape[1]
    heads = share // HD
    block = mask_ref.shape[0]
    count = normed.shape[0] // block
    bias = mask_ref[...]
    lane = lax.broadcasted_iota(jnp.int32, (1, share), 1)
    head_lanes = [
        ((lane >= HD * h) & (lane < HD * (h + 1))).astype(jnp.int32).astype(F32).astype(BF16)
        for h in range(heads)
    ]
    scale = math.log2(math.e) / math.sqrt(HD)
    projected = []
    for side, qkv in enumerate((qkv_me, qkv_other)):
        projected.append(
            [
                lax.dot_general(
                    normed, qkv[t], (((1,), (1,)), ((), ())), preferred_element_type=F32
                ).astype(BF16)
                for t in range(3)
            ]
        )
    units = [(side, slice(b * block, (b + 1) * block)) for side in range(2) for b in range(count)]
    scores = []
    for side, at in units:
        query, key = projected[side][0][at], projected[side][1][at]
        keys = jnp.concatenate([key * lanes for lanes in head_lanes], axis=0)
        raw = lax.dot_general(query, keys, (((1,), (1,)), ((), ())), preferred_element_type=F32)
        scores += [
            raw[:, h * block : (h + 1) * block] + bias for h in range(heads)
        ]
    tops = [jnp.max(s, axis=-1, keepdims=True) for s in scores]
    weights_of = [jnp.exp2((s - t) * scale) for s, t in zip(scores, tops)]
    parts = [1.0 / jnp.sum(w, axis=-1, keepdims=True) for w in weights_of]
    shares = [(w * part).astype(BF16) for w, part in zip(weights_of, parts)]
    attended = []
    for n, (side, at) in enumerate(units):
        value = projected[side][2][at]
        values = jnp.concatenate([value * lanes for lanes in head_lanes], axis=0)
        row = jnp.concatenate(shares[n * heads : (n + 1) * heads], axis=1)
        attended.append(jnp.dot(row, values, preferred_element_type=F32).astype(BF16))
    sides = [attended[side * count : (side + 1) * count] for side in range(2)]
    sides = [x[0] if count == 1 else jnp.concatenate(x, axis=0) for x in sides]
    full, _ = tiles_of(share)
    tiles = [x[:, t * LANES : (t + 1) * LANES] for x in sides for t in range(full)]
    pack_half(out_ref, tiles, jnp.concatenate([x[:, full * LANES :] for x in sides], axis=1))


def shifted_in(rows, fresh_row):
    frames = rows.shape[0]
    first = lax.broadcasted_iota(jnp.int32, (frames, 1), 0) == 0
    return jnp.where(first, fresh_row, pltpu.roll(rows, 1, 0))


def first_attention_kernel(
    count, mine_ref, other_ref, flag_ref, norm_ref, mask_ref,
    qkv_me, qkv_other, cur_ref, part_ref, fresh_ref,
):
    groups, cores = mine_ref.shape[:2]
    frames = norm_ref.shape[1]
    here = frames // groups
    share = qkv_me.shape[1]
    first_half = flag_ref[0:1, :] > 0.5
    blocks = []
    for g in range(groups):
        left, right = [], []
        for c in range(cores):
            mine, other = mine_ref[g, c].astype(F32), other_ref[g, c].astype(F32)
            left.append(jnp.where(first_half, mine, other))
            right.append(jnp.where(first_half, other, mine))
        if g < count:
            cuts = [fresh_piece(block, count, here, share) for block in left + right]
            fresh_ref[g : g + 1, :] = jnp.concatenate(cuts, axis=1)
        blocks.append([chunk_rows(block, count, here, share) for block in left + right])
    current = []
    for p in range(count):
        rows = [jnp.concatenate([part[p] for part in parts], axis=1) for parts in blocks]
        rows = pltpu.roll(jnp.concatenate(rows, axis=0), 1, 0)
        cur_ref[p * frames : (p + 1) * frames, :] = rows.astype(BF16)
        current.append(rows)
    attention_rows(current, norm_ref, mask_ref, (qkv_me, qkv_other), part_ref)


def next_attention_kernel(
    count, old_ref, after_ref, mine_ref, other_ref, fresh_ref, norm_ref, gate_ref, pair_ref,
    mask_ref, qkv_me, qkv_other, cur_ref, part_ref,
):
    frames = norm_ref.shape[1]
    keep, layer = pair_ref[:, 0:1], pair_ref[:, 1:2]
    current = []
    for p in range(count):
        at = slice(p * frames, (p + 1) * frames)
        total = mine_ref[at, :].astype(F32) + other_ref[at, :].astype(F32)
        rows = keep * old_ref[at, :].astype(F32) + layer * (
            after_ref[at, :].astype(F32) + gate_ref[0] * total
        )
        rows = shifted_in(rows, fresh_ref[p : p + 1, :]).astype(BF16)
        cur_ref[at, :] = rows
        current.append(rows.astype(F32))
    attention_rows(current, norm_ref, mask_ref, (qkv_me, qkv_other), part_ref)


def attention_call(kernel, arrays, rows, features, fresh_count=0):
    outs = (
        jax.ShapeDtypeStruct((rows, features), BF16),
        jax.ShapeDtypeStruct((rows * features // 2 // LANES, LANES), BF16),
    )
    if fresh_count:
        outs += (jax.ShapeDtypeStruct((fresh_count, features), F32),)
    return pl.pallas_call(
        kernel,
        out_shape=outs,
        in_specs=[VMEM_SPEC] * len(arrays),
        out_specs=(VMEM_SPEC,) * len(outs),
        compiler_params=params(*arrays, *outs),
        name="attention",
    )(*arrays)


def pack_half(ref, tiles, tail):
    rows = tail.shape[0]
    for n, tile in enumerate(tiles):
        ref[n * rows : (n + 1) * rows, :] = tile
    ref[len(tiles) * rows :, :] = jnp.concatenate([tail[: rows // 2], tail[rows // 2 :]], axis=1)


def pick_half(first_half, value):
    middle = value.shape[1] // 2 // LANES
    tiles = []
    for t in range(middle):
        left, right = (value[:, n * LANES : (n + 1) * LANES] for n in (t, t + middle + 1))
        tiles.append(jnp.where(first_half, left, right))
    split = value[:, middle * LANES : (middle + 1) * LANES]
    cut = LANES // 2
    return tiles, jnp.where(first_half[:, :cut], split[:, :cut], split[:, cut:])


def unpack_half(ref, rows):
    count = ref.shape[0] // rows
    tail = ref[count * rows :, :]
    tail = jnp.concatenate([tail[:, : LANES // 2], tail[:, LANES // 2 :]], axis=0)
    tiles = [ref[n * rows : (n + 1) * rows, :] for n in range(count)]
    return jnp.concatenate(tiles, axis=1), tail


def gelu(x):
    scale = math.sqrt(2.0 / math.pi)
    half = 0.5 * x
    return half + half * jnp.tanh(x * (scale + (0.044715 * scale) * (x * x)))


def pieces_of(width, size):
    return [(s, min(size, width - s)) for s in range(0, width, size)]


def feed_kernel(
    halves, flag_ref, cur_ref, mine_ref, other_ref, mod_ref,
    out_all, fc1_me, fc1_other, fc2_me, fc2_other, *rest,
):
    outs, hidden_ref = (rest[:-2], rest[-2]) if halves else (rest[:-1], rest[-1])
    after_ref = outs[0]
    frames = mod_ref.shape[1]
    tokens = cur_ref.shape[0] // frames
    normed = []
    rows = cur_ref.shape[0]
    both = [unpack_half(ref, rows) for ref in (mine_ref, other_ref)]
    main = jnp.concatenate([tiles for tiles, _ in both], axis=1)
    tail = jnp.concatenate([rest_of for _, rest_of in both], axis=1)
    attention_total = jnp.dot(
        main, out_all[: main.shape[1]], preferred_element_type=F32
    ) + jnp.dot(tail, out_all[main.shape[1] :], preferred_element_type=F32)
    for p in range(tokens):
        at = slice(p * frames, (p + 1) * frames)
        after = (cur_ref[at, :].astype(F32) + mod_ref[0] * attention_total[at]).astype(BF16)
        after_ref[at, :] = after
        normed.append(normalise(after.astype(F32), mod_ref[1], mod_ref[2]).astype(BF16))
    normed = normed[0] if tokens == 1 else jnp.concatenate(normed, axis=0)
    units, features = fc2_me.shape
    for side, w1 in enumerate((fc1_me, fc1_other)):
        for start, size in pieces_of(units, 256):
            hidden = gelu(
                jnp.dot(normed, w1[:, start : start + size], preferred_element_type=F32)
            )
            hidden_ref[:, side * units + start : side * units + start + size] = hidden.astype(BF16)

    def product(at):
        return jnp.dot(
            hidden_ref[:, :units], fc2_me[:, at], preferred_element_type=F32
        ) + jnp.dot(hidden_ref[:, units:], fc2_other[:, at], preferred_element_type=F32)

    target = rest[-1] if halves else outs[1]
    for start, size in pieces_of(features, 256):
        at = slice(start, start + size)
        target[:, at] = product(at).astype(BF16)
    if not halves:
        return
    first_half = flag_ref[0:1, :] > 0.5
    pack_half(outs[1], *pick_half(first_half, target[...]))
    pack_half(outs[2], *pick_half(jnp.logical_not(first_half), target[...]))


def feed_call(flag, cur, mine, other, mod, weights, halves):
    rows, features = cur.shape
    shape = jax.ShapeDtypeStruct((rows, features), BF16)
    packed = jax.ShapeDtypeStruct((rows * features // 2 // LANES, LANES), BF16)
    outs = (shape, packed, packed) if halves else (shape, shape)
    return pl.pallas_call(
        functools.partial(feed_kernel, halves),
        out_shape=outs,
        in_specs=[VMEM_SPEC] * 10,
        out_specs=(VMEM_SPEC,) * len(outs),
        scratch_shapes=[pltpu.VMEM((rows, 2 * weights[1].shape[1]), BF16)]
        + ([pltpu.VMEM((rows, features), BF16)] if halves else []),
        compiler_params=params(cur, mine, other, mod, *weights, *outs),
        name="feed",
    )(flag, cur, mine, other, mod, *weights)


def finish_kernel(chunks, flag_ref, gate_ref, pair_ref, *refs):
    out_ref = refs[-1]
    groups, cores = out_ref.shape[:2]
    _, frames, features = gate_ref.shape
    here = frames // groups
    half = features // 2
    share = half // cores
    full, rest = tiles_of(share)
    first_half = flag_ref[0:1, :] > 0.5
    keep, layer = pair_ref[:, 0:1], pair_ref[:, 1:2]
    gates = pick_half(first_half, gate_ref[0])
    gates = gates[0] + [gates[1]]
    results = []
    for n in range(chunks):
        old_ref, after_ref, mine_ref, other_ref = refs[4 * n : 4 * n + 4]
        rows = old_ref.shape[0]
        (mine, mine_tail), (theirs, their_tail) = (
            unpack_half(ref, rows) for ref in (mine_ref, other_ref)
        )
        main = mine.astype(F32) + theirs.astype(F32)
        main_tail = mine_tail.astype(F32) + their_tail.astype(F32)
        for p in range(rows // frames):
            at = slice(p * frames, (p + 1) * frames)
            old, after = (
                pick_half(first_half, ref[at, :].astype(F32)) for ref in (old_ref, after_ref)
            )
            old, after = old[0] + [old[1]], after[0] + [after[1]]
            total = [main[at, t * LANES : (t + 1) * LANES] for t in range(len(old) - 1)]
            total.append(main_tail[at])
            done = [
                keep * o + layer * (a + g * t) for o, a, g, t in zip(old, after, gates, total)
            ]
            left, right = jnp.concatenate(done, axis=1), jnp.concatenate(done[-1:] + done[:-1], axis=1)
            results.append(jnp.where(first_half[:, 0:1], left, right))
    unused = LANES - len(results) * rest
    for c in range(cores):
        shares = [r[:, c * share : (c + 1) * share] for r in results]
        for g in range(groups):
            rows = [s[g * here : (g + 1) * here] for s in shares]
            pieces = [r[:, t * LANES : (t + 1) * LANES] for t in range(full) for r in rows]
            tails = [r[:, full * LANES :] for r in rows]
            if unused:
                tails.append(jnp.zeros((here, unused), F32))
            pieces.append(jnp.concatenate(tails, axis=1))
            out_ref[g, c] = jnp.concatenate(pieces, axis=0).astype(BF16)


def finish(flag, gate, pair, parts, groups):
    _, frames, features = gate.shape
    tokens = sum(part[0].shape[0] for part in parts) // frames
    full, _ = tiles_of(features // 4)
    arrays = [array for part in parts for array in part]
    out = jax.ShapeDtypeStruct((groups, 2, (full * tokens + 1) * (frames // groups), LANES), BF16)
    return pl.pallas_call(
        functools.partial(finish_kernel, len(parts)),
        out_shape=out,
        in_specs=[VMEM_SPEC] * (3 + len(arrays)),
        out_specs=VMEM_SPEC,
        compiler_params=params(gate, pair, out, *arrays),
        cost_estimate=takes(0.8),
        name="finish",
    )(flag, gate, pair, *arrays)


def unpack_kernel(rows_ref, out_ref, wide_ref):
    here, tokens, share = out_ref.shape
    sources = rows_ref.shape[0]
    size = tokens // sources
    full, rest = tiles_of(share)
    for d in range(sources):
        block = rows_ref[d].astype(F32)
        first = d * size * here
        for t in range(full):
            wide_ref[t, first : first + size * here, :] = block[t * size * here : (t + 1) * size * here]
        tail = block[full * size * here :]
        for p in range(size):
            wide_ref[full, first + p * here : first + (p + 1) * here, :rest] = tail[
                :, p * rest : (p + 1) * rest
            ]
    for i in range(here):
        pieces = [wide_ref[t, pl.ds(i, tokens, stride=here), :] for t in range(full + 1)]
        out_ref[i] = jnp.concatenate(pieces, axis=1)[:, :share].astype(BF16)


def unpack(rows, here, tokens, share):
    full, _ = tiles_of(share)
    out = jax.ShapeDtypeStruct((here, tokens, share), BF16)
    scratch = jax.ShapeDtypeStruct((full + 1, tokens * here, LANES), F32)
    return pl.pallas_call(
        unpack_kernel,
        out_shape=out,
        in_specs=[VMEM_SPEC],
        out_specs=VMEM_SPEC,
        scratch_shapes=[pltpu.VMEM(scratch.shape, F32)],
        compiler_params=params(rows, out, scratch),
        cost_estimate=takes(0.9),
        name="unpack",
    )(rows)


SWAP = [(0, 1), (1, 0)]


def on_device(
    latents, fresh, noise_level, window_mask, mod_table, keep_coef, layer_coef,
    w_qkv, w_out, w_fc1, w_fc2,
):
    here, tokens_all, share = latents.shape
    features = mod_table.shape[2]
    groups = lax.axis_size("frame")
    frames = groups * here
    frame_index = lax.axis_index("frame")
    y_index, core_index = lax.axis_index("y"), lax.axis_index("core")
    place = (2 * y_index + core_index).astype(jnp.int32).reshape(1)
    group_tokens = tokens_all // groups
    split = group_tokens % 2 == 0
    tokens = group_tokens // 2 if split else group_tokens
    block = max(frames, LANES)
    chunk_count = 2 if tokens % 2 == 0 and tokens * frames // 2 % block == 0 else 1
    size = tokens // chunk_count
    rows = size * frames

    swap_core = functools.partial(lax.ppermute, axis_name="core", perm=SWAP)
    swap_y = functools.partial(lax.ppermute, axis_name="y", perm=SWAP)
    w_qkv = jnp.swapaxes(w_qkv, 1, 2)
    qkv_other = swap_core(w_qkv)
    out_far = swap_y(w_out)
    out_core, out_corner, fc2_other = swap_core(w_out), swap_core(out_far), swap_core(w_fc2)
    payload = make_payload(
        frame_index.astype(jnp.int32).reshape(1), noise_level, window_mask, latents, fresh,
        frames, tokens_all // tokens, chunk_count,
    )
    if split:
        received = lax.all_to_all(payload, ("frame", "core"), 0, 0, tiled=True)
        received = received.reshape((groups, 2) + received.shape[1:])
    else:
        received = lax.all_to_all(payload, "frame", 0, 0, tiled=True)
        partner = swap_core(received)
        first = core_index == 0
        received = jnp.stack(
            [jnp.where(first, received, partner), jnp.where(first, partner, received)], axis=1
        )
    received, qkv_other, out_core, out_far, fc2_other = lax.optimization_barrier(
        (received, qkv_other, out_core, out_far, fc2_other)
    )
    full, rest = tiles_of(share)
    arrived = [received[:, :, n] for n in range(chunk_count)]
    arrived_other = [swap_y(part) for part in arrived]
    weights = [qkv_other]
    places = [(0, 0, 0, w_qkv.shape[0])]
    for n in range(2):
        first, second = ((w_out, out_core), (out_far, out_corner))[n]
        weights += [first, second, first, second]
        to = 2 * n * full * LANES
        places += [(1, to, 0, full * LANES), (1, to + full * LANES, 0, full * LANES)]
        to = 4 * full * LANES + 2 * n * rest
        places += [(1, to, full * LANES, rest), (1, to + rest, full * LANES, rest)]
    weights.append(fc2_other)
    places.append((2, 0, 0, w_fc2.shape[0]))
    held = (w_qkv.shape, (4 * share, features), w_fc2.shape)
    norm_mod, feed_mod, gate_mod, pair, mask, flag, qkv_other, out_all, fc2_other = prepare(
        place, arrived[0], jnp.swapaxes(mod_table, 0, 1), keep_coef, layer_coef,
        weights, places, held, here, size * rest, block,
    )
    attention_weights = (w_qkv, qkv_other)

    state = []
    for n in range(chunk_count):
        results = attention_call(
            functools.partial(first_attention_kernel, size),
            (arrived[n], arrived_other[n], flag, norm_mod, mask) + attention_weights,
            rows, features, size,
        )
        current, part, later = results
        state.append((current, part, swap_y(part), later))
    feed_weights = (out_all, w_fc1, swap_core(w_fc1), w_fc2, fc2_other)
    fed = []
    for current, part, part_other, later in state:
        after, feed = feed_call(flag, current, part, part_other, feed_mod, feed_weights, False)
        fed.append((current, after, feed, swap_y(feed), later))
    state = []
    for arrays in fed:
        current, part = attention_call(
            functools.partial(next_attention_kernel, size),
            arrays + (norm_mod, gate_mod, pair, mask) + attention_weights,
            rows, features,
        )
        state.append((current, part, swap_y(part)))
    parts = []
    for current, part, part_other in state:
        after, feed_here, feed_there = feed_call(
            flag, current, part, part_other, feed_mod, feed_weights, True
        )
        parts.append((current, after, feed_here, swap_y(feed_there)))
    result = finish(flag, gate_mod, pair, parts, groups)
    if split:
        result = result.reshape((groups * 2,) + result.shape[2:])
        result = lax.all_to_all(result, ("frame", "core"), 0, 0, tiled=True)
    else:
        result = jnp.where(core_index == 0, result[:, 0], result[:, 1])
        result = lax.all_to_all(result, "frame", 0, 0, tiled=True)
    return unpack(result, here, tokens_all, share)


def solution(mesh):
    groups, heads = mesh.shape["frame"], mesh.shape["head"]
    inner = Mesh(mesh.devices.reshape(groups, heads // 2, 2), ("frame", "y", "core"))
    head = ("y", "core")
    in_specs = (
        P("frame", None, head),
        P(None, None, head),
        P("frame"),
        P("frame", None),
        P(),
        P(),
        P(),
        P(None, None, head),
        P(head, None),
        P(None, head),
        P(head, None),
    )
    return jax.shard_map(
        on_device, mesh=inner, in_specs=in_specs, out_specs=P("frame", None, head), check_vma=False
    )
```
